256 devices in a mesh: gx: 8 (over z), gy: 4 (over y_lo, core), gz: 8 (over y_hi, x).
Axes of the slice: x: 4, y: 4 (y_hi: 2, y_lo: 2; y = y_hi * 2 + y_lo), z: 8, core: 2. Of those that a mesh axis runs over, the one named last changes fastest.
Arguments:
- strain: float32 [3, 256, 128, 2048], P(None, 'gx', 'gy', 'gz'), may hold values from -6 to 6
- plastic_old: float32 [256, 128, 2048], P('gx', 'gy', 'gz'), may hold values from -8 to 0
- alpha_old: float32 [256, 128, 2048], P('gx', 'gy', 'gz'), may hold values from 0 to 1.2
- kappa_old: float32 [256, 128, 2048], P('gx', 'gy', 'gz'), may hold values from 2.8 to 4.2
- flags: int32 [256, 128, 8], P('gx', 'gy', 'gz'), may hold values from 0 to 1, as said below
Outputs:
- internal_force: float32 [256, 128, 2048], P('gx', 'gy', 'gz')
- kappa_new: float32 [256, 128, 2048], P('gx', 'gy', 'gz')
The draws below stay inside these ranges and needn't reach their ends.
Inputs may be any that keep to these rules, and one draw needn't show every extreme that they name: `flags`: at most 512 blocks of one device are active; on the devices at the lowest position along the first dimension exactly 512 are.
All inputs are finite; a program needn't handle non-finite values.
Results may differ from the reference program's by a relative error of at most 0.000057.
Values sent between devices are 32-bit elements; how exact they have to be, the bound alone decides.
No kernel may reach another device: no remote copies, remote signals or barrier semaphores. Data moves between devices by JAX's collectives and lax.ppermute only.
A program may use at most 64 MiB of HBM per device.

```python
import math
import jax
import jax.numpy as jnp
from jax import lax

CX = 32
CY = 32
CZ = 256
REACH = 6
RM_ITERS = 2
NX = 256
NY = 128
NZ = 2048
BLOCKS_Z = 8
MAXF = 512


def draw_flags(key, part):
    key = jax.random.fold_in(key, 11)
    blocks_x = NX // CX
    blocks_y = NY // CY
    columns = CX * CY
    scores = jax.random.randint(key, (blocks_x, blocks_y, BLOCKS_Z, columns), 0, 1 << 16) * columns
    scores = scores + jnp.arange(columns, dtype=jnp.int32)
    ranks = jnp.argsort(jnp.argsort(scores, axis=-1), axis=-1)
    limit = MAXF // (1 + jnp.arange(blocks_x, dtype=jnp.int32))
    active = (ranks < limit[:, None, None, None]).astype(jnp.int32)
    active = active.reshape(blocks_x, blocks_y, BLOCKS_Z, CX, CY)
    active = jnp.transpose(active, (0, 3, 1, 4, 2))
    return active.reshape(NX, NY, BLOCKS_Z)


def levels(rng, dims, shards, least, high):
    level, own = 1.0, jax.random.fold_in(rng, 6)
    for axis_at, blocks in shards:
        steps = jnp.exp(jax.random.uniform(jax.random.fold_in(own, axis_at), (blocks,), jnp.float32, least / len(shards), high / len(shards)))
        level = level * jnp.repeat(steps, dims[axis_at] // blocks).reshape([-1 if axis == axis_at else 1 for axis in range(len(dims))])
    return level


def normal_values(rng, extent, scale, most, split=(), held_as=jnp.bfloat16):
    entries = jax.random.normal(rng, extent, jnp.float32) * scale
    if len(split) > 0:
        entries = levels(rng, extent, split, -0.22, 0.18) * entries
    return jnp.clip(entries, min=-most, max=most).astype(held_as)


def setup_inputs(seed: int = 0) -> dict:
    key_list = jax.random.split(jax.random.key(seed), 6)
    strain = normal_values(key_list[0], (3, NX, NY, NZ), 1.0, 6.0, ((1, 8), (2, 4), (3, 8)), jnp.float32)
    plastic_old = jnp.clip(-8.0 + 8.0 * jax.random.uniform(key_list[1], (NX, NY, NZ), jnp.float32) ** levels(key_list[1], (NX, NY, NZ), ((0, 8), (1, 4), (2, 8)), -0.2, 0.2), -8.0, 0.0)
    alpha_old = jnp.clip(1.2 * jax.random.uniform(key_list[2], (NX, NY, NZ), jnp.float32) ** levels(key_list[2], (NX, NY, NZ), ((0, 8), (1, 4), (2, 8)), -0.2, 0.2), 0.0, 1.2)
    kappa_old = jnp.clip(2.8 + 1.3999999 * jax.random.uniform(key_list[3], (NX, NY, NZ), jnp.float32) ** levels(key_list[3], (NX, NY, NZ), ((0, 8), (1, 4), (2, 8)), -0.2, 0.2), 2.8, 4.2)
    flags = draw_flags(jax.random.fold_in(key_list[5], 71), 0)
    return dict(strain=strain, plastic_old=plastic_old, alpha_old=alpha_old, kappa_old=kappa_old, flags=flags)


length_scale = 3.0


def gauss(offset):
    return math.exp(-offset * offset / (2.0 * length_scale * length_scale))


def smooth(field, axis):
    length = field.shape[axis]
    widths = [(0, 0)] * field.ndim
    widths[axis] = (REACH, REACH)
    padded = jnp.pad(field, widths)
    total = jnp.zeros(field.shape, jnp.float32)
    for offset in range(-REACH, REACH + 1):
        total = total + gauss(offset) * lax.slice_in_dim(padded, REACH + offset, REACH + offset + length, axis=axis)
    return total


def smooth_all(field):
    return smooth(smooth(smooth(field, 0), 1), 2)


def newton_plastic(trial, alpha_old):
    increment = jnp.zeros(trial.shape, jnp.float32)
    for repeat in range(RM_ITERS):
        hardened = alpha_old + increment
        soft = 0.5 * jnp.exp(-5.0 * hardened)
        excess = trial - increment - (1.0 + 0.5 * hardened - soft)
        increment = jnp.maximum(increment + excess / (1.5 + 5.0 * soft), 0.0)
    return increment


def assemble(first, second, third):
    shape = first.shape
    nodes = jnp.zeros((shape[0] + 1, shape[1] + 1, shape[2] + 1), jnp.float32)
    for side_x in (0, 1):
        for side_y in (0, 1):
            for side_z in (0, 1):
                term = 0.25 * ((2 * side_x - 1) * first + (2 * side_y - 1) * second + (2 * side_z - 1) * third)
                nodes = nodes + jnp.pad(term, ((side_x, 1 - side_x), (side_y, 1 - side_y), (side_z, 1 - side_z)))
    return nodes


def reference(strain, plastic_old, alpha_old, kappa_old, flags):
    local_drive = strain[0] * strain[0] + strain[1] * strain[1] + strain[2] * strain[2]
    trial = strain[0] - plastic_old
    active = jnp.repeat(flags, CZ, axis=2).astype(jnp.float32)
    increment = newton_plastic(trial, alpha_old) * active
    weight_x = smooth(jnp.ones((NX,), jnp.float32), 0)
    weight_y = smooth(jnp.ones((NY,), jnp.float32), 0)
    weight_z = smooth(jnp.ones((NZ,), jnp.float32), 0)
    weight_total = weight_x[:, None, None] * weight_y[None, :, None] * weight_z[None, None, :]
    avg_drive = smooth_all(local_drive) / weight_total
    avg_plastic = smooth_all(increment) / weight_total
    kappa_new = jnp.maximum(kappa_old, avg_drive + 4.0 * avg_plastic)
    integrity = jnp.exp(-jnp.maximum(kappa_new - 3.2, 0.0) / 3.0)
    nodes = assemble(integrity * (strain[0] - plastic_old - increment), integrity * strain[1], integrity * strain[2])
    return nodes[:NX, :NY, :NZ], kappa_new
```

```python
import functools
import math

import jax
import jax.numpy as jnp
import numpy as np
from jax import lax
from jax.experimental import pallas as pl
from jax.experimental.pallas import tpu as pltpu
from jax.sharding import PartitionSpec as P

REACH = 6
RM_ITERS = 2
LENGTH_SCALE = 3.0
HIGHEST = lax.Precision.HIGHEST
F32 = jnp.float32
VMEM_LIMIT = 40 * 1024 * 1024
INTERPRET = False


def gauss(offset):
    return math.exp(-offset * offset / (2.0 * LENGTH_SCALE * LENGTH_SCALE))


def band(offset):
    return gauss(offset) if abs(offset) <= REACH else 0.0


def z_band(width):
    return np.array([[band(i - k) for k in range(width)] for i in range(width)], np.float32)


def z_low_rows():
    out = np.zeros((240, 128), np.float32)
    for c in range(7):
        for k in range(128):
            out[112 + c, k] = band(k - (c - 7))
    return out


def z_high_rows():
    out = np.zeros((240, 128), np.float32)
    for c in range(6):
        for k in range(128):
            out[112 + c, k] = band(128 + c - k)
    return out


def plane_from_low():
    out = np.zeros((40, 128), np.float32)
    for g in range(8):
        for c in range(7):
            out[g, 16 * g + c] = band(c - 6)
        for e in range(4):
            out[8 * (1 + e) + g, 16 * g + 7 + e] = 1.0
    return out


def plane_from_own():
    out = np.zeros((40, 128), np.float32)
    for g in range(8):
        for c in range(6):
            out[g, 16 * g + c] = band(c + 1)
    return out


def rows_matrix():
    out = np.zeros((40, 48), np.float32)
    for r in range(33):
        at = r if r < 32 else -1
        for k in range(1, 46):
            out[r, k] = band(k - 8 - at)
    return out


def plane_y_matrices():
    own = np.zeros((256, 256), np.float32)
    low = np.zeros((256, 256), np.float32)
    high = np.zeros((256, 256), np.float32)
    for y in range(-1, 32):
        for l in range(32):
            own[l, y + 1] = band(l - y)
            low[l, y + 1] = band(l - 32 - y) if l >= 25 else 0.0
            high[l, y + 1] = band(32 + l - y) if l < 6 else 0.0
    for c in range(1, 5):
        for y in range(32):
            own[32 * c + y, 40 * c + y + 1] = 1.0
        low[32 * c + 31, 40 * c] = 1.0
    return own, low, high


def lanes(shape):
    return lax.broadcasted_iota(jnp.int32, shape, len(shape) - 1)


def rows(shape):
    return lax.broadcasted_iota(jnp.int32, shape, len(shape) - 2)


def inverse_total(position, extent):
    total = jnp.zeros(position.shape, F32)
    for offset in range(-REACH, REACH + 1):
        inside = (position + offset >= 0) & (position + offset < extent)
        total = total + jnp.where(inside, F32(gauss(offset)), F32(0.0))
    return 1.0 / total


def newton_plastic(trial, alpha_old):
    increment = jnp.zeros(trial.shape, F32)
    for _ in range(RM_ITERS):
        hardened = alpha_old + increment
        soft = 0.5 * jnp.exp(-5.0 * hardened)
        excess = trial - increment - (1.0 + 0.5 * hardened - soft)
        increment = jnp.maximum(increment + excess / (1.5 + 5.0 * soft), 0.0)
    return increment


def integrity_of(kappa):
    return jnp.exp(-jnp.maximum(kappa - 3.2, 0.0) / 3.0)


def by_parity(even, first, second, use):
    @pl.when(even)
    def _():
        use(first, second)

    @pl.when(jnp.logical_not(even))
    def _():
        use(second, first)


CHUNK = 8


def local_kernel(
    where_ref, strain, plastic, alpha, kappa, flags,
    field, free, yext, xext, z_a, z_b, flags_t, up, low,
):
    step = pl.program_id(0)

    @pl.when(step == 0)
    def _():
        eye = (rows((32, 32)) == lanes((32, 32))).astype(F32)
        flags_t[...] = lax.dot_general(
            eye, flags[...].astype(F32), (((1,), (1,)), ((), ())), preferred_element_type=F32
        )
        up[...] = jnp.zeros_like(up)
        low[...] = jnp.zeros_like(low)

    lane = lanes((128, 128))
    for half in range(CHUNK // 4):
        for i in range(4):
            x = half * 4 + i
            here = (rows((32, 256)) == step * CHUNK + x).astype(F32)
            flag = jnp.dot(flags_t[...], here, preferred_element_type=F32)
            s0, s1, s2 = strain[0, x], strain[1, x], strain[2, x]
            trial = s0 - plastic[x]
            increment = newton_plastic(trial, alpha[x]) * flag
            field[x] = s0 * s0 + s1 * s1 + s2 * s2 + 4.0 * increment
            free[x] = trial - increment
        g = step * (CHUNK // 4) + half
        part = pl.ds(half * 4, 4)

        def high_half(ref):
            return ref[part, :, 128:256].reshape(128, 128)

        packed = jnp.where(lane < 7, pltpu.roll(high_half(field), 7, 1), 0.0)
        extras = (free, strain.at[1], strain.at[2], kappa)
        for e, ref in enumerate(extras):
            packed = jnp.where(lane == 7 + e, pltpu.roll(high_half(ref), 8 + e, 1), packed)
        up[...] += pltpu.roll(packed, 16 * g, 1)
        first = jnp.where(lane < 6, field[part, :, 0:128].reshape(128, 128), 0.0)
        low[...] += pltpu.roll(first, 16 * g, 1)
    for x in range(CHUNK):
        for e, ref in enumerate((free, strain.at[1], strain.at[2], kappa)):
            yext[e, pl.ds(x, 1), :] = ref[x, 31:32, :]

    @pl.when(step == pl.num_programs(0) - 1)
    def _():
        for e, ref in enumerate((free, strain.at[1], strain.at[2], kappa)):
            xext[e] = ref[CHUNK - 1]

        def store(upper, lower):
            upper[...] = up[...]
            lower[...] = low[...]

        by_parity(lax.rem(where_ref[2], 2) == 0, z_a, z_b, store)


def z_kernel(
    where_ref, field, yext, sent_a, sent_b, got_a, got_b, bz, t_low, t_high, w_low, w_own,
    smooth, plane, y_a, y_b, z_low, z_high, own_low, head_rows, tail_rows,
):
    def choose(upper, lower):
        z_high[...] = upper[0][...]
        z_low[...] = lower[0][...]
        own_low[...] = lower[1][...]

    by_parity(lax.rem(where_ref[2], 2) == 0, (got_a, sent_a), (got_b, sent_b), choose)
    for g in range(8):
        part = field[4 * g : 4 * g + 4].reshape(128, 256)
        main = jnp.dot(part, bz[...], precision=HIGHEST, preferred_element_type=F32)
        start = 112 - 16 * g
        first = jnp.dot(
            z_low[...], t_low[start : start + 128], precision=HIGHEST, preferred_element_type=F32
        )
        last = jnp.dot(
            z_high[...], t_high[start : start + 128], precision=HIGHEST, preferred_element_type=F32
        )
        smooth[4 * g : 4 * g + 4, :, 0:128] = (main[:, 0:128] + first).reshape(4, 32, 128)
        smooth[4 * g : 4 * g + 4, :, 128:256] = (main[:, 128:256] + last).reshape(4, 32, 128)
    contract = (((1,), (1,)), ((), ()))
    turned = lax.dot_general(
        w_low[...], z_low[...], contract, precision=HIGHEST, preferred_element_type=F32
    ) + lax.dot_general(
        w_own[...], own_low[...], contract, precision=HIGHEST, preferred_element_type=F32
    )
    lane = lanes((8, 128))
    for b in range(4):
        head = jnp.zeros((8, 128), F32)
        for c in range(4):
            moved = pltpu.roll(turned[8 * c : 8 * c + 8], (32 * (c - b)) % 128, 1)
            head = jnp.where(lane // 32 == c, moved, head)
        tail = jnp.where(lane < 32, pltpu.roll(turned[32:40], (-32 * b) % 128, 1), 0.0)
        head_rows[pl.ds(b, 8, stride=4), :] = head
        tail_rows[pl.ds(b, 8, stride=4), :] = tail
    plane[:, 0:128] = head_rows[...]
    plane[:, 128:256] = tail_rows[...]

    def store(upper, lower):
        for j in range(7):
            upper[j] = smooth[:, 25 + j, :]
        for e in range(4):
            upper[7 + e] = yext[e]
        upper[11] = plane[...]
        for j in range(6):
            lower[j] = smooth[:, j, :]
        lower[11] = plane[...]

    by_parity(lax.rem(where_ref[1], 2) == 0, y_a, y_b, store)


def y_kernel(
    where_ref, smooth, plane, xext, got_a, got_b, my, v_own, v_low, v_high,
    out, out_face, out_plane, face_ext, x_a, x_b, ext, plane_low, plane_high,
):
    for x in range(32):
        ext[x, 8:40, :] = smooth[x]
        ext[x, 0:8, :] = jnp.zeros((8, 256), F32)
        ext[x, 40:48, :] = jnp.zeros((8, 256), F32)

    def choose(upper, lower):
        for j in range(7):
            ext[:, 1 + j, :] = lower[j]
        for j in range(6):
            ext[:, 40 + j, :] = upper[j]
        for e in range(4):
            face_ext[e] = lower[7 + e]
        plane_low[...] = lower[11]
        plane_high[...] = upper[11]

    by_parity(lax.rem(where_ref[1], 2) == 0, got_a, got_b, choose)
    for x in range(32):
        both = jnp.dot(my[...], ext[x], precision=HIGHEST, preferred_element_type=F32)
        out[x] = both[0:32]
        out_face[x : x + 1, :] = both[32:33]
    total = jnp.dot(plane[...], v_own[...], precision=HIGHEST, preferred_element_type=F32)
    total += jnp.dot(plane_low[...], v_low[...], precision=HIGHEST, preferred_element_type=F32)
    total += jnp.dot(plane_high[...], v_high[...], precision=HIGHEST, preferred_element_type=F32)
    out_plane[...] = total

    def store(upper, lower):
        for j in range(7):
            upper[j] = out[25 + j]
        for e in range(4):
            upper[7 + e] = xext[e]
        upper[11] = jnp.zeros((32, 256), F32)
        upper[11, 0:8, :] = out_face[24:32, :]
        for e in range(4):
            upper[11, 8 + e : 9 + e, :] = face_ext[e, 31:32, :]
        upper[11, 16:24, :] = out_plane[24:32, :]
        for j in range(6):
            lower[j] = out[j]
        lower[11] = jnp.zeros((32, 256), F32)
        lower[11, 0:8, :] = out_face[0:8, :]
        lower[11, 16:24, :] = out_plane[0:8, :]

    by_parity(lax.rem(where_ref[0], 2) == 0, x_a, x_b, store)


def final_kernel(
    extents, where_ref, strain, free, kappa, smooth, face, plane, face_ext, got_a, got_b, mx,
    force, kappa_new,
    ext, face_all, plane_all, side, before, face_e, face_a, column, inv_x, inv_yz,
):
    step = pl.program_id(0)
    nx, ny, nz = extents
    ix, iy, iz = where_ref[0], where_ref[1], where_ref[2]

    def layer(at):
        total = gauss(0) * ext[at + 7]
        for a in range(1, REACH + 1):
            total = total + gauss(a) * (ext[at + 7 - a] + ext[at + 7 + a])
        return total

    @pl.when(step == 0)
    def _():
        def choose(upper, lower):
            for j in range(7):
                ext[j] = lower[j]
            for j in range(6):
                ext[39 + j] = upper[j]
            face_all[0:8, :] = lower[11, 0:8, :]
            face_all[40:48, :] = upper[11, 0:8, :]
            plane_all[0:8, :] = lower[11, 16:24, :]
            plane_all[40:48, :] = upper[11, 16:24, :]
            for e in range(4):
                side[e, 32:33, :] = lower[11, 8 + e : 9 + e, :]
                before[e] = lower[7 + e]

        for e in range(4):
            side[e, 0:32, :] = face_ext[e]
            side[e, 32:40, :] = jnp.zeros((8, 256), F32)
        by_parity(lax.rem(ix, 2) == 0, got_a, got_b, choose)
        for x in range(32):
            ext[7 + x] = smooth[x]
        face_all[8:40, :] = face[...]
        plane_all[8:40, :] = plane[...]

        shape = (40, 256)
        r = rows(shape)
        invx = inverse_total(ix * 32 + jnp.where(r < 32, r, -1), nx)
        inv_x[...] = invx
        small = (32, 256)
        invz = inverse_total(iz * 256 + lanes(small), nz)
        inv_yz[...] = inverse_total(iy * 32 + rows(small), ny) * invz

        at_y = inverse_total(jnp.full((1, 256), iy * 32 - 1, jnp.int32), ny)
        avg = jnp.dot(mx[...], face_all[...], precision=HIGHEST, preferred_element_type=F32)
        kap = jnp.maximum(side[3], avg * (invx * (at_y * invz[0:1, :])))
        integ = integrity_of(kap)
        row = rows(shape)

        def previous(value):
            return jnp.where(row == 0, value[32:33, :], pltpu.roll(value, 1, 0))

        t0, t1, t2 = integ * side[0], integ * side[1], integ * side[2]
        a0 = previous(t0) - t0
        a1 = previous(t1) + t1
        a2 = previous(t2) + t2
        face_e[...] = (a0 + a1)[0:32]
        face_a[...] = a2[0:32]

        avg = jnp.dot(mx[...], plane_all[...], precision=HIGHEST, preferred_element_type=F32)
        own = plane_all[8:48, :]
        own = jnp.where(row == 32, plane_all[7:8, :], own)

        def value(c):
            return pltpu.roll(own, (256 - 40 * c) % 256, 1)

        lane = lanes(shape)
        at_z = inverse_total(jnp.full((1, 256), iz * 256 - 1, jnp.int32), nz)
        invy = inverse_total(iy * 32 - 1 + jnp.minimum(lane, 32), ny)
        kap = jnp.maximum(value(4), avg * (invx * (invy * at_z)))
        integ = integrity_of(kap)
        t0, t1, t2 = integ * value(1), integ * value(2), integ * value(3)
        a0 = previous(t0) - t0
        a1 = previous(t1) + t1
        a2 = previous(t2) + t2
        e, f = a0 + a1, a0 - a1
        parts = e + a2 + pltpu.roll(f + a2, 255, 1)
        parts = jnp.where(lane < 32, parts, 0.0)
        eye = (rows((32, 128)) == lanes((32, 128))).astype(F32)
        pad = jnp.concatenate([parts[0:32, 0:128], jnp.zeros((96, 128), F32)], axis=0)
        column[...] = lax.dot_general(
            eye, pad, (((1,), (1,)), ((), ())), precision=HIGHEST, preferred_element_type=F32
        )

        kap = jnp.maximum(before[3], layer(-1) * (inv_x[32:33, :] * inv_yz[...]))
        integ = integrity_of(kap)
        for e in range(3):
            before[e] = integ * before[e]

    first_row = rows((32, 256)) == 0
    first_lane = lanes((32, 128)) == 0

    @pl.loop(0, CHUNK)
    def _(i):
        x = step * CHUNK + i
        kap = jnp.maximum(kappa[i], layer(x) * (inv_x[pl.ds(x, 1), :] * inv_yz[...]))
        kappa_new[i] = kap
        integ = integrity_of(kap)
        s0, s1, s2 = integ * free[i], integ * strain[1, i], integ * strain[2, i]
        a0 = before[0] - s0
        a1 = before[1] + s1
        a2 = before[2] + s2
        before[0] = s0
        before[1] = s1
        before[2] = s2
        e, f = a0 + a1, a0 - a1
        b = f + jnp.where(first_row, face_e[pl.ds(x, 1), :], pltpu.roll(e, 1, 0))
        c = a2 + jnp.where(first_row, face_a[pl.ds(x, 1), :], pltpu.roll(a2, 1, 0))
        p, q = b + c, b - c
        moved = pltpu.roll(p, 1, 1)
        edge = pltpu.roll(column[...], lax.rem(128 - x, 128), 1)
        force[i, :, 0:128] = 0.25 * (q[:, 0:128] + jnp.where(first_lane, edge, moved[:, 0:128]))
        force[i, :, 128:256] = 0.25 * (q[:, 128:256] + moved[:, 128:256])


def swap(first, second, axis):
    count = lax.axis_size(axis)

    def route(start):
        out = []
        for i in range(start, count - 1, 2):
            out += [(i, i + 1), (i + 1, i)]
        return out

    return lax.ppermute(first, axis, route(0)), lax.ppermute(second, axis, route(1))


def shape_of(*dims):
    return jax.ShapeDtypeStruct(dims, F32)


VM = pl.BlockSpec(memory_space=pltpu.VMEM)
SM = pl.BlockSpec(memory_space=pltpu.SMEM)


def call(kernel, name, **kwargs):
    return pl.pallas_call(
        kernel,
        name=name,
        interpret=INTERPRET,
        compiler_params=pltpu.CompilerParams(vmem_limit_bytes=VMEM_LIMIT),
        **kwargs,
    )


def body(strain, plastic_old, alpha_old, kappa_old, flags):
    where = jnp.stack([lax.axis_index(a) for a in ("gx", "gy", "gz")]).astype(jnp.int32)
    cells = pl.BlockSpec((CHUNK, 32, 256), lambda s: (s, 0, 0))
    three = pl.BlockSpec((3, CHUNK, 32, 256), lambda s: (0, s, 0, 0))

    def whole(*dims):
        return pl.BlockSpec(dims, lambda s: (0,) * len(dims))

    field, free, yext, xext, z_a, z_b = call(
        local_kernel,
        "local",
        grid=(32 // CHUNK,),
        in_specs=[SM, three, cells, cells, cells, whole(32, 32)],
        out_specs=[
            cells, cells, pl.BlockSpec((4, CHUNK, 256), lambda s: (0, s, 0)),
            whole(4, 32, 256), whole(128, 128), whole(128, 128),
        ],
        out_shape=[
            shape_of(32, 32, 256), shape_of(32, 32, 256), shape_of(4, 32, 256),
            shape_of(4, 32, 256), shape_of(128, 128), shape_of(128, 128),
        ],
        scratch_shapes=[
            pltpu.VMEM((32, 32), F32), pltpu.VMEM((128, 128), F32), pltpu.VMEM((128, 128), F32),
        ],
    )(where, strain, plastic_old, alpha_old, kappa_old, flags.reshape(32, 32))
    got_a, got_b = swap(z_a, z_b, "gz")

    smooth, plane, y_a, y_b = call(
        z_kernel,
        "along_z",
        in_specs=[SM] + [VM] * 11,
        out_specs=[VM] * 4,
        out_shape=[
            shape_of(32, 32, 256), shape_of(32, 256), shape_of(12, 32, 256), shape_of(12, 32, 256),
        ],
        scratch_shapes=[pltpu.VMEM((128, 128), F32)] * 3 + [pltpu.VMEM((32, 128), F32)] * 2,
    )(
        where, field, yext, z_a, z_b, got_a, got_b,
        z_band(256), z_low_rows(), z_high_rows(), plane_from_low(), plane_from_own(),
    )
    got_a, got_b = swap(y_a, y_b, "gy")

    smooth, face, plane, face_ext, x_a, x_b = call(
        y_kernel,
        "along_y",
        in_specs=[SM] + [VM] * 9,
        out_specs=[VM] * 6,
        out_shape=[
            shape_of(32, 32, 256), shape_of(32, 256), shape_of(32, 256), shape_of(4, 32, 256),
            shape_of(12, 32, 256), shape_of(12, 32, 256),
        ],
        scratch_shapes=[
            pltpu.VMEM((32, 48, 256), F32), pltpu.VMEM((32, 256), F32), pltpu.VMEM((32, 256), F32),
        ],
    )(where, smooth, plane, xext, got_a, got_b, rows_matrix(), *plane_y_matrices())
    got_a, got_b = swap(x_a, x_b, "gx")

    extents = (
        32 * lax.axis_size("gx"), 32 * lax.axis_size("gy"), 256 * lax.axis_size("gz"),
    )
    force, kappa_new = call(
        functools.partial(final_kernel, extents),
        "along_x",
        grid=(32 // CHUNK,),
        in_specs=[
            SM, three, cells, cells, whole(32, 32, 256), whole(32, 256), whole(32, 256),
            whole(4, 32, 256), whole(12, 32, 256), whole(12, 32, 256), whole(40, 48),
        ],
        out_specs=[cells, cells],
        out_shape=[shape_of(32, 32, 256), shape_of(32, 32, 256)],
        scratch_shapes=[
            pltpu.VMEM((45, 32, 256), F32), pltpu.VMEM((48, 256), F32), pltpu.VMEM((48, 256), F32),
            pltpu.VMEM((4, 40, 256), F32), pltpu.VMEM((4, 32, 256), F32),
            pltpu.VMEM((32, 256), F32), pltpu.VMEM((32, 256), F32), pltpu.VMEM((32, 128), F32),
            pltpu.VMEM((40, 256), F32), pltpu.VMEM((32, 256), F32),
        ],
    )(where, strain, free, kappa_old, smooth, face, plane, face_ext, got_a, got_b, rows_matrix())
    return (force, kappa_new)


def solution(mesh):
    in_specs = (
        P(None, "gx", "gy", "gz"),
        P("gx", "gy", "gz"),
        P("gx", "gy", "gz"),
        P("gx", "gy", "gz"),
        P("gx", "gy", "gz"),
    )
    out_specs = (P("gx", "gy", "gz"), P("gx", "gy", "gz"))
    return jax.shard_map(body, mesh=mesh, in_specs=in_specs, out_specs=out_specs, check_vma=False)
```

```python
import functools
import math

import jax
import jax.numpy as jnp
import numpy as np
from jax import lax
from jax.experimental import pallas as pl
from jax.experimental.pallas import tpu as pltpu
from jax.sharding import PartitionSpec as P

REACH = 6
RM_ITERS = 2
LENGTH_SCALE = 3.0
HIGHEST = lax.Precision.HIGHEST
F32 = jnp.float32
VMEM_LIMIT = 40 * 1024 * 1024
INTERPRET = False


def gauss(offset):
    return math.exp(-offset * offset / (2.0 * LENGTH_SCALE * LENGTH_SCALE))


def band(offset):
    return gauss(offset) if abs(offset) <= REACH else 0.0


def z_band(width):
    return np.array([[band(i - k) for k in range(width)] for i in range(width)], np.float32)


def z_low_rows():
    out = np.zeros((240, 128), np.float32)
    for c in range(7):
        for k in range(128):
            out[112 + c, k] = band(k - (c - 7))
    return out


def z_high_rows():
    out = np.zeros((240, 128), np.float32)
    for c in range(6):
        for k in range(128):
            out[112 + c, k] = band(128 + c - k)
    return out


def plane_from_low():
    out = np.zeros((40, 128), np.float32)
    for g in range(8):
        for c in range(7):
            out[g, 16 * g + c] = band(c - 6)
        for e in range(4):
            out[8 * (1 + e) + g, 16 * g + 7 + e] = 1.0
    return out


def plane_from_own():
    out = np.zeros((40, 128), np.float32)
    for g in range(8):
        for c in range(6):
            out[g, 16 * g + c] = band(c + 1)
    return out


def rows_matrix():
    out = np.zeros((40, 48), np.float32)
    for r in range(33):
        at = r if r < 32 else -1
        for k in range(1, 46):
            out[r, k] = band(k - 8 - at)
    return out


def plane_y_matrices():
    own = np.zeros((256, 256), np.float32)
    low = np.zeros((256, 256), np.float32)
    high = np.zeros((256, 256), np.float32)
    for y in range(-1, 32):
        for l in range(32):
            own[l, y + 1] = band(l - y)
            low[l, y + 1] = band(l - 32 - y) if l >= 25 else 0.0
            high[l, y + 1] = band(32 + l - y) if l < 6 else 0.0
    for c in range(1, 5):
        for y in range(32):
            own[32 * c + y, 40 * c + y + 1] = 1.0
        low[32 * c + 31, 40 * c] = 1.0
    return own, low, high


def lanes(shape):
    return lax.broadcasted_iota(jnp.int32, shape, len(shape) - 1)


def rows(shape):
    return lax.broadcasted_iota(jnp.int32, shape, len(shape) - 2)


def inverse_total(position, extent):
    total = jnp.zeros(position.shape, F32)
    for offset in range(-REACH, REACH + 1):
        inside = (position + offset >= 0) & (position + offset < extent)
        total = total + jnp.where(inside, F32(gauss(offset)), F32(0.0))
    return 1.0 / total


def newton_plastic(trial, alpha_old):
    increment = jnp.zeros(trial.shape, F32)
    for _ in range(RM_ITERS):
        hardened = alpha_old + increment
        soft = 0.5 * jnp.exp(-5.0 * hardened)
        excess = trial - increment - (1.0 + 0.5 * hardened - soft)
        increment = jnp.maximum(increment + excess / (1.5 + 5.0 * soft), 0.0)
    return increment


def field_of(first, second, third):
    return first * first + second * second + third * third


def integrity_of(kappa):
    return jnp.exp(-jnp.maximum(kappa - 3.2, 0.0) / 3.0)


def by_parity(even, first, second, use):
    @pl.when(even)
    def _():
        use(first, second)

    @pl.when(jnp.logical_not(even))
    def _():
        use(second, first)


CONTRACT_LANES = (((1,), (1,)), ((), ()))
CHUNK = 8
CHUNKS = 4


def dot(left, right):
    return jnp.dot(left, right, precision=HIGHEST, preferred_element_type=F32)


def dot_lanes(left, right, precision=HIGHEST):
    return lax.dot_general(
        left, right, CONTRACT_LANES, precision=precision, preferred_element_type=F32
    )


def turned_flags(flags):
    eye = (rows((32, 32)) == lanes((32, 32))).astype(F32)
    return dot_lanes(eye, flags[...].astype(F32), None)


def pack_kernel(
    where_ref, strain_in, plastic_in, alpha_in, kappa_in, flags,
    strain, plastic, alpha, kappa, z_a, z_b,
    up_trial, up_alpha, up_drive, low_trial, low_alpha, low_drive, sems,
):
    copies = []
    for c in range(CHUNKS):
        part = pl.ds(c * CHUNK, CHUNK)
        pairs = [(strain_in.at[:, part], strain.at[:, part])]
        pairs += [
            (src.at[part], dst.at[part])
            for src, dst in ((plastic_in, plastic), (alpha_in, alpha), (kappa_in, kappa))
        ]
        copies.append(
            [pltpu.make_async_copy(src, dst, sems.at[c, i]) for i, (src, dst) in enumerate(pairs)]
        )
    for group in copies:
        for copy in group:
            copy.start()
    turned = turned_flags(flags)
    flag = jnp.concatenate(
        [
            jnp.dot(
                turned,
                (rows((32, 128)) == 4 * (lanes((32, 128)) // 16) + b).astype(F32),
                preferred_element_type=F32,
            )
            for b in range(4)
        ],
        axis=0,
    )
    lane = lanes((128, 128))
    for c in range(CHUNKS):
        for copy in copies[c]:
            copy.wait()
        for g in (2 * c, 2 * c + 1):
            inside = lane // 16 == g

            def tile(ref, half):
                cells = ref[4 * g : 4 * g + 4, :, 128 * half : 128 * half + 128]
                return cells.reshape(128, 128)

            def place(ref, value, move):
                moved = pltpu.roll(value, (move + 16 * g) % 128, 1) if move + 16 * g else value
                ref[...] = jnp.where(inside, moved, ref[...])

            s0, s1, s2 = (tile(strain.at[i], 1) for i in range(3))
            place(up_trial, s0 - tile(plastic, 1), 7)
            place(up_alpha, tile(alpha, 1), 7)
            place(up_drive, field_of(s0, s1, s2), 7)
            mixed = up_drive[...]
            for e, value in enumerate((s1, s2, tile(kappa, 1))):
                moved = pltpu.roll(value, (9 + e + 16 * g) % 128, 1)
                mixed = jnp.where(lane == 16 * g + 8 + e, moved, mixed)
            up_drive[...] = mixed
            s0, s1, s2 = (tile(strain.at[i], 0) for i in range(3))
            place(low_trial, s0 - tile(plastic, 0), 0)
            place(low_alpha, tile(alpha, 0), 0)
            place(low_drive, field_of(s0, s1, s2), 0)

    increment = newton_plastic(up_trial[...], up_alpha[...]) * flag
    free = pltpu.roll(up_trial[...] - increment, 1, 1)
    up_drive[...] = jnp.where(
        lane % 16 < 7,
        up_drive[...] + 4.0 * increment,
        jnp.where(lane % 16 == 7, free, up_drive[...]),
    )
    increment = newton_plastic(low_trial[...], low_alpha[...]) * flag
    low_drive[...] = low_drive[...] + 4.0 * increment

    def store(upper, lower):
        upper[...] = up_drive[...]
        lower[...] = low_drive[...]

    by_parity(lax.rem(where_ref[2], 2) == 0, z_a, z_b, store)


def inner_kernel(strain, plastic, alpha, kappa, flags, bz, smooth, free, yext, xext, turned, field):
    turned[...] = turned_flags(flags)

    @pl.loop(0, 8)
    def _(g):
        for i in range(4):
            x = 4 * g + i
            here = (rows((32, 256)) == x).astype(F32)
            flag = jnp.dot(turned[...], here, preferred_element_type=F32)
            s0 = strain[0, x]
            trial = s0 - plastic[x]
            increment = newton_plastic(trial, alpha[x]) * flag
            field[x] = field_of(s0, strain[1, x], strain[2, x]) + 4.0 * increment
            free[x] = trial - increment

    for g in range(4):
        part = field[8 * g : 8 * g + 8].reshape(256, 256)
        smooth[8 * g : 8 * g + 8] = dot(part, bz[...]).reshape(8, 32, 256)
    for e, ref in enumerate((free, strain.at[1], strain.at[2], kappa)):
        xext[e] = ref[31]
        for x in range(32):
            yext[e, x : x + 1, :] = ref[x, 31:32, :]


def z_kernel(
    where_ref, own, yext, sent_a, sent_b, got_a, got_b, t_low, t_high, w_low, w_own,
    smooth, plane, y_a, y_b, z_low, z_high, own_low, head_rows, tail_rows,
):
    def choose(upper, lower):
        z_high[...] = upper[0][...]
        z_low[...] = lower[0][...]
        own_low[...] = lower[1][...]

    by_parity(lax.rem(where_ref[2], 2) == 0, (got_a, sent_a), (got_b, sent_b), choose)
    for g in range(8):
        part = slice(4 * g, 4 * g + 4)
        start = 112 - 16 * g
        first = dot(z_low[...], t_low[start : start + 128])
        last = dot(z_high[...], t_high[start : start + 128])
        smooth[part, :, 0:128] = own[part, :, 0:128] + first.reshape(4, 32, 128)
        smooth[part, :, 128:256] = own[part, :, 128:256] + last.reshape(4, 32, 128)
    turned = dot_lanes(w_low[...], z_low[...]) + dot_lanes(w_own[...], own_low[...])
    lane = lanes((8, 128))
    for b in range(4):
        head = jnp.zeros((8, 128), F32)
        for c in range(4):
            moved = pltpu.roll(turned[8 * c : 8 * c + 8], (32 * (c - b)) % 128, 1)
            head = jnp.where(lane // 32 == c, moved, head)
        tail = jnp.where(lane < 32, pltpu.roll(turned[32:40], (-32 * b) % 128, 1), 0.0)
        head_rows[pl.ds(b, 8, stride=4), :] = head
        tail_rows[pl.ds(b, 8, stride=4), :] = tail
    plane[:, 0:128] = head_rows[...]
    plane[:, 128:256] = tail_rows[...]

    def store(upper, lower):
        for j in range(7):
            upper[j] = smooth[:, 25 + j, :]
        for e in range(4):
            upper[7 + e] = yext[e]
        upper[11] = plane[...]
        for j in range(6):
            lower[j] = smooth[:, j, :]
        lower[11] = plane[...]

    by_parity(lax.rem(where_ref[1], 2) == 0, y_a, y_b, store)


def own_rows_kernel(smooth, my, out, out_face):
    for x in range(32):
        both = dot(my[...], smooth[x])
        out[x] = both[0:32]
        out_face[x : x + 1, :] = both[32:33]


def y_kernel(
    where_ref, own, own_face, plane, xext, got_a, got_b, my, v_own, v_low, v_high,
    edges, out_face, out_plane, face_ext, halo, x_a, x_b, plane_low, plane_high,
):
    def choose(upper, lower):
        for j in range(7):
            halo[:, j, :] = lower[j]
        for j in range(6):
            halo[:, 8 + j, :] = upper[j]
        for e in range(4):
            face_ext[e] = lower[7 + e]
        plane_low[...] = lower[11]
        plane_high[...] = upper[11]

    halo[:, 0:8, :] = jnp.zeros((32, 8, 256), F32)
    halo[:, 8:16, :] = jnp.zeros((32, 8, 256), F32)
    by_parity(lax.rem(where_ref[1], 2) == 0, got_a, got_b, choose)
    for x in range(32):
        if x < 8 or x >= 24:
            both = dot(my[...], halo[x])
            edges[x if x < 8 else x - 16] = own[x] + both[0:32]
            out_face[x : x + 1, :] = own_face[x : x + 1, :] + both[32:33]
        else:
            both = dot(my[32:40, :], halo[x])
            out_face[x : x + 1, :] = own_face[x : x + 1, :] + both[0:1]
    total = dot(plane[...], v_own[...])
    total += dot(plane_low[...], v_low[...])
    total += dot(plane_high[...], v_high[...])
    out_plane[...] = total

    def store(upper, lower):
        for j in range(7):
            upper[j] = edges[9 + j]
        for e in range(4):
            upper[7 + e] = xext[e]
        upper[11] = jnp.zeros((32, 256), F32)
        upper[11, 0:8, :] = out_face[24:32, :]
        for e in range(4):
            upper[11, 8 + e : 9 + e, :] = face_ext[e, 31:32, :]
        upper[11, 16:24, :] = out_plane[24:32, :]
        for j in range(6):
            lower[j] = edges[j]
        lower[11] = jnp.zeros((32, 256), F32)
        lower[11, 0:8, :] = out_face[0:8, :]
        lower[11, 16:24, :] = out_plane[0:8, :]

    by_parity(lax.rem(where_ref[0], 2) == 0, x_a, x_b, store)


def faces(extents, at, mx, face_all, plane_all, side, face_e, face_a, column, inv_x, inv_yz):
    nx, ny, nz = extents
    ix, iy, iz = at
    shape = (40, 256)
    row, lane = rows(shape), lanes(shape)
    invx = inverse_total(ix * 32 + jnp.where(row < 32, row, -1), nx)
    inv_x[...] = invx
    small = (32, 256)
    invz = inverse_total(iz * 256 + lanes(small), nz)
    inv_yz[...] = inverse_total(iy * 32 + rows(small), ny) * invz

    def previous(value):
        return jnp.where(row == 0, value[32:33, :], pltpu.roll(value, 1, 0))

    def joined(t0, t1, t2):
        a0 = previous(t0) - t0
        a1 = previous(t1) + t1
        a2 = previous(t2) + t2
        return a0 + a1, a0 - a1, a2

    at_y = inverse_total(jnp.full((1, 256), iy * 32 - 1, jnp.int32), ny)
    kap = jnp.maximum(side[3], dot(mx[...], face_all[...]) * (invx * (at_y * invz[0:1, :])))
    integ = integrity_of(kap)
    e, _, a2 = joined(integ * side[0], integ * side[1], integ * side[2])
    face_e[...] = e[0:32]
    face_a[...] = a2[0:32]

    avg = dot(mx[...], plane_all[...])
    own = jnp.where(row == 32, plane_all[7:8, :], plane_all[8:48, :])

    def value(c):
        return pltpu.roll(own, (256 - 40 * c) % 256, 1)

    at_z = inverse_total(jnp.full((1, 256), iz * 256 - 1, jnp.int32), nz)
    invy = inverse_total(iy * 32 - 1 + jnp.minimum(lane, 32), ny)
    kap = jnp.maximum(value(4), avg * (invx * (invy * at_z)))
    integ = integrity_of(kap)
    e, f, a2 = joined(integ * value(1), integ * value(2), integ * value(3))
    parts = e + a2 + pltpu.roll(f + a2, 255, 1)
    parts = jnp.where(lane < 32, parts, 0.0)
    eye = (rows((32, 128)) == lanes((32, 128))).astype(F32)
    pad = jnp.concatenate([parts[0:32, 0:128], jnp.zeros((96, 128), F32)], axis=0)
    column[...] = dot_lanes(eye, pad)


def layer_results(x, avg, kappa, free, strain, before, face_e, face_a, column, force_at, kappa_at):
    first_row = rows((32, 256)) == 0
    first_lane = lanes((32, 128)) == 0
    kap = jnp.maximum(kappa[x], avg)
    integ = integrity_of(kap)
    s0, s1, s2 = integ * free[x], integ * strain[1, x], integ * strain[2, x]
    if force_at is not None:
        kappa_at[...] = kap
        a0 = before[0] - s0
        a1 = before[1] + s1
        a2 = before[2] + s2
        e, f = a0 + a1, a0 - a1
        b = f + jnp.where(first_row, face_e[pl.ds(x, 1), :], pltpu.roll(e, 1, 0))
        c = a2 + jnp.where(first_row, face_a[pl.ds(x, 1), :], pltpu.roll(a2, 1, 0))
        p, q = b + c, b - c
        moved = pltpu.roll(p, 1, 1)
        edge = pltpu.roll(column[...], lax.rem(128 - x, 128), 1)
        force_at[:, 0:128] = 0.25 * (q[:, 0:128] + jnp.where(first_lane, edge, moved[:, 0:128]))
        force_at[:, 128:256] = 0.25 * (q[:, 128:256] + moved[:, 128:256])
    before[0] = s0
    before[1] = s1
    before[2] = s2


def middle_kernel(
    extents, where_ref, strain, free, kappa, own, edges, halo, face, plane, face_ext, my,
    force, kappa_new, part,
    ext, face_all, plane_all, side, before, face_e, face_a, column, inv_x, inv_yz,
    force_v, kappa_v, sems,
):
    at = (where_ref[0], where_ref[1], where_ref[2])
    for x in range(32):
        if x < 8:
            ext[x] = edges[x]
        elif x >= 24:
            ext[x] = edges[x - 16]
        else:
            ext[x] = own[x] + dot(my[:, 32:48][0:32], halo[x])
    for ref, value in ((face_all, face), (plane_all, plane)):
        ref[0:8, :] = jnp.zeros((8, 256), F32)
        ref[8:40, :] = value[...]
        ref[40:48, :] = jnp.zeros((8, 256), F32)
    for e in range(4):
        side[e, 0:32, :] = face_ext[e]
        side[e, 32:40, :] = jnp.zeros((8, 256), F32)
    faces(
        extents, at, my.at[:, 48:96], face_all, plane_all, side,
        face_e, face_a, column, inv_x, inv_yz,
    )

    def layer(x):
        total = gauss(0) * ext[x]
        for a in range(1, REACH + 1):
            total = total + gauss(a) * (ext[x - a] + ext[x + a])
        return total * (inv_x[pl.ds(x, 1), :] * inv_yz[...])

    layer_results(7, layer(7), kappa, free, strain, before, None, None, None, None, None)
    copies = []
    for c in (1, 2):

        @pl.loop(0, CHUNK)
        def _(i):
            x = c * CHUNK + i
            layer_results(
                x, layer(x), kappa, free, strain, before, face_e, face_a, column,
                force_v.at[x - CHUNK], kappa_v.at[x - CHUNK],
            )

        here = pl.ds((c - 1) * CHUNK, CHUNK)
        there = pl.ds(c * CHUNK, CHUNK)
        for k, (src, dst) in enumerate(((force_v, force), (kappa_v, kappa_new))):
            copy = pltpu.make_async_copy(src.at[here], dst.at[there], sems.at[c - 1, k])
            copy.start()
            copies.append(copy)
    for i in range(18):
        x = i - 1 if i < 9 else i + 14
        total = None
        for a in range(-REACH, REACH + 1):
            if 0 <= x + a < 32:
                term = gauss(a) * ext[x + a]
                total = term if total is None else total + term
        part[i] = total
    for copy in copies:
        copy.wait()


def outer_kernel(
    extents, where_ref, strain, free, kappa, part, face, plane, face_ext, got_a, got_b, my,
    force_in, kappa_in,
    force, kappa_new,
    low, high, face_all, plane_all, side, before, face_e, face_a, column, inv_x, inv_yz,
    force_v, kappa_v, sems,
):
    at = (where_ref[0], where_ref[1], where_ref[2])

    def choose(upper, lower):
        for j in range(7):
            low[j] = lower[j]
        for j in range(6):
            high[j] = upper[j]
        face_all[0:8, :] = lower[11, 0:8, :]
        face_all[40:48, :] = upper[11, 0:8, :]
        plane_all[0:8, :] = lower[11, 16:24, :]
        plane_all[40:48, :] = upper[11, 16:24, :]
        for e in range(4):
            side[e, 32:33, :] = lower[11, 8 + e : 9 + e, :]
            before[e] = lower[7 + e]

    for e in range(4):
        side[e, 0:32, :] = face_ext[e]
        side[e, 32:40, :] = jnp.zeros((8, 256), F32)
    by_parity(lax.rem(at[0], 2) == 0, got_a, got_b, choose)
    face_all[8:40, :] = face[...]
    plane_all[8:40, :] = plane[...]
    faces(
        extents, at, my.at[:, 48:96], face_all, plane_all, side,
        face_e, face_a, column, inv_x, inv_yz,
    )

    def layer(x):
        total = part[x + 1 if x < 8 else x - 14]
        for a in range(-REACH, REACH + 1):
            if x + a < 0:
                total = total + gauss(a) * low[x + a + 7]
            elif x + a >= 32:
                total = total + gauss(a) * high[x + a - 32]
        return total * (inv_x[x % 33 : x % 33 + 1, :] * inv_yz[...])

    kap = jnp.maximum(before[3], layer(-1))
    integ = integrity_of(kap)
    for e in range(3):
        before[e] = integ * before[e]
    copies = []
    for c in (0, 3):
        if c == 3:
            layer_results(23, layer(23), kappa, free, strain, before, None, None, None, None, None)
        for i in range(CHUNK):
            x = c * CHUNK + i
            slot = i if c == 0 else CHUNK + i
            layer_results(
                x, layer(x), kappa, free, strain, before, face_e, face_a, column,
                force_v.at[slot], kappa_v.at[slot],
            )
        here = pl.ds(0 if c == 0 else CHUNK, CHUNK)
        there = pl.ds(c * CHUNK, CHUNK)
        for k, (src, dst) in enumerate(((force_v, force), (kappa_v, kappa_new))):
            copy = pltpu.make_async_copy(src.at[here], dst.at[there], sems.at[c // 3, k])
            copy.start()
            copies.append(copy)
    for copy in copies:
        copy.wait()


def swap(first, second, axis):
    count = lax.axis_size(axis)

    def route(start):
        out = []
        for i in range(start, count - 1, 2):
            out += [(i, i + 1), (i + 1, i)]
        return out

    return lax.ppermute(first, axis, route(0)), lax.ppermute(second, axis, route(1))


def shape_of(*dims):
    return jax.ShapeDtypeStruct(dims, F32)


VM = pl.BlockSpec(memory_space=pltpu.VMEM)
SM = pl.BlockSpec(memory_space=pltpu.SMEM)
HBM = pl.BlockSpec(memory_space=pltpu.HBM)
BLOCK = shape_of(32, 32, 256)
FACE = shape_of(32, 256)


def vmem(*dims):
    return pltpu.VMEM(dims, F32)


def call(kernel, name, in_specs, out_shape, out_specs=None, scratch=(), **kwargs):
    return pl.pallas_call(
        kernel,
        name=name,
        in_specs=in_specs,
        out_specs=out_specs or [VM] * len(out_shape),
        out_shape=out_shape,
        scratch_shapes=list(scratch),
        interpret=INTERPRET,
        compiler_params=pltpu.CompilerParams(vmem_limit_bytes=VMEM_LIMIT),
        **kwargs,
    )


def body(strain_in, plastic_in, alpha_in, kappa_in, flags):
    where = jnp.stack([lax.axis_index(a) for a in ("gx", "gy", "gz")]).astype(jnp.int32)
    flags = flags.reshape(32, 32)
    extents = (
        32 * lax.axis_size("gx"), 32 * lax.axis_size("gy"), 256 * lax.axis_size("gz"),
    )
    rows_all = rows_matrix()
    rows_own = np.ascontiguousarray(rows_all[:, 8:40])
    rows_halo = np.concatenate(
        [rows_all[:, 1:8], np.zeros((40, 1), np.float32), rows_all[:, 40:48]], axis=1
    )
    rows_three = np.zeros((40, 128), np.float32)
    rows_three[:, 32:48] = rows_halo
    rows_three[:, 48:96] = rows_all

    strain, plastic, alpha, kappa, z_a, z_b = call(
        pack_kernel,
        "pack",
        [SM, HBM, HBM, HBM, HBM, VM],
        [shape_of(3, 32, 32, 256), BLOCK, BLOCK, BLOCK, shape_of(128, 128), shape_of(128, 128)],
        scratch=[vmem(128, 128)] * 6 + [pltpu.SemaphoreType.DMA((CHUNKS, 4))],
    )(where, strain_in, plastic_in, alpha_in, kappa_in, flags)
    got_a, got_b = swap(z_a, z_b, "gz")
    own, free, yext, xext = call(
        inner_kernel,
        "inner",
        [VM] * 6,
        [BLOCK, BLOCK, shape_of(4, 32, 256), shape_of(4, 32, 256)],
        scratch=[vmem(32, 32), vmem(32, 32, 256)],
    )(strain, plastic, alpha, kappa, flags, z_band(256))

    smooth, plane, y_a, y_b = call(
        z_kernel,
        "along_z",
        [SM] + [VM] * 10,
        [BLOCK, FACE, shape_of(12, 32, 256), shape_of(12, 32, 256)],
        scratch=[vmem(128, 128)] * 3 + [vmem(32, 128)] * 2,
    )(
        where, own, yext, z_a, z_b, got_a, got_b,
        z_low_rows(), z_high_rows(), plane_from_low(), plane_from_own(),
    )
    got_a, got_b = swap(y_a, y_b, "gy")
    own, own_face = call(own_rows_kernel, "own_rows", [VM] * 2, [BLOCK, FACE])(smooth, rows_own)

    edges, face, plane, face_ext, halo, x_a, x_b = call(
        y_kernel,
        "along_y",
        [SM] + [VM] * 10,
        [
            shape_of(16, 32, 256), FACE, FACE, shape_of(4, 32, 256), shape_of(32, 16, 256),
            shape_of(12, 32, 256), shape_of(12, 32, 256),
        ],
        scratch=[vmem(32, 256), vmem(32, 256)],
    )(where, own, own_face, plane, xext, got_a, got_b, rows_halo, *plane_y_matrices())
    got_a, got_b = swap(x_a, x_b, "gx")

    shared = [
        vmem(48, 256), vmem(48, 256), vmem(4, 40, 256), vmem(4, 32, 256),
        vmem(32, 256), vmem(32, 256), vmem(32, 128), vmem(40, 256), vmem(32, 256),
        vmem(16, 32, 256), vmem(16, 32, 256), pltpu.SemaphoreType.DMA((2, 2)),
    ]
    force, kappa_new, part = call(
        functools.partial(middle_kernel, extents),
        "middle",
        [SM] + [VM] * 10,
        [BLOCK, BLOCK, shape_of(18, 32, 256)],
        out_specs=[HBM, HBM, VM],
        scratch=[vmem(32, 32, 256)] + shared,
    )(where, strain, free, kappa, own, edges, halo, face, plane, face_ext, rows_three)
    force, kappa_new = call(
        functools.partial(outer_kernel, extents),
        "outer",
        [SM] + [VM] * 10 + [HBM, HBM],
        [BLOCK, BLOCK],
        out_specs=[HBM, HBM],
        scratch=[vmem(7, 32, 256), vmem(6, 32, 256)] + shared,
        input_output_aliases={11: 0, 12: 1},
    )(
        where, strain, free, kappa, part, face, plane, face_ext, got_a, got_b, rows_three,
        force, kappa_new,
    )
    return (force, kappa_new)


def solution(mesh):
    in_specs = (
        P(None, "gx", "gy", "gz"),
        P("gx", "gy", "gz"),
        P("gx", "gy", "gz"),
        P("gx", "gy", "gz"),
        P("gx", "gy", "gz"),
    )
    out_specs = (P("gx", "gy", "gz"), P("gx", "gy", "gz"))
    return jax.shard_map(body, mesh=mesh, in_specs=in_specs, out_specs=out_specs, check_vma=False)
```

```python
import functools
import math

import jax
import jax.numpy as jnp
import numpy as np
from jax import lax
from jax.experimental import pallas as pl
from jax.experimental.pallas import tpu as pltpu
from jax.sharding import PartitionSpec as P

REACH = 6
RM_ITERS = 2
LENGTH_SCALE = 3.0
HIGHEST = lax.Precision.HIGHEST
F32 = jnp.float32
VMEM_LIMIT = 40 * 1024 * 1024
INTERPRET = False


def gauss(offset):
    return math.exp(-offset * offset / (2.0 * LENGTH_SCALE * LENGTH_SCALE))


def band(offset):
    return gauss(offset) if abs(offset) <= REACH else 0.0


def z_band(width):
    return np.array([[band(i - k) for k in range(width)] for i in range(width)], np.float32)


def z_low_rows():
    out = np.zeros((128, 128), np.float32)
    for r in range(128):
        if r % 16 < 7:
            out[r] = [band(k - (r % 16 - 7)) for k in range(128)]
    return out


def z_high_rows():
    out = np.zeros((128, 128), np.float32)
    for r in range(128):
        if r % 16 < 6:
            out[r] = [band(128 + r % 16 - k) for k in range(128)]
    return out


def plane_from_low():
    out = np.zeros((40, 128), np.float32)
    for g in range(8):
        for c in range(7):
            out[g, 16 * g + c] = band(c - 6)
        for e in range(4):
            out[8 * (1 + e) + g, 16 * g + 7 + e] = 1.0
    return out


def plane_from_own():
    out = np.zeros((40, 128), np.float32)
    for g in range(8):
        for c in range(6):
            out[g, 16 * g + c] = band(c + 1)
    return out


def rows_matrix():
    out = np.zeros((40, 48), np.float32)
    for r in range(33):
        at = r if r < 32 else -1
        for k in range(1, 46):
            out[r, k] = band(k - 8 - at)
    return out


def plane_y_matrix():
    out = np.zeros((128, 128), np.float32)
    for y in range(-1, 32):
        for k in range(45):
            out[k, y + 1] = band(k - 7 - y)
    return out


def lanes(shape):
    return lax.broadcasted_iota(jnp.int32, shape, len(shape) - 1)


def rows(shape):
    return lax.broadcasted_iota(jnp.int32, shape, len(shape) - 2)


def inverse_total(position, extent):
    total = jnp.zeros(position.shape, F32)
    for offset in range(-REACH, REACH + 1):
        inside = (position + offset >= 0) & (position + offset < extent)
        total = total + jnp.where(inside, F32(gauss(offset)), F32(0.0))
    return 1.0 / total


def newton_plastic(trial, alpha_old):
    increment = jnp.zeros(trial.shape, F32)
    for _ in range(RM_ITERS):
        hardened = alpha_old + increment
        soft = 0.5 * jnp.exp(-5.0 * hardened)
        excess = trial - increment - (1.0 + 0.5 * hardened - soft)
        increment = jnp.maximum(increment + excess / (1.5 + 5.0 * soft), 0.0)
    return increment


def field_of(first, second, third):
    return first * first + second * second + third * third


def integrity_of(kappa):
    return jnp.exp(-jnp.maximum(kappa - 3.2, 0.0) / 3.0)


def by_parity(even, first, second, use):
    @pl.when(even)
    def _():
        use(first, second)

    @pl.when(jnp.logical_not(even))
    def _():
        use(second, first)


CONTRACT_LANES = (((1,), (1,)), ((), ()))
CHUNK = 8
CHUNKS = 4


def dot(left, right):
    return jnp.dot(left, right, precision=HIGHEST, preferred_element_type=F32)


def dot_lanes(left, right, precision=HIGHEST):
    return lax.dot_general(
        left, right, CONTRACT_LANES, precision=precision, preferred_element_type=F32
    )


def turned_flags(flags):
    eye = (rows((32, 32)) == lanes((32, 32))).astype(F32)
    return dot_lanes(eye, flags[...].astype(F32), None)


def pack_kernel(
    where_ref, strain_in, plastic_in, alpha_in, kappa_in, flags,
    strain, plastic, alpha, kappa, turned, z_a, z_b,
    flags_v, up_trial, up_alpha, up_drive, low_trial, low_alpha, low_drive, sems,
):
    flags_copy = pltpu.make_async_copy(flags, flags_v, sems.at[CHUNKS, 0])
    flags_copy.start()
    copies = []
    for c in range(CHUNKS):
        part = pl.ds(c * CHUNK, CHUNK)
        pairs = [(strain_in.at[:, part], strain.at[:, part])]
        pairs += [
            (src.at[part], dst.at[part])
            for src, dst in ((plastic_in, plastic), (alpha_in, alpha), (kappa_in, kappa))
        ]
        copies.append(
            [pltpu.make_async_copy(src, dst, sems.at[c, i]) for i, (src, dst) in enumerate(pairs)]
        )
    for group in copies:
        for copy in group:
            copy.start()
    flags_copy.wait()
    turned[...] = turned_flags(flags_v)
    flag = jnp.concatenate(
        [
            jnp.dot(
                turned[...],
                (rows((32, 128)) == 4 * (lanes((32, 128)) // 16) + b).astype(F32),
                preferred_element_type=F32,
            )
            for b in range(4)
        ],
        axis=0,
    )
    lane = lanes((128, 128))
    for c in range(CHUNKS):
        for copy in copies[c]:
            copy.wait()
        for g in (2 * c, 2 * c + 1):
            inside = lane // 16 == g

            def tile(ref, half):
                cells = ref[4 * g : 4 * g + 4, :, 128 * half : 128 * half + 128]
                return cells.reshape(128, 128)

            def place(ref, value, move):
                moved = pltpu.roll(value, (move + 16 * g) % 128, 1) if move + 16 * g else value
                ref[...] = jnp.where(inside, moved, ref[...])

            s0, s1, s2 = (tile(strain.at[i], 1) for i in range(3))
            place(up_trial, s0 - tile(plastic, 1), 7)
            place(up_alpha, tile(alpha, 1), 7)
            place(up_drive, field_of(s0, s1, s2), 7)
            mixed = up_drive[...]
            for e, value in enumerate((s1, s2, tile(kappa, 1))):
                moved = pltpu.roll(value, (9 + e + 16 * g) % 128, 1)
                mixed = jnp.where(lane == 16 * g + 8 + e, moved, mixed)
            up_drive[...] = mixed
            s0, s1, s2 = (tile(strain.at[i], 0) for i in range(3))
            place(low_trial, s0 - tile(plastic, 0), 0)
            place(low_alpha, tile(alpha, 0), 0)
            place(low_drive, field_of(s0, s1, s2), 0)

    increment = newton_plastic(up_trial[...], up_alpha[...]) * flag
    free = pltpu.roll(up_trial[...] - increment, 1, 1)
    up_drive[...] = jnp.where(
        lane % 16 < 7,
        up_drive[...] + 4.0 * increment,
        jnp.where(lane % 16 == 7, free, up_drive[...]),
    )
    increment = newton_plastic(low_trial[...], low_alpha[...]) * flag
    low_drive[...] = low_drive[...] + 4.0 * increment

    def store(upper, lower):
        upper[...] = up_drive[...]
        lower[...] = low_drive[...]

    by_parity(lax.rem(where_ref[2], 2) == 0, z_a, z_b, store)


def inner_kernel(strain, plastic, alpha, kappa, turned, bz, smooth, free, yext, xext, field):
    @pl.loop(0, 8)
    def _(g):
        for i in range(4):
            x = 4 * g + i
            here = (rows((32, 256)) == x).astype(F32)
            flag = jnp.dot(turned[...], here, preferred_element_type=F32)
            s0 = strain[0, x]
            trial = s0 - plastic[x]
            increment = newton_plastic(trial, alpha[x]) * flag
            field[x] = field_of(s0, strain[1, x], strain[2, x]) + 4.0 * increment
            free[x] = trial - increment

    for g in range(4):
        part = field[8 * g : 8 * g + 8].reshape(256, 256)
        smooth[8 * g : 8 * g + 8] = dot(part, bz[...]).reshape(8, 32, 256)
    for e, ref in enumerate((free, strain.at[1], strain.at[2], kappa)):
        xext[e] = ref[31]
        for x in range(32):
            yext[e, x : x + 1, :] = ref[x, 31:32, :]


def z_kernel(
    where_ref, own, yext_in, xext_in, sent_a, sent_b, got_a, got_b, t_low, t_high, w_low, w_own,
    plane, y_a, y_b, z_low, z_high, yext, xext,
    own_low, head_rows, tail_rows, some_low, some_high, ends,
):
    yext[...] = yext_in[...]
    xext[...] = xext_in[...]

    def choose(upper, lower):
        z_high[...] = upper[0][...]
        z_low[...] = lower[0][...]
        own_low[...] = lower[1][...]

    by_parity(lax.rem(where_ref[2], 2) == 0, (got_a, sent_a), (got_b, sent_b), choose)
    group = lanes((8, 128)) // 16
    for half in range(2):
        for x in range(32):
            start = 32 * (x % 4) + 24 * half
            at = 256 * half + 8 * x
            inside = group == x // 4
            for some, ref in ((some_low, z_low), (some_high, z_high)):
                some[at : at + 8, :] = jnp.where(inside, ref[start : start + 8, :], 0.0)
    first = dot(some_low[...], t_low[...])
    last = dot(some_high[...], t_high[...])
    for half in range(2):
        part = slice(256 * half, 256 * half + 256)
        here = slice(24 * half, 24 * half + 8)
        ends[half, :, :, 0:128] = own[:, here, 0:128] + first[part].reshape(32, 8, 128)
        ends[half, :, :, 128:256] = own[:, here, 128:256] + last[part].reshape(32, 8, 128)
    turned = dot_lanes(w_low[...], z_low[...]) + dot_lanes(w_own[...], own_low[...])
    lane = lanes((8, 128))
    for b in range(4):
        head = jnp.zeros((8, 128), F32)
        for c in range(4):
            moved = pltpu.roll(turned[8 * c : 8 * c + 8], (32 * (c - b)) % 128, 1)
            head = jnp.where(lane // 32 == c, moved, head)
        tail = jnp.where(lane < 32, pltpu.roll(turned[32:40], (-32 * b) % 128, 1), 0.0)
        head_rows[pl.ds(b, 8, stride=4), :] = head
        tail_rows[pl.ds(b, 8, stride=4), :] = tail
    plane[:, 0:128] = head_rows[...]
    plane[:, 128:256] = tail_rows[...]

    def store(upper, lower):
        for j in range(7):
            upper[j] = ends[1, :, 1 + j, :]
        upper[7] = plane[...]
        for j in range(6):
            lower[j] = ends[0, :, j, :]
        lower[6] = plane[...]
        lower[7] = plane[...]

    by_parity(lax.rem(where_ref[1], 2) == 0, y_a, y_b, store)


def own_rows_kernel(own, z_low, z_high, t_low, t_high, my, out, out_face, some, smooth):
    group = lanes((128, 128)) // 16
    for half, (ref, band_rows) in enumerate(((z_low, t_low), (z_high, t_high))):
        for g in range(8):
            some[128 * g : 128 * g + 128, :] = jnp.where(group == g, ref[...], 0.0)
        here = slice(128 * half, 128 * half + 128)
        for c in range(4):
            part = dot(some[256 * c : 256 * c + 256, :], band_rows[...])
            at = slice(8 * c, 8 * c + 8)
            smooth[at, :, here] = own[at, :, here] + part.reshape(8, 32, 128)
    for x in range(32):
        both = dot(my[...], smooth[x])
        out[x] = both[0:32]
        out_face[x : x + 1, :] = both[32:33]


def y_kernel(
    where_ref, own, own_face, plane, got_a, got_b, face_ext, _, my, v,
    edges, out_face, out_plane, halo, x_a, x_b, plane_low, plane_high,
):
    def choose(upper, lower):
        for j in range(7):
            halo[:, j, :] = lower[j]
        for j in range(6):
            halo[:, 8 + j, :] = upper[j]
        plane_low[...] = lower[7]
        plane_high[...] = upper[7]

    halo[:, 0:8, :] = jnp.zeros((32, 8, 256), F32)
    halo[:, 8:16, :] = jnp.zeros((32, 8, 256), F32)
    by_parity(lax.rem(where_ref[1], 2) == 0, got_a, got_b, choose)
    out_face[8:24, :] = own_face[8:24, :]
    for i in range(16):
        x = i if i < 8 else i + 16
        both = dot(my[...], halo[x])
        edges[i] = own[x] + both[0:32]
        out_face[x : x + 1, :] = own_face[x : x + 1, :] + both[32:33]
    mine, low, high = plane[...], plane_low[...], plane_high[...]
    lane = lanes((32, 256))
    total = jnp.zeros((32, 256), F32)
    for c in range(1, 5):
        inside = (lane > 40 * c) & (lane <= 40 * c + 32)
        total = jnp.where(inside, pltpu.roll(mine, 8 * c + 1, 1), total)
        total = jnp.where(lane == 40 * c, pltpu.roll(low, (8 * c - 31) % 256, 1), total)
    wide = jnp.where(
        lane < 7,
        pltpu.roll(low, 256 - 25, 1),
        jnp.where(lane < 39, pltpu.roll(mine, 7, 1), jnp.where(lane < 45, pltpu.roll(high, 39, 1), 0.0)),
    )
    smoothed = dot(wide[:, 0:128], v[...])
    out_plane[:, 0:128] = jnp.where(lanes((32, 128)) < 40, smoothed, total[:, 0:128])
    out_plane[:, 128:256] = total[:, 128:256]

    def store(upper, lower):
        for j in range(7):
            upper[j] = edges[9 + j]
        upper[7] = jnp.zeros((32, 256), F32)
        upper[7, 0:8, :] = out_face[24:32, :]
        for e in range(4):
            corner = face_ext[e, 31:32, :]
            upper[7, 8 + e : 9 + e, :] = jnp.where(where_ref[1] == 0, 0.0, corner)
        upper[7, 16:24, :] = out_plane[24:32, :]
        for j in range(6):
            lower[j] = edges[j]
        lower[6] = jnp.zeros((32, 256), F32)
        lower[7] = jnp.zeros((32, 256), F32)
        lower[7, 0:8, :] = out_face[0:8, :]
        lower[7, 16:24, :] = out_plane[0:8, :]

    by_parity(lax.rem(where_ref[0], 2) == 0, x_a, x_b, store)


def fill_side(at, side, face_ext):
    for e in range(4):
        side[e, 0:32, :] = face_ext[e]
        side[e, 32:40, :] = jnp.zeros((8, 256), F32)

    @pl.when(at[1] == 0)
    def _():
        side[...] = jnp.zeros_like(side)


def faces(extents, at, mx, face_all, plane_all, side, face_e, face_a, column, inv_x, inv_yz):
    nx, ny, nz = extents
    ix, iy, iz = at
    shape = (40, 256)
    row, lane = rows(shape), lanes(shape)
    invx = inverse_total(ix * 32 + jnp.where(row < 32, row, -1), nx)
    inv_x[...] = invx
    small = (32, 256)
    invz = inverse_total(iz * 256 + lanes(small), nz)
    inv_yz[...] = inverse_total(iy * 32 + rows(small), ny) * invz

    def previous(value):
        return jnp.where(row == 0, value[32:33, :], pltpu.roll(value, 1, 0))

    def joined(t0, t1, t2):
        a0 = previous(t0) - t0
        a1 = previous(t1) + t1
        a2 = previous(t2) + t2
        return a0 + a1, a0 - a1, a2

    at_y = inverse_total(jnp.full((1, 256), iy * 32 - 1, jnp.int32), ny)
    kap = jnp.maximum(side[3], dot(mx[...], face_all[...]) * (invx * (at_y * invz[0:1, :])))
    integ = integrity_of(kap)
    e, _, a2 = joined(integ * side[0], integ * side[1], integ * side[2])
    face_e[...] = e[0:32]
    face_a[...] = a2[0:32]

    avg = dot(mx[...], plane_all[...])
    own = jnp.where(row == 32, plane_all[7:8, :], plane_all[8:48, :])

    def value(c):
        return pltpu.roll(own, (256 - 40 * c) % 256, 1)

    at_z = inverse_total(jnp.full((1, 256), iz * 256 - 1, jnp.int32), nz)
    invy = inverse_total(iy * 32 - 1 + jnp.minimum(lane, 32), ny)
    kap = jnp.maximum(value(4), avg * (invx * (invy * at_z)))
    integ = integrity_of(kap)
    e, f, a2 = joined(integ * value(1), integ * value(2), integ * value(3))
    parts = e + a2 + pltpu.roll(f + a2, 255, 1)
    parts = jnp.where(lane < 32, parts, 0.0)
    eye = (rows((32, 128)) == lanes((32, 128))).astype(F32)
    pad = jnp.concatenate([parts[0:32, 0:128], jnp.zeros((96, 128), F32)], axis=0)
    column[...] = dot_lanes(eye, pad)


def layer_results(x, avg, kappa, free, strain, before, face_e, face_a, column, force_at, kappa_at):
    first_row = rows((32, 256)) == 0
    first_lane = lanes((32, 128)) == 0
    kap = jnp.maximum(kappa[x], avg)
    integ = integrity_of(kap)
    s0, s1, s2 = integ * free[x], integ * strain[1, x], integ * strain[2, x]
    if force_at is not None:
        kappa_at[...] = kap
        a0 = before[0] - s0
        a1 = before[1] + s1
        a2 = before[2] + s2
        e, f = a0 + a1, a0 - a1
        b = f + jnp.where(first_row, face_e[pl.ds(x, 1), :], pltpu.roll(e, 1, 0))
        c = a2 + jnp.where(first_row, face_a[pl.ds(x, 1), :], pltpu.roll(a2, 1, 0))
        p, q = b + c, b - c
        moved = pltpu.roll(p, 1, 1)
        edge = pltpu.roll(column[...], lax.rem(128 - x, 128), 1)
        force_at[:, 0:128] = 0.25 * (q[:, 0:128] + jnp.where(first_lane, edge, moved[:, 0:128]))
        force_at[:, 128:256] = 0.25 * (q[:, 128:256] + moved[:, 128:256])
    before[0] = s0
    before[1] = s1
    before[2] = s2


def middle_kernel(
    extents, where_ref, strain, free, kappa, own, edges, halo, face, plane, face_ext, my,
    force, kappa_new, part, face_out,
    ext, face_all, plane_all, side, before, face_e, face_a, column, inv_x, inv_yz,
    force_v, kappa_v, sems,
):
    at = (where_ref[0], where_ref[1], where_ref[2])
    for x in range(32):
        if x < 8:
            ext[x] = edges[x]
        elif x >= 24:
            ext[x] = edges[x - 16]
        else:
            both = dot(my[:, 32:48], halo[x])
            ext[x] = own[x] + both[0:32]
            face_out[x : x + 1, :] = face[x : x + 1, :] + both[32:33]
    face_out[0:8, :] = face[0:8, :]
    face_out[24:32, :] = face[24:32, :]
    for ref, value in ((face_all, face_out), (plane_all, plane)):
        ref[0:8, :] = jnp.zeros((8, 256), F32)
        ref[8:40, :] = value[...]
        ref[40:48, :] = jnp.zeros((8, 256), F32)
    fill_side(at, side, face_ext)
    faces(
        extents, at, my.at[:, 48:96], face_all, plane_all, side,
        face_e, face_a, column, inv_x, inv_yz,
    )

    def layer(x):
        total = gauss(0) * ext[x]
        for a in range(1, REACH + 1):
            total = total + gauss(a) * (ext[x - a] + ext[x + a])
        return total * (inv_x[pl.ds(x, 1), :] * inv_yz[...])

    layer_results(7, layer(7), kappa, free, strain, before, None, None, None, None, None)
    copies = []
    for c in (1, 2):

        @pl.loop(0, CHUNK)
        def _(i):
            x = c * CHUNK + i
            layer_results(
                x, layer(x), kappa, free, strain, before, face_e, face_a, column,
                force_v.at[x - CHUNK], kappa_v.at[x - CHUNK],
            )

        here = pl.ds((c - 1) * CHUNK, CHUNK)
        there = pl.ds(c * CHUNK, CHUNK)
        for k, (src, dst) in enumerate(((force_v, force), (kappa_v, kappa_new))):
            copy = pltpu.make_async_copy(src.at[here], dst.at[there], sems.at[c - 1, k])
            copy.start()
            copies.append(copy)
    for i in range(18):
        x = i - 1 if i < 9 else i + 14
        total = None
        for a in range(-REACH, REACH + 1):
            if 0 <= x + a < 32:
                term = gauss(a) * ext[x + a]
                total = term if total is None else total + term
        part[i] = total
    for copy in copies:
        copy.wait()


def outer_kernel(
    extents, where_ref, strain, free, kappa, part, face, plane, face_ext, got_a, got_b, got_ext, my,
    force_in, kappa_in,
    force, kappa_new,
    low, high, face_all, plane_all, side, before, face_e, face_a, column, inv_x, inv_yz,
    force_v, kappa_v, sems,
):
    at = (where_ref[0], where_ref[1], where_ref[2])

    def choose(upper, lower):
        for j in range(7):
            low[j] = lower[j]
        for j in range(6):
            high[j] = upper[j]
        face_all[0:8, :] = lower[7, 0:8, :]
        face_all[40:48, :] = upper[7, 0:8, :]
        plane_all[0:8, :] = lower[7, 16:24, :]
        plane_all[40:48, :] = upper[7, 16:24, :]
        for e in range(4):
            side[e, 32:33, :] = lower[7, 8 + e : 9 + e, :]

    fill_side(at, side, face_ext)
    by_parity(lax.rem(at[0], 2) == 0, got_a, got_b, choose)
    before[...] = got_ext[...]

    @pl.when(at[0] == 0)
    def _():
        low[...] = jnp.zeros_like(low)
        before[...] = jnp.zeros_like(before)
        face_all[0:8, :] = jnp.zeros((8, 256), F32)
        plane_all[0:8, :] = jnp.zeros((8, 256), F32)
        for e in range(4):
            side[e, 32:33, :] = jnp.zeros((1, 256), F32)

    @pl.when(at[0] == extents[0] // 32 - 1)
    def _():
        high[...] = jnp.zeros_like(high)
        face_all[40:48, :] = jnp.zeros((8, 256), F32)
        plane_all[40:48, :] = jnp.zeros((8, 256), F32)

    face_all[8:40, :] = face[...]
    plane_all[8:40, :] = plane[...]
    faces(
        extents, at, my.at[:, 48:96], face_all, plane_all, side,
        face_e, face_a, column, inv_x, inv_yz,
    )

    def layer(x):
        total = part[x + 1 if x < 8 else x - 14]
        for a in range(-REACH, REACH + 1):
            if x + a < 0:
                total = total + gauss(a) * low[x + a + 7]
            elif x + a >= 32:
                total = total + gauss(a) * high[x + a - 32]
        return total * (inv_x[x % 33 : x % 33 + 1, :] * inv_yz[...])

    kap = jnp.maximum(before[3], layer(-1))
    integ = integrity_of(kap)
    for e in range(3):
        before[e] = integ * before[e]
    copies = []
    for c in (0, 3):
        if c == 3:
            layer_results(23, layer(23), kappa, free, strain, before, None, None, None, None, None)
        for i in range(CHUNK):
            x = c * CHUNK + i
            slot = i if c == 0 else CHUNK + i
            layer_results(
                x, layer(x), kappa, free, strain, before, face_e, face_a, column,
                force_v.at[slot], kappa_v.at[slot],
            )
        here = pl.ds(0 if c == 0 else CHUNK, CHUNK)
        there = pl.ds(c * CHUNK, CHUNK)
        for k, (src, dst) in enumerate(((force_v, force), (kappa_v, kappa_new))):
            copy = pltpu.make_async_copy(src.at[here], dst.at[there], sems.at[c // 3, k])
            copy.start()
            copies.append(copy)
    for copy in copies:
        copy.wait()


def swap(first, second, axis, around=False):
    count = lax.axis_size(axis)

    def route(start):
        out = []
        for i in range(start, count - 1, 2):
            out += [(i, i + 1), (i + 1, i)]
        if start and around:
            out += [(count - 1, 0), (0, count - 1)]
        return out

    return lax.ppermute(first, axis, route(0)), lax.ppermute(second, axis, route(1))


def to_next(block, axis):
    count = lax.axis_size(axis)
    return lax.ppermute(block, axis, [(i, (i + 1) % count) for i in range(count)])


def shape_of(*dims):
    return jax.ShapeDtypeStruct(dims, F32)


VM = pl.BlockSpec(memory_space=pltpu.VMEM)
SM = pl.BlockSpec(memory_space=pltpu.SMEM)
HBM = pl.BlockSpec(memory_space=pltpu.HBM)
BLOCK = shape_of(32, 32, 256)
FACE = shape_of(32, 256)


def vmem(*dims):
    return pltpu.VMEM(dims, F32)


def call(kernel, name, in_specs, out_shape, out_specs=None, scratch=(), **kwargs):
    return pl.pallas_call(
        kernel,
        name=name,
        in_specs=in_specs,
        out_specs=out_specs or [VM] * len(out_shape),
        out_shape=out_shape,
        scratch_shapes=list(scratch),
        interpret=INTERPRET,
        compiler_params=pltpu.CompilerParams(vmem_limit_bytes=VMEM_LIMIT),
        **kwargs,
    )


def body(strain_in, plastic_in, alpha_in, kappa_in, flags):
    where = jnp.stack([lax.axis_index(a) for a in ("gx", "gy", "gz")]).astype(jnp.int32)
    flags = flags.reshape(32, 32)
    extents = (
        32 * lax.axis_size("gx"), 32 * lax.axis_size("gy"), 256 * lax.axis_size("gz"),
    )
    rows_all = rows_matrix()
    rows_own = np.ascontiguousarray(rows_all[:, 8:40])
    rows_halo = np.concatenate(
        [rows_all[:, 1:8], np.zeros((40, 1), np.float32), rows_all[:, 40:48]], axis=1
    )
    rows_three = np.zeros((40, 128), np.float32)
    rows_three[:, 32:48] = rows_halo
    rows_three[:, 48:96] = rows_all

    whole_in = [
        pltpu.with_memory_space_constraint(v, pltpu.HBM)
        for v in (strain_in, plastic_in, alpha_in, kappa_in, flags)
    ]
    ends, eight = shape_of(4, 32, 256), shape_of(8, 32, 256)
    square = shape_of(128, 128)
    strain, plastic, alpha, kappa, turned, z_a, z_b = call(
        pack_kernel,
        "pack",
        [SM] + [HBM] * 5,
        [shape_of(3, 32, 32, 256), BLOCK, BLOCK, BLOCK, shape_of(32, 32), square, square],
        scratch=[pltpu.VMEM((32, 32), jnp.int32)] + [vmem(128, 128)] * 6
        + [pltpu.SemaphoreType.DMA((CHUNKS + 1, 4))],
    )(where, *whole_in)
    got_a, got_b = swap(z_a, z_b, "gz")
    own, free, yext, xext = call(
        inner_kernel, "inner", [VM] * 6, [BLOCK, BLOCK, ends, ends], scratch=[vmem(32, 32, 256)]
    )(strain, plastic, alpha, kappa, turned, z_band(256))
    t_low, t_high = z_low_rows(), z_high_rows()
    plane, y_a, y_b, z_low, z_high, yext, xext = call(
        z_kernel,
        "along_z",
        [SM] + [VM] * 11,
        [FACE, eight, eight, square, square, ends, ends],
        scratch=[vmem(128, 128)] + [vmem(32, 128)] * 2 + [vmem(512, 128)] * 2
        + [vmem(2, 32, 8, 256)],
    )(
        where, own, yext, xext, z_a, z_b, got_a, got_b,
        t_low, t_high, plane_from_low(), plane_from_own(),
    )
    got_a, got_b = swap(y_a, y_b, "gy")
    face_ext = to_next(yext, "gy")
    got_ext = to_next(xext, "gx")
    own, own_face = call(
        own_rows_kernel,
        "own_rows",
        [VM] * 6,
        [BLOCK, FACE],
        scratch=[vmem(1024, 128), vmem(32, 32, 256)],
    )(own, z_low, z_high, t_low, t_high, rows_own)

    edges, face, plane, halo, x_a, x_b = call(
        y_kernel,
        "along_y",
        [SM] + [VM] * 9,
        [shape_of(16, 32, 256), FACE, FACE, shape_of(32, 16, 256), eight, eight],
        scratch=[vmem(32, 256), vmem(32, 256)],
    )(where, own, own_face, plane, got_a, got_b, face_ext, got_ext, rows_halo, plane_y_matrix())
    got_a, got_b = swap(x_a, x_b, "gx", around=True)

    shared = [
        vmem(48, 256), vmem(48, 256), vmem(4, 40, 256), vmem(4, 32, 256),
        vmem(32, 256), vmem(32, 256), vmem(32, 128), vmem(40, 256), vmem(32, 256),
        vmem(16, 32, 256), vmem(16, 32, 256), pltpu.SemaphoreType.DMA((2, 2)),
    ]
    force, kappa_new, part, face = call(
        functools.partial(middle_kernel, extents),
        "middle",
        [SM] + [VM] * 10,
        [BLOCK, BLOCK, shape_of(18, 32, 256), FACE],
        out_specs=[HBM, HBM, VM, VM],
        scratch=[vmem(32, 32, 256)] + shared,
    )(where, strain, free, kappa, own, edges, halo, face, plane, face_ext, rows_three)
    force, kappa_new = call(
        functools.partial(outer_kernel, extents),
        "outer",
        [SM] + [VM] * 11 + [HBM, HBM],
        [BLOCK, BLOCK],
        out_specs=[HBM, HBM],
        scratch=[vmem(7, 32, 256), vmem(6, 32, 256)] + shared,
        input_output_aliases={12: 0, 13: 1},
    )(
        where, strain, free, kappa, part, face, plane, face_ext, got_a, got_b, got_ext, rows_three,
        force, kappa_new,
    )
    return (force, kappa_new)


def solution(mesh):
    in_specs = (
        P(None, "gx", "gy", "gz"),
        P("gx", "gy", "gz"),
        P("gx", "gy", "gz"),
        P("gx", "gy", "gz"),
        P("gx", "gy", "gz"),
    )
    out_specs = (P("gx", "gy", "gz"), P("gx", "gy", "gz"))
    return jax.shard_map(body, mesh=mesh, in_specs=in_specs, out_specs=out_specs, check_vma=False)
```

```python
import functools
import math

import jax
import jax.numpy as jnp
import numpy as np
from jax import lax
from jax.experimental import pallas as pl
from jax.experimental.pallas import tpu as pltpu
from jax.sharding import PartitionSpec as P

REACH = 6
RM_ITERS = 2
LENGTH_SCALE = 3.0
HIGHEST = lax.Precision.HIGHEST
F32 = jnp.float32
VMEM_LIMIT = 40 * 1024 * 1024
INTERPRET = False


def gauss(offset):
    return math.exp(-offset * offset / (2.0 * LENGTH_SCALE * LENGTH_SCALE))


def band(offset):
    return gauss(offset) if abs(offset) <= REACH else 0.0


def z_band(width):
    return np.array([[band(i - k) for k in range(width)] for i in range(width)], np.float32)


def z_low_rows():
    out = np.zeros((128, 128), np.float32)
    for r in range(128):
        if r % 16 < 7:
            out[r] = [band(k - (r % 16 - 7)) for k in range(128)]
    return out


def z_high_rows():
    out = np.zeros((128, 128), np.float32)
    for r in range(128):
        if r % 16 < 6:
            out[r] = [band(128 + r % 16 - k) for k in range(128)]
    return out


def plane_from_low():
    out = np.zeros((40, 128), np.float32)
    for g in range(8):
        for c in range(7):
            out[g, 16 * g + c] = band(c - 6)
        for e in range(4):
            out[8 * (1 + e) + g, 16 * g + 7 + e] = 1.0
    return out


def plane_from_own():
    out = np.zeros((40, 128), np.float32)
    for g in range(8):
        for c in range(6):
            out[g, 16 * g + c] = band(c + 1)
    return out


def rows_matrix():
    out = np.zeros((40, 48), np.float32)
    for r in range(33):
        at = r if r < 32 else -1
        for k in range(1, 46):
            out[r, k] = band(k - 8 - at)
    return out


def plane_y_matrix():
    out = np.zeros((128, 128), np.float32)
    for y in range(-1, 32):
        for k in range(45):
            out[k, y + 1] = band(k - 7 - y)
    return out


def lanes(shape):
    return lax.broadcasted_iota(jnp.int32, shape, len(shape) - 1)


def rows(shape):
    return lax.broadcasted_iota(jnp.int32, shape, len(shape) - 2)


def inverse_total(position, extent):
    total = jnp.zeros(position.shape, F32)
    for offset in range(-REACH, REACH + 1):
        inside = (position + offset >= 0) & (position + offset < extent)
        total = total + jnp.where(inside, F32(gauss(offset)), F32(0.0))
    return 1.0 / total


def newton_plastic(trial, alpha_old):
    increment = jnp.zeros(trial.shape, F32)
    for _ in range(RM_ITERS):
        hardened = alpha_old + increment
        soft = 0.5 * jnp.exp(-5.0 * hardened)
        excess = trial - increment - (1.0 + 0.5 * hardened - soft)
        increment = jnp.maximum(increment + excess / (1.5 + 5.0 * soft), 0.0)
    return increment


def field_of(first, second, third):
    return first * first + second * second + third * third


def integrity_of(kappa):
    return jnp.exp(-jnp.maximum(kappa - 3.2, 0.0) / 3.0)


def by_parity(even, first, second, use):
    @pl.when(even)
    def _():
        use(first, second)

    @pl.when(jnp.logical_not(even))
    def _():
        use(second, first)


CONTRACT_LANES = (((1,), (1,)), ((), ()))
CHUNK = 8
CHUNKS = 4


def dot(left, right):
    return jnp.dot(left, right, precision=HIGHEST, preferred_element_type=F32)


def dot_lanes(left, right, precision=HIGHEST):
    return lax.dot_general(
        left, right, CONTRACT_LANES, precision=precision, preferred_element_type=F32
    )


def turned_flags(flags):
    eye = (rows((32, 32)) == lanes((32, 32))).astype(F32)
    return dot_lanes(eye, flags[...].astype(F32), None)


def pack_kernel(
    where_ref, strain_in, plastic_in, alpha_in, kappa_in, flags,
    strain, plastic, alpha, kappa, turned, z_a, z_b, yext, xext,
    flags_v, up_trial, up_alpha, up_drive, low_trial, low_alpha, low_drive, sems,
):
    flags_copy = pltpu.make_async_copy(flags, flags_v, sems.at[CHUNKS, 0])
    flags_copy.start()
    copies = []
    for c in range(CHUNKS):
        part = pl.ds(c * CHUNK, CHUNK)
        pairs = [(strain_in.at[:, part], strain.at[:, part])]
        pairs += [
            (src.at[part], dst.at[part])
            for src, dst in ((plastic_in, plastic), (alpha_in, alpha), (kappa_in, kappa))
        ]
        copies.append(
            [pltpu.make_async_copy(src, dst, sems.at[c, i]) for i, (src, dst) in enumerate(pairs)]
        )
    for group in copies:
        for copy in group:
            copy.start()
    flags_copy.wait()
    turned[...] = turned_flags(flags_v)
    flag = jnp.concatenate(
        [
            jnp.dot(
                turned[...],
                (rows((32, 128)) == 4 * (lanes((32, 128)) // 16) + b).astype(F32),
                preferred_element_type=F32,
            )
            for b in range(4)
        ],
        axis=0,
    )
    lane = lanes((128, 128))
    for c in range(CHUNKS):
        for copy in copies[c]:
            copy.wait()
        for g in (2 * c, 2 * c + 1):
            inside = lane // 16 == g

            def tile(ref, half):
                cells = ref[4 * g : 4 * g + 4, :, 128 * half : 128 * half + 128]
                return cells.reshape(128, 128)

            def place(ref, value, move):
                moved = pltpu.roll(value, (move + 16 * g) % 128, 1) if move + 16 * g else value
                ref[...] = jnp.where(inside, moved, ref[...])

            s0, s1, s2 = (tile(strain.at[i], 1) for i in range(3))
            place(up_trial, s0 - tile(plastic, 1), 7)
            place(up_alpha, tile(alpha, 1), 7)
            place(up_drive, field_of(s0, s1, s2), 7)
            mixed = up_drive[...]
            for e, value in enumerate((s1, s2, tile(kappa, 1))):
                moved = pltpu.roll(value, (9 + e + 16 * g) % 128, 1)
                mixed = jnp.where(lane == 16 * g + 8 + e, moved, mixed)
            up_drive[...] = mixed
            s0, s1, s2 = (tile(strain.at[i], 0) for i in range(3))
            place(low_trial, s0 - tile(plastic, 0), 0)
            place(low_alpha, tile(alpha, 0), 0)
            place(low_drive, field_of(s0, s1, s2), 0)

    trial = strain[0, 31] - plastic[31]
    here = (rows((32, 256)) == 31).astype(F32)
    flag_x = jnp.dot(turned[...], here, preferred_element_type=F32)
    xext[0] = trial - newton_plastic(trial, alpha[31]) * flag_x
    trial = strain[0, :, 31, :] - plastic[:, 31, :]
    flag_y = jnp.broadcast_to(flags_v[:, 31:32].astype(F32), (32, 256))
    yext[0] = trial - newton_plastic(trial, alpha[:, 31, :]) * flag_y
    for e, ref in enumerate((strain.at[1], strain.at[2], kappa)):
        xext[1 + e] = ref[31]
        yext[1 + e] = ref[:, 31, :]

    increment = newton_plastic(up_trial[...], up_alpha[...]) * flag
    free = pltpu.roll(up_trial[...] - increment, 1, 1)
    up_drive[...] = jnp.where(
        lane % 16 < 7,
        up_drive[...] + 4.0 * increment,
        jnp.where(lane % 16 == 7, free, up_drive[...]),
    )
    increment = newton_plastic(low_trial[...], low_alpha[...]) * flag
    low_drive[...] = low_drive[...] + 4.0 * increment

    def store(upper, lower):
        upper[...] = up_drive[...]
        lower[...] = low_drive[...]

    by_parity(lax.rem(where_ref[2], 2) == 0, z_a, z_b, store)


def inner_kernel(strain, plastic, alpha, turned, bz, smooth, free, field):
    @pl.loop(0, 8)
    def _(g):
        for i in range(4):
            x = 4 * g + i
            here = (rows((32, 256)) == x).astype(F32)
            flag = jnp.dot(turned[...], here, preferred_element_type=F32)
            s0 = strain[0, x]
            trial = s0 - plastic[x]
            increment = newton_plastic(trial, alpha[x]) * flag
            field[x] = field_of(s0, strain[1, x], strain[2, x]) + 4.0 * increment
            free[x] = trial - increment

    for g in range(4):
        part = field[8 * g : 8 * g + 8].reshape(256, 256)
        smooth[8 * g : 8 * g + 8] = dot(part, bz[...]).reshape(8, 32, 256)


def z_kernel(
    counts, where_ref, own, xext_in, sent_a, sent_b, got_a, got_b, _, t_low, t_high, w_low, w_own,
    plane, y_a, y_b, z_low, z_high, xext,
    own_low, head_rows, tail_rows, some_low, some_high, ends,
):
    xext[...] = xext_in[...]

    def choose(upper, lower):
        z_high[...] = upper[0][...]
        z_low[...] = lower[0][...]
        own_low[...] = lower[1][...]

    by_parity(lax.rem(where_ref[2], 2) == 0, (got_a, sent_a), (got_b, sent_b), choose)

    @pl.when(where_ref[2] == 0)
    def _():
        z_low[...] = jnp.zeros_like(z_low)

    @pl.when(where_ref[2] == counts[2] - 1)
    def _():
        z_high[...] = jnp.zeros_like(z_high)

    group = lanes((8, 128)) // 16
    for half in range(2):
        for x in range(32):
            start = 32 * (x % 4) + 24 * half
            at = 256 * half + 8 * x
            inside = group == x // 4
            for some, ref in ((some_low, z_low), (some_high, z_high)):
                some[at : at + 8, :] = jnp.where(inside, ref[start : start + 8, :], 0.0)
    first = dot(some_low[...], t_low[...])
    last = dot(some_high[...], t_high[...])
    for half in range(2):
        part = slice(256 * half, 256 * half + 256)
        here = slice(24 * half, 24 * half + 8)
        ends[half, :, :, 0:128] = own[:, here, 0:128] + first[part].reshape(32, 8, 128)
        ends[half, :, :, 128:256] = own[:, here, 128:256] + last[part].reshape(32, 8, 128)
    turned = dot_lanes(w_low[...], z_low[...]) + dot_lanes(w_own[...], own_low[...])
    lane = lanes((8, 128))
    for b in range(4):
        head = jnp.zeros((8, 128), F32)
        for c in range(4):
            moved = pltpu.roll(turned[8 * c : 8 * c + 8], (32 * (c - b)) % 128, 1)
            head = jnp.where(lane // 32 == c, moved, head)
        tail = jnp.where(lane < 32, pltpu.roll(turned[32:40], (-32 * b) % 128, 1), 0.0)
        head_rows[pl.ds(b, 8, stride=4), :] = head
        tail_rows[pl.ds(b, 8, stride=4), :] = tail
    plane[:, 0:128] = head_rows[...]
    plane[:, 128:256] = tail_rows[...]

    def store(upper, lower):
        for j in range(7):
            upper[j] = ends[1, :, 1 + j, :]
        upper[7] = plane[...]
        for j in range(6):
            lower[j] = ends[0, :, j, :]
        lower[6] = plane[...]
        lower[7] = plane[...]

    by_parity(lax.rem(where_ref[1], 2) == 0, y_a, y_b, store)


def own_rows_kernel(own, z_low, z_high, t_low, t_high, my, out, out_face, some, smooth):
    group = lanes((128, 128)) // 16
    for half, (ref, band_rows) in enumerate(((z_low, t_low), (z_high, t_high))):
        for g in range(8):
            some[128 * g : 128 * g + 128, :] = jnp.where(group == g, ref[...], 0.0)
        here = slice(128 * half, 128 * half + 128)
        for c in range(4):
            part = dot(some[256 * c : 256 * c + 256, :], band_rows[...])
            at = slice(8 * c, 8 * c + 8)
            smooth[at, :, here] = own[at, :, here] + part.reshape(8, 32, 128)
    for x in range(32):
        both = dot(my[...], smooth[x])
        out[x] = both[0:32]
        out_face[x : x + 1, :] = both[32:33]


def y_kernel(
    counts, where_ref, own, own_face, plane, got_a, got_b, face_ext, ext_a, ext_b, my, v,
    edges, out_face, out_plane, halo, x_a, x_b, got_ext, plane_low, plane_high,
):
    def choose(upper, lower):
        for j in range(7):
            halo[:, j, :] = lower[j]
        for j in range(6):
            halo[:, 8 + j, :] = upper[j]
        plane_low[...] = lower[7]
        plane_high[...] = upper[7]

    halo[:, 7, :] = jnp.zeros((32, 256), F32)
    halo[:, 14, :] = jnp.zeros((32, 256), F32)
    halo[:, 15, :] = jnp.zeros((32, 256), F32)
    by_parity(lax.rem(where_ref[1], 2) == 0, got_a, got_b, choose)

    @pl.when(where_ref[1] == 0)
    def _():
        halo[:, 0:8, :] = jnp.zeros((32, 8, 256), F32)
        plane_low[...] = jnp.zeros_like(plane_low)

    @pl.when(where_ref[1] == counts[1] - 1)
    def _():
        halo[:, 8:16, :] = jnp.zeros((32, 8, 256), F32)
        plane_high[...] = jnp.zeros_like(plane_high)

    out_face[8:24, :] = own_face[8:24, :]
    for i in range(16):
        x = i if i < 8 else i + 16
        both = dot(my[...], halo[x])
        edges[i] = own[x] + both[0:32]
        out_face[x : x + 1, :] = own_face[x : x + 1, :] + both[32:33]
    mine, low, high = plane[...], plane_low[...], plane_high[...]
    lane = lanes((32, 256))
    total = jnp.zeros((32, 256), F32)
    for c in range(1, 5):
        inside = (lane > 40 * c) & (lane <= 40 * c + 32)
        total = jnp.where(inside, pltpu.roll(mine, 8 * c + 1, 1), total)
        total = jnp.where(lane == 40 * c, pltpu.roll(low, (8 * c - 31) % 256, 1), total)
    wide = jnp.where(
        lane < 7,
        pltpu.roll(low, 256 - 25, 1),
        jnp.where(lane < 39, pltpu.roll(mine, 7, 1), jnp.where(lane < 45, pltpu.roll(high, 39, 1), 0.0)),
    )
    smoothed = dot(wide[:, 0:128], v[...])
    out_plane[:, 0:128] = jnp.where(lanes((32, 128)) < 40, smoothed, total[:, 0:128])
    out_plane[:, 128:256] = total[:, 128:256]

    def store(upper, lower):
        for j in range(7):
            upper[j] = edges[9 + j]
        upper[7] = jnp.zeros((32, 256), F32)
        upper[7, 0:8, :] = out_face[24:32, :]
        for e in range(4):
            corner = face_ext[e, 31:32, :]
            upper[7, 8 + e : 9 + e, :] = jnp.where(where_ref[1] == 0, 0.0, corner)
        upper[7, 16:24, :] = out_plane[24:32, :]
        for j in range(6):
            lower[j] = edges[j]
        lower[6] = jnp.zeros((32, 256), F32)
        lower[7] = jnp.zeros((32, 256), F32)
        lower[7, 0:8, :] = out_face[0:8, :]
        lower[7, 16:24, :] = out_plane[0:8, :]

    by_parity(lax.rem(where_ref[0], 2) == 0, x_a, x_b, store)

    def keep(_, lower):
        got_ext[...] = lower[...]

    by_parity(lax.rem(where_ref[0], 2) == 0, ext_a, ext_b, keep)


def fill_side(at, side, face_ext):
    for e in range(4):
        side[e, 0:32, :] = face_ext[e]
        side[e, 32:40, :] = jnp.zeros((8, 256), F32)

    @pl.when(at[1] == 0)
    def _():
        side[...] = jnp.zeros_like(side)


def faces(extents, at, mx, face_all, plane_all, side, face_e, face_a, column, inv_x, inv_yz):
    nx, ny, nz = extents
    ix, iy, iz = at
    shape = (40, 256)
    row, lane = rows(shape), lanes(shape)
    invx = inverse_total(ix * 32 + jnp.where(row < 32, row, -1), nx)
    inv_x[...] = invx
    small = (32, 256)
    invz = inverse_total(iz * 256 + lanes(small), nz)
    inv_yz[...] = inverse_total(iy * 32 + rows(small), ny) * invz

    def previous(value):
        return jnp.where(row == 0, value[32:33, :], pltpu.roll(value, 1, 0))

    def joined(t0, t1, t2):
        a0 = previous(t0) - t0
        a1 = previous(t1) + t1
        a2 = previous(t2) + t2
        return a0 + a1, a0 - a1, a2

    at_y = inverse_total(jnp.full((1, 256), iy * 32 - 1, jnp.int32), ny)
    kap = jnp.maximum(side[3], dot(mx[...], face_all[...]) * (invx * (at_y * invz[0:1, :])))
    integ = integrity_of(kap)
    e, _, a2 = joined(integ * side[0], integ * side[1], integ * side[2])
    face_e[...] = e[0:32]
    face_a[...] = a2[0:32]

    avg = dot(mx[...], plane_all[...])
    own = jnp.where(row == 32, plane_all[7:8, :], plane_all[8:48, :])

    def value(c):
        return pltpu.roll(own, (256 - 40 * c) % 256, 1)

    at_z = inverse_total(jnp.full((1, 256), iz * 256 - 1, jnp.int32), nz)
    invy = inverse_total(iy * 32 - 1 + jnp.minimum(lane, 32), ny)
    kap = jnp.maximum(value(4), avg * (invx * (invy * at_z)))
    integ = integrity_of(kap)
    e, f, a2 = joined(integ * value(1), integ * value(2), integ * value(3))
    parts = e + a2 + pltpu.roll(f + a2, 255, 1)
    parts = jnp.where(lane < 32, parts, 0.0)
    eye = (rows((32, 128)) == lanes((32, 128))).astype(F32)
    pad = jnp.concatenate([parts[0:32, 0:128], jnp.zeros((96, 128), F32)], axis=0)
    column[...] = dot_lanes(eye, pad)


def layer_results(x, avg, kappa, free, strain, before, face_e, face_a, column, force_at, kappa_at):
    first_row = rows((32, 256)) == 0
    first_lane = lanes((32, 128)) == 0
    kap = jnp.maximum(kappa[x], avg)
    integ = integrity_of(kap)
    s0, s1, s2 = integ * free[x], integ * strain[1, x], integ * strain[2, x]
    if force_at is not None:
        kappa_at[...] = kap
        a0 = before[0] - s0
        a1 = before[1] + s1
        a2 = before[2] + s2
        e, f = a0 + a1, a0 - a1
        b = f + jnp.where(first_row, face_e[pl.ds(x, 1), :], pltpu.roll(e, 1, 0))
        c = a2 + jnp.where(first_row, face_a[pl.ds(x, 1), :], pltpu.roll(a2, 1, 0))
        p, q = b + c, b - c
        moved = pltpu.roll(p, 1, 1)
        edge = pltpu.roll(column[...], lax.rem(128 - x, 128), 1)
        force_at[:, 0:128] = 0.25 * (q[:, 0:128] + jnp.where(first_lane, edge, moved[:, 0:128]))
        force_at[:, 128:256] = 0.25 * (q[:, 128:256] + moved[:, 128:256])
    before[0] = s0
    before[1] = s1
    before[2] = s2


def middle_kernel(
    extents, where_ref, strain, free, kappa, own, edges, halo, face, plane, face_ext, my,
    force, kappa_new, part, face_out,
    ext, face_all, plane_all, side, before, face_e, face_a, column, inv_x, inv_yz,
    force_v, kappa_v, sems,
):
    at = (where_ref[0], where_ref[1], where_ref[2])
    for x in range(32):
        if x < 8:
            ext[x] = edges[x]
        elif x >= 24:
            ext[x] = edges[x - 16]
        else:
            both = dot(my[:, 32:48], halo[x])
            ext[x] = own[x] + both[0:32]
            face_out[x : x + 1, :] = face[x : x + 1, :] + both[32:33]
    face_out[0:8, :] = face[0:8, :]
    face_out[24:32, :] = face[24:32, :]
    for ref, value in ((face_all, face_out), (plane_all, plane)):
        ref[0:8, :] = jnp.zeros((8, 256), F32)
        ref[8:40, :] = value[...]
        ref[40:48, :] = jnp.zeros((8, 256), F32)
    fill_side(at, side, face_ext)
    faces(
        extents, at, my.at[:, 48:96], face_all, plane_all, side,
        face_e, face_a, column, inv_x, inv_yz,
    )

    def layer(x):
        total = gauss(0) * ext[x]
        for a in range(1, REACH + 1):
            total = total + gauss(a) * (ext[x - a] + ext[x + a])
        return total * (inv_x[pl.ds(x, 1), :] * inv_yz[...])

    layer_results(7, layer(7), kappa, free, strain, before, None, None, None, None, None)
    copies = []
    for c in (1, 2):

        @pl.loop(0, CHUNK)
        def _(i):
            x = c * CHUNK + i
            layer_results(
                x, layer(x), kappa, free, strain, before, face_e, face_a, column,
                force_v.at[x - CHUNK], kappa_v.at[x - CHUNK],
            )

        here = pl.ds((c - 1) * CHUNK, CHUNK)
        there = pl.ds(c * CHUNK, CHUNK)
        for k, (src, dst) in enumerate(((force_v, force), (kappa_v, kappa_new))):
            copy = pltpu.make_async_copy(src.at[here], dst.at[there], sems.at[c - 1, k])
            copy.start()
            copies.append(copy)
    for i in range(18):
        x = i - 1 if i < 9 else i + 14
        total = None
        for a in range(-REACH, REACH + 1):
            if 0 <= x + a < 32:
                term = gauss(a) * ext[x + a]
                total = term if total is None else total + term
        part[i] = total
    for copy in copies:
        copy.wait()


def outer_kernel(
    extents, where_ref, strain, free, kappa, part, face, plane, face_ext, got_a, got_b, got_ext, my,
    force_in, kappa_in,
    force, kappa_new,
    low, high, face_all, plane_all, side, before, face_e, face_a, column, inv_x, inv_yz,
    force_v, kappa_v, sems,
):
    at = (where_ref[0], where_ref[1], where_ref[2])

    def choose(upper, lower):
        for j in range(7):
            low[j] = lower[j]
        for j in range(6):
            high[j] = upper[j]
        face_all[0:8, :] = lower[7, 0:8, :]
        face_all[40:48, :] = upper[7, 0:8, :]
        plane_all[0:8, :] = lower[7, 16:24, :]
        plane_all[40:48, :] = upper[7, 16:24, :]
        for e in range(4):
            side[e, 32:33, :] = lower[7, 8 + e : 9 + e, :]

    fill_side(at, side, face_ext)
    by_parity(lax.rem(at[0], 2) == 0, got_a, got_b, choose)
    before[...] = got_ext[...]

    @pl.when(at[0] == 0)
    def _():
        low[...] = jnp.zeros_like(low)
        before[...] = jnp.zeros_like(before)
        face_all[0:8, :] = jnp.zeros((8, 256), F32)
        plane_all[0:8, :] = jnp.zeros((8, 256), F32)
        for e in range(4):
            side[e, 32:33, :] = jnp.zeros((1, 256), F32)

    @pl.when(at[0] == extents[0] // 32 - 1)
    def _():
        high[...] = jnp.zeros_like(high)
        face_all[40:48, :] = jnp.zeros((8, 256), F32)
        plane_all[40:48, :] = jnp.zeros((8, 256), F32)

    face_all[8:40, :] = face[...]
    plane_all[8:40, :] = plane[...]
    faces(
        extents, at, my.at[:, 48:96], face_all, plane_all, side,
        face_e, face_a, column, inv_x, inv_yz,
    )

    def layer(x):
        total = part[x + 1 if x < 8 else x - 14]
        for a in range(-REACH, REACH + 1):
            if x + a < 0:
                total = total + gauss(a) * low[x + a + 7]
            elif x + a >= 32:
                total = total + gauss(a) * high[x + a - 32]
        return total * (inv_x[x % 33 : x % 33 + 1, :] * inv_yz[...])

    kap = jnp.maximum(before[3], layer(-1))
    integ = integrity_of(kap)
    for e in range(3):
        before[e] = integ * before[e]
    copies = []
    for c in (0, 3):
        if c == 3:
            layer_results(23, layer(23), kappa, free, strain, before, None, None, None, None, None)
        for i in range(CHUNK):
            x = c * CHUNK + i
            slot = i if c == 0 else CHUNK + i
            layer_results(
                x, layer(x), kappa, free, strain, before, face_e, face_a, column,
                force_v.at[slot], kappa_v.at[slot],
            )
        here = pl.ds(0 if c == 0 else CHUNK, CHUNK)
        there = pl.ds(c * CHUNK, CHUNK)
        for k, (src, dst) in enumerate(((force_v, force), (kappa_v, kappa_new))):
            copy = pltpu.make_async_copy(src.at[here], dst.at[there], sems.at[c // 3, k])
            copy.start()
            copies.append(copy)
    for copy in copies:
        copy.wait()


AXES = ("gx", "gy", "gz")


def swap(first, second, axis):
    sizes = [lax.axis_size(a) for a in AXES]
    at = AXES.index(axis)
    other = 2 if at == 1 else 1

    def route(start):
        out = []
        for place in np.ndindex(*sizes):
            there = list(place)
            if place[at] >= start and place[at] - start < (sizes[at] - start) // 2 * 2:
                there[at] += 1 if (place[at] - start) % 2 == 0 else -1
            else:
                there[other] ^= 1
            out.append(tuple(int(np.ravel_multi_index(p, sizes)) for p in (place, tuple(there))))
        return out

    return lax.ppermute(first, AXES, route(0)), lax.ppermute(second, AXES, route(1))


def to_next(block, axis):
    count = lax.axis_size(axis)
    return lax.ppermute(block, axis, [(i, (i + 1) % count) for i in range(count)])


def shape_of(*dims):
    return jax.ShapeDtypeStruct(dims, F32)


VM = pl.BlockSpec(memory_space=pltpu.VMEM)
SM = pl.BlockSpec(memory_space=pltpu.SMEM)
HBM = pl.BlockSpec(memory_space=pltpu.HBM)
BLOCK = shape_of(32, 32, 256)
FACE = shape_of(32, 256)


def vmem(*dims):
    return pltpu.VMEM(dims, F32)


def call(kernel, name, in_specs, out_shape, out_specs=None, scratch=(), **kwargs):
    return pl.pallas_call(
        kernel,
        name=name,
        in_specs=in_specs,
        out_specs=out_specs or [VM] * len(out_shape),
        out_shape=out_shape,
        scratch_shapes=list(scratch),
        interpret=INTERPRET,
        compiler_params=pltpu.CompilerParams(vmem_limit_bytes=VMEM_LIMIT),
        **kwargs,
    )


def body(strain_in, plastic_in, alpha_in, kappa_in, flags):
    where = jnp.stack([lax.axis_index(a) for a in AXES]).astype(jnp.int32)
    flags = flags.reshape(32, 32)
    counts = tuple(lax.axis_size(a) for a in AXES)
    extents = (32 * counts[0], 32 * counts[1], 256 * counts[2])
    rows_all = rows_matrix()
    rows_own = np.ascontiguousarray(rows_all[:, 8:40])
    rows_halo = np.concatenate(
        [rows_all[:, 1:8], np.zeros((40, 1), np.float32), rows_all[:, 40:48]], axis=1
    )
    rows_three = np.zeros((40, 128), np.float32)
    rows_three[:, 32:48] = rows_halo
    rows_three[:, 48:96] = rows_all

    whole_in = [
        pltpu.with_memory_space_constraint(v, pltpu.HBM)
        for v in (strain_in, plastic_in, alpha_in, kappa_in, flags)
    ]
    ends, eight = shape_of(4, 32, 256), shape_of(8, 32, 256)
    square = shape_of(128, 128)
    strain, plastic, alpha, kappa, turned, z_a, z_b, yext, xext = call(
        pack_kernel,
        "pack",
        [SM] + [HBM] * 5,
        [
            shape_of(3, 32, 32, 256), BLOCK, BLOCK, BLOCK, shape_of(32, 32), square, square,
            ends, ends,
        ],
        scratch=[pltpu.VMEM((32, 32), jnp.int32)] + [vmem(128, 128)] * 6
        + [pltpu.SemaphoreType.DMA((CHUNKS + 1, 4))],
    )(where, *whole_in)
    got_a, got_b = swap(z_a, z_b, "gz")
    face_ext = to_next(yext, "gy")
    own, free = call(
        inner_kernel, "inner", [VM] * 5, [BLOCK, BLOCK], scratch=[vmem(32, 32, 256)]
    )(strain, plastic, alpha, turned, z_band(256))
    t_low, t_high = z_low_rows(), z_high_rows()
    plane, y_a, y_b, z_low, z_high, xext = call(
        functools.partial(z_kernel, counts),
        "along_z",
        [SM] + [VM] * 11,
        [FACE, eight, eight, square, square, ends],
        scratch=[vmem(128, 128)] + [vmem(32, 128)] * 2 + [vmem(512, 128)] * 2
        + [vmem(2, 32, 8, 256)],
    )(
        where, own, xext, z_a, z_b, got_a, got_b, face_ext,
        t_low, t_high, plane_from_low(), plane_from_own(),
    )
    got_a, got_b = swap(y_a, y_b, "gy")
    ext_a, ext_b = swap(xext, xext, "gx")
    own, own_face = call(
        own_rows_kernel,
        "own_rows",
        [VM] * 6,
        [BLOCK, FACE],
        scratch=[vmem(1024, 128), vmem(32, 32, 256)],
    )(own, z_low, z_high, t_low, t_high, rows_own)

    edges, face, plane, halo, x_a, x_b, got_ext = call(
        functools.partial(y_kernel, counts),
        "along_y",
        [SM] + [VM] * 10,
        [shape_of(16, 32, 256), FACE, FACE, shape_of(32, 16, 256), eight, eight, ends],
        scratch=[vmem(32, 256), vmem(32, 256)],
    )(where, own, own_face, plane, got_a, got_b, face_ext, ext_a, ext_b, rows_halo, plane_y_matrix())
    got_a, got_b = swap(x_a, x_b, "gx")

    shared = [
        vmem(48, 256), vmem(48, 256), vmem(4, 40, 256), vmem(4, 32, 256),
        vmem(32, 256), vmem(32, 256), vmem(32, 128), vmem(40, 256), vmem(32, 256),
        vmem(16, 32, 256), vmem(16, 32, 256), pltpu.SemaphoreType.DMA((2, 2)),
    ]
    force, kappa_new, part, face = call(
        functools.partial(middle_kernel, extents),
        "middle",
        [SM] + [VM] * 10,
        [BLOCK, BLOCK, shape_of(18, 32, 256), FACE],
        out_specs=[HBM, HBM, VM, VM],
        scratch=[vmem(32, 32, 256)] + shared,
    )(where, strain, free, kappa, own, edges, halo, face, plane, face_ext, rows_three)
    force, kappa_new = call(
        functools.partial(outer_kernel, extents),
        "outer",
        [SM] + [VM] * 11 + [HBM, HBM],
        [BLOCK, BLOCK],
        out_specs=[HBM, HBM],
        scratch=[vmem(7, 32, 256), vmem(6, 32, 256)] + shared,
        input_output_aliases={12: 0, 13: 1},
    )(
        where, strain, free, kappa, part, face, plane, face_ext, got_a, got_b, got_ext, rows_three,
        force, kappa_new,
    )
    return (force, kappa_new)


def solution(mesh):
    in_specs = (
        P(None, "gx", "gy", "gz"),
        P("gx", "gy", "gz"),
        P("gx", "gy", "gz"),
        P("gx", "gy", "gz"),
        P("gx", "gy", "gz"),
    )
    out_specs = (P("gx", "gy", "gz"), P("gx", "gy", "gz"))
    return jax.shard_map(body, mesh=mesh, in_specs=in_specs, out_specs=out_specs, check_vma=False)
```

```python
import functools
import math

import jax
import jax.numpy as jnp
import numpy as np
from jax import lax
from jax.experimental import pallas as pl
from jax.experimental.pallas import tpu as pltpu
from jax.sharding import PartitionSpec as P

REACH = 6
RM_ITERS = 2
LENGTH_SCALE = 3.0
HIGHEST = lax.Precision.HIGHEST
F32 = jnp.float32
VMEM_LIMIT = 40 * 1024 * 1024
INTERPRET = False


def gauss(offset):
    return math.exp(-offset * offset / (2.0 * LENGTH_SCALE * LENGTH_SCALE))


def band(offset):
    return gauss(offset) if abs(offset) <= REACH else 0.0


def z_band(width):
    return np.array([[band(i - k) for k in range(width)] for i in range(width)], np.float32)


def z_low_rows():
    out = np.zeros((128, 128), np.float32)
    for r in range(128):
        if r % 16 < 7:
            out[r] = [band(k - (r % 16 - 7)) for k in range(128)]
    return out


def z_high_rows():
    out = np.zeros((128, 128), np.float32)
    for r in range(128):
        if r % 16 < 6:
            out[r] = [band(128 + r % 16 - k) for k in range(128)]
    return out


def plane_from_low():
    out = np.zeros((40, 128), np.float32)
    for g in range(8):
        for c in range(7):
            out[g, 16 * g + c] = band(c - 6)
        for e in range(4):
            out[8 * (1 + e) + g, 16 * g + 7 + e] = 1.0
    return out


def plane_from_own():
    out = np.zeros((40, 128), np.float32)
    for g in range(8):
        for c in range(6):
            out[g, 16 * g + c] = band(c + 1)
    return out


def rows_matrix():
    out = np.zeros((40, 48), np.float32)
    for r in range(33):
        at = r if r < 32 else -1
        for k in range(1, 46):
            out[r, k] = band(k - 8 - at)
    return out


def plane_y_matrix():
    out = np.zeros((128, 128), np.float32)
    for y in range(-1, 32):
        for k in range(45):
            out[k, y + 1] = band(k - 7 - y)
    return out


def lanes(shape):
    return lax.broadcasted_iota(jnp.int32, shape, len(shape) - 1)


def rows(shape):
    return lax.broadcasted_iota(jnp.int32, shape, len(shape) - 2)


def inverse_total(position, extent):
    total = jnp.zeros(position.shape, F32)
    for offset in range(-REACH, REACH + 1):
        inside = (position + offset >= 0) & (position + offset < extent)
        total = total + jnp.where(inside, F32(gauss(offset)), F32(0.0))
    return 1.0 / total


def newton_plastic(trial, alpha_old):
    increment = jnp.zeros(trial.shape, F32)
    for _ in range(RM_ITERS):
        hardened = alpha_old + increment
        soft = 0.5 * jnp.exp(-5.0 * hardened)
        excess = trial - increment - (1.0 + 0.5 * hardened - soft)
        increment = jnp.maximum(increment + excess / (1.5 + 5.0 * soft), 0.0)
    return increment


def field_of(first, second, third):
    return first * first + second * second + third * third


def integrity_of(kappa):
    return jnp.exp(-jnp.maximum(kappa - 3.2, 0.0) / 3.0)


def by_parity(even, first, second, use):
    @pl.when(even)
    def _():
        use(first, second)

    @pl.when(jnp.logical_not(even))
    def _():
        use(second, first)


CONTRACT_LANES = (((1,), (1,)), ((), ()))
CHUNK = 8
CHUNKS = 4


def dot(left, right):
    return jnp.dot(left, right, precision=HIGHEST, preferred_element_type=F32)


def dot_lanes(left, right, precision=HIGHEST):
    return lax.dot_general(
        left, right, CONTRACT_LANES, precision=precision, preferred_element_type=F32
    )


def turned_flags(flags):
    eye = (rows((32, 32)) == lanes((32, 32))).astype(F32)
    return dot_lanes(eye, flags[...].astype(F32), None)


def pack_kernel(
    where_ref, strain_in, plastic_in, alpha_in, kappa_in, flags,
    strain, plastic, alpha, kappa, turned, z_a, z_b, yext, xext,
    flags_v, up_trial, up_alpha, up_drive, low_trial, low_alpha, low_drive, sems,
):
    flags_copy = pltpu.make_async_copy(flags, flags_v, sems.at[CHUNKS, 0])
    flags_copy.start()
    copies = []
    for c in range(CHUNKS):
        part = pl.ds(c * CHUNK, CHUNK)
        pairs = [(strain_in.at[:, part], strain.at[:, part])]
        pairs += [
            (src.at[part], dst.at[part])
            for src, dst in ((plastic_in, plastic), (alpha_in, alpha), (kappa_in, kappa))
        ]
        copies.append(
            [pltpu.make_async_copy(src, dst, sems.at[c, i]) for i, (src, dst) in enumerate(pairs)]
        )
    for group in copies:
        for copy in group:
            copy.start()
    flags_copy.wait()
    turned[...] = turned_flags(flags_v)
    flag = jnp.concatenate(
        [
            jnp.dot(
                turned[...],
                (rows((32, 128)) == 4 * (lanes((32, 128)) // 16) + b).astype(F32),
                preferred_element_type=F32,
            )
            for b in range(4)
        ],
        axis=0,
    )
    lane = lanes((128, 128))
    for c in range(CHUNKS):
        for copy in copies[c]:
            copy.wait()
        for g in (2 * c, 2 * c + 1):
            inside = lane // 16 == g

            def tile(ref, half):
                cells = ref[4 * g : 4 * g + 4, :, 128 * half : 128 * half + 128]
                return cells.reshape(128, 128)

            def place(ref, value, move):
                moved = pltpu.roll(value, (move + 16 * g) % 128, 1) if move + 16 * g else value
                ref[...] = jnp.where(inside, moved, ref[...])

            s0, s1, s2 = (tile(strain.at[i], 1) for i in range(3))
            place(up_trial, s0 - tile(plastic, 1), 7)
            place(up_alpha, tile(alpha, 1), 7)
            place(up_drive, field_of(s0, s1, s2), 7)
            mixed = up_drive[...]
            for e, value in enumerate((s1, s2, tile(kappa, 1))):
                moved = pltpu.roll(value, (9 + e + 16 * g) % 128, 1)
                mixed = jnp.where(lane == 16 * g + 8 + e, moved, mixed)
            up_drive[...] = mixed
            s0, s1, s2 = (tile(strain.at[i], 0) for i in range(3))
            place(low_trial, s0 - tile(plastic, 0), 0)
            place(low_alpha, tile(alpha, 0), 0)
            place(low_drive, field_of(s0, s1, s2), 0)

    trial = strain[0, 31] - plastic[31]
    here = (rows((32, 256)) == 31).astype(F32)
    flag_x = jnp.dot(turned[...], here, preferred_element_type=F32)
    xext[0] = trial - newton_plastic(trial, alpha[31]) * flag_x
    trial = strain[0, :, 31, :] - plastic[:, 31, :]
    flag_y = jnp.broadcast_to(flags_v[:, 31:32].astype(F32), (32, 256))
    yext[0] = trial - newton_plastic(trial, alpha[:, 31, :]) * flag_y
    for e, ref in enumerate((strain.at[1], strain.at[2], kappa)):
        xext[1 + e] = ref[31]
        yext[1 + e] = ref[:, 31, :]

    increment = newton_plastic(up_trial[...], up_alpha[...]) * flag
    free = pltpu.roll(up_trial[...] - increment, 1, 1)
    up_drive[...] = jnp.where(
        lane % 16 < 7,
        up_drive[...] + 4.0 * increment,
        jnp.where(lane % 16 == 7, free, up_drive[...]),
    )
    increment = newton_plastic(low_trial[...], low_alpha[...]) * flag
    low_drive[...] = low_drive[...] + 4.0 * increment

    def store(upper, lower):
        upper[...] = up_drive[...]
        lower[...] = low_drive[...]

    by_parity(lax.rem(where_ref[2], 2) == 0, z_a, z_b, store)


def inner_kernel(strain, plastic, alpha, turned, bz, smooth, free, field):
    @pl.loop(0, 8)
    def _(g):
        for i in range(4):
            x = 4 * g + i
            here = (rows((32, 256)) == x).astype(F32)
            flag = jnp.dot(turned[...], here, preferred_element_type=F32)
            s0 = strain[0, x]
            trial = s0 - plastic[x]
            increment = newton_plastic(trial, alpha[x]) * flag
            field[x] = field_of(s0, strain[1, x], strain[2, x]) + 4.0 * increment
            free[x] = trial - increment

    for g in range(4):
        part = field[8 * g : 8 * g + 8].reshape(256, 256)
        smooth[8 * g : 8 * g + 8] = dot(part, bz[...]).reshape(8, 32, 256)


def z_kernel(
    counts, where_ref, own, xext_in, sent_a, sent_b, got_b, got_a, _, t_low, t_high, w_low, w_own,
    plane, y_a, y_b, z_low, z_high, xext,
    own_low, head_rows, tail_rows, some_low, some_high, ends,
):
    xext[...] = xext_in[...]

    def choose(upper, lower):
        z_high[...] = upper[0][...]
        z_low[...] = lower[0][...]
        own_low[...] = lower[1][...]

    by_parity(lax.rem(where_ref[2], 2) == 0, (got_a, sent_a), (got_b, sent_b), choose)

    @pl.when(where_ref[2] == 0)
    def _():
        z_low[...] = jnp.zeros_like(z_low)

    @pl.when(where_ref[2] == counts[2] - 1)
    def _():
        z_high[...] = jnp.zeros_like(z_high)

    group = lanes((8, 128)) // 16
    for half in range(2):
        for x in range(32):
            start = 32 * (x % 4) + 24 * half
            at = 256 * half + 8 * x
            inside = group == x // 4
            for some, ref in ((some_low, z_low), (some_high, z_high)):
                some[at : at + 8, :] = jnp.where(inside, ref[start : start + 8, :], 0.0)
    first = dot(some_low[...], t_low[...])
    last = dot(some_high[...], t_high[...])
    for half in range(2):
        part = slice(256 * half, 256 * half + 256)
        here = slice(24 * half, 24 * half + 8)
        ends[half, :, :, 0:128] = own[:, here, 0:128] + first[part].reshape(32, 8, 128)
        ends[half, :, :, 128:256] = own[:, here, 128:256] + last[part].reshape(32, 8, 128)
    turned = dot_lanes(w_low[...], z_low[...]) + dot_lanes(w_own[...], own_low[...])
    lane = lanes((8, 128))
    for b in range(4):
        head = jnp.zeros((8, 128), F32)
        for c in range(4):
            moved = pltpu.roll(turned[8 * c : 8 * c + 8], (32 * (c - b)) % 128, 1)
            head = jnp.where(lane // 32 == c, moved, head)
        tail = jnp.where(lane < 32, pltpu.roll(turned[32:40], (-32 * b) % 128, 1), 0.0)
        head_rows[pl.ds(b, 8, stride=4), :] = head
        tail_rows[pl.ds(b, 8, stride=4), :] = tail
    plane[:, 0:128] = head_rows[...]
    plane[:, 128:256] = tail_rows[...]

    def store(upper, lower):
        for j in range(7):
            upper[j] = ends[1, :, 1 + j, :]
        upper[7] = plane[...]
        for j in range(6):
            lower[j] = ends[0, :, j, :]
        lower[6] = plane[...]
        lower[7] = plane[...]

    by_parity(lax.rem(where_ref[1], 2) == 0, y_a, y_b, store)


def own_rows_kernel(own, z_low, z_high, t_low, t_high, my, out, out_face, some, smooth):
    group = lanes((128, 128)) // 16
    for half, (ref, band_rows) in enumerate(((z_low, t_low), (z_high, t_high))):
        for g in range(8):
            some[128 * g : 128 * g + 128, :] = jnp.where(group == g, ref[...], 0.0)
        here = slice(128 * half, 128 * half + 128)
        for c in range(4):
            part = dot(some[256 * c : 256 * c + 256, :], band_rows[...])
            at = slice(8 * c, 8 * c + 8)
            smooth[at, :, here] = own[at, :, here] + part.reshape(8, 32, 128)
    for x in range(32):
        both = dot(my[...], smooth[x])
        out[x] = both[0:32]
        out_face[x : x + 1, :] = both[32:33]


def y_kernel(
    counts, where_ref, own, own_face, plane, got_b, got_a, face_ext, ext_b, ext_a, my, v,
    edges, out_face, out_plane, halo, x_a, x_b, got_ext, plane_low, plane_high,
):
    def choose(upper, lower):
        for j in range(7):
            halo[:, j, :] = lower[j]
        for j in range(6):
            halo[:, 8 + j, :] = upper[j]
        plane_low[...] = lower[7]
        plane_high[...] = upper[7]

    halo[:, 7, :] = jnp.zeros((32, 256), F32)
    halo[:, 14, :] = jnp.zeros((32, 256), F32)
    halo[:, 15, :] = jnp.zeros((32, 256), F32)
    by_parity(lax.rem(where_ref[1], 2) == 0, got_a, got_b, choose)

    @pl.when(where_ref[1] == 0)
    def _():
        halo[:, 0:8, :] = jnp.zeros((32, 8, 256), F32)
        plane_low[...] = jnp.zeros_like(plane_low)

    @pl.when(where_ref[1] == counts[1] - 1)
    def _():
        halo[:, 8:16, :] = jnp.zeros((32, 8, 256), F32)
        plane_high[...] = jnp.zeros_like(plane_high)

    out_face[8:24, :] = own_face[8:24, :]
    for i in range(16):
        x = i if i < 8 else i + 16
        both = dot(my[...], halo[x])
        edges[i] = own[x] + both[0:32]
        out_face[x : x + 1, :] = own_face[x : x + 1, :] + both[32:33]
    mine, low, high = plane[...], plane_low[...], plane_high[...]
    lane = lanes((32, 256))
    total = jnp.zeros((32, 256), F32)
    for c in range(1, 5):
        inside = (lane > 40 * c) & (lane <= 40 * c + 32)
        total = jnp.where(inside, pltpu.roll(mine, 8 * c + 1, 1), total)
        total = jnp.where(lane == 40 * c, pltpu.roll(low, (8 * c - 31) % 256, 1), total)
    wide = jnp.where(
        lane < 7,
        pltpu.roll(low, 256 - 25, 1),
        jnp.where(lane < 39, pltpu.roll(mine, 7, 1), jnp.where(lane < 45, pltpu.roll(high, 39, 1), 0.0)),
    )
    smoothed = dot(wide[:, 0:128], v[...])
    out_plane[:, 0:128] = jnp.where(lanes((32, 128)) < 40, smoothed, total[:, 0:128])
    out_plane[:, 128:256] = total[:, 128:256]

    def store(upper, lower):
        for j in range(7):
            upper[j] = edges[9 + j]
        upper[7] = jnp.zeros((32, 256), F32)
        upper[7, 0:8, :] = out_face[24:32, :]
        for e in range(4):
            corner = face_ext[e, 31:32, :]
            upper[7, 8 + e : 9 + e, :] = jnp.where(where_ref[1] == 0, 0.0, corner)
        upper[7, 16:24, :] = out_plane[24:32, :]
        for j in range(6):
            lower[j] = edges[j]
        lower[6] = jnp.zeros((32, 256), F32)
        lower[7] = jnp.zeros((32, 256), F32)
        lower[7, 0:8, :] = out_face[0:8, :]
        lower[7, 16:24, :] = out_plane[0:8, :]

    by_parity(lax.rem(where_ref[0], 2) == 0, x_a, x_b, store)

    def keep(_, lower):
        got_ext[...] = lower[...]

    by_parity(lax.rem(where_ref[0], 2) == 0, ext_a, ext_b, keep)


def fill_side(at, side, face_ext):
    for e in range(4):
        side[e, 0:32, :] = face_ext[e]
        side[e, 32:40, :] = jnp.zeros((8, 256), F32)

    @pl.when(at[1] == 0)
    def _():
        side[...] = jnp.zeros_like(side)


def faces(extents, at, mx, face_all, plane_all, side, face_e, face_a, column, inv_x, inv_yz):
    nx, ny, nz = extents
    ix, iy, iz = at
    shape = (40, 256)
    row, lane = rows(shape), lanes(shape)
    invx = inverse_total(ix * 32 + jnp.where(row < 32, row, -1), nx)
    inv_x[...] = invx
    small = (32, 256)
    invz = inverse_total(iz * 256 + lanes(small), nz)
    inv_yz[...] = inverse_total(iy * 32 + rows(small), ny) * invz

    def previous(value):
        return jnp.where(row == 0, value[32:33, :], pltpu.roll(value, 1, 0))

    def joined(t0, t1, t2):
        a0 = previous(t0) - t0
        a1 = previous(t1) + t1
        a2 = previous(t2) + t2
        return a0 + a1, a0 - a1, a2

    at_y = inverse_total(jnp.full((1, 256), iy * 32 - 1, jnp.int32), ny)
    kap = jnp.maximum(side[3], dot(mx[...], face_all[...]) * (invx * (at_y * invz[0:1, :])))
    integ = integrity_of(kap)
    e, _, a2 = joined(integ * side[0], integ * side[1], integ * side[2])
    face_e[...] = e[0:32]
    face_a[...] = a2[0:32]

    avg = dot(mx[...], plane_all[...])
    own = jnp.where(row == 32, plane_all[7:8, :], plane_all[8:48, :])

    def value(c):
        return pltpu.roll(own, (256 - 40 * c) % 256, 1)

    at_z = inverse_total(jnp.full((1, 256), iz * 256 - 1, jnp.int32), nz)
    invy = inverse_total(iy * 32 - 1 + jnp.minimum(lane, 32), ny)
    kap = jnp.maximum(value(4), avg * (invx * (invy * at_z)))
    integ = integrity_of(kap)
    e, f, a2 = joined(integ * value(1), integ * value(2), integ * value(3))
    parts = e + a2 + pltpu.roll(f + a2, 255, 1)
    parts = jnp.where(lane < 32, parts, 0.0)
    eye = (rows((32, 128)) == lanes((32, 128))).astype(F32)
    pad = jnp.concatenate([parts[0:32, 0:128], jnp.zeros((96, 128), F32)], axis=0)
    column[...] = dot_lanes(eye, pad)


def layer_results(x, avg, kappa, free, strain, before, face_e, face_a, column, force_at, kappa_at):
    first_row = rows((32, 256)) == 0
    first_lane = lanes((32, 128)) == 0
    kap = jnp.maximum(kappa[x], avg)
    integ = integrity_of(kap)
    s0, s1, s2 = integ * free[x], integ * strain[1, x], integ * strain[2, x]
    if force_at is not None:
        kappa_at[...] = kap
        a0 = before[0] - s0
        a1 = before[1] + s1
        a2 = before[2] + s2
        e, f = a0 + a1, a0 - a1
        b = f + jnp.where(first_row, face_e[pl.ds(x, 1), :], pltpu.roll(e, 1, 0))
        c = a2 + jnp.where(first_row, face_a[pl.ds(x, 1), :], pltpu.roll(a2, 1, 0))
        p, q = b + c, b - c
        moved = pltpu.roll(p, 1, 1)
        edge = pltpu.roll(column[...], lax.rem(128 - x, 128), 1)
        force_at[:, 0:128] = 0.25 * (q[:, 0:128] + jnp.where(first_lane, edge, moved[:, 0:128]))
        force_at[:, 128:256] = 0.25 * (q[:, 128:256] + moved[:, 128:256])
    before[0] = s0
    before[1] = s1
    before[2] = s2


def middle_kernel(
    extents, where_ref, strain, free, kappa, own, edges, halo, face, plane, face_ext, my,
    force, kappa_new, part, face_out,
    ext, face_all, plane_all, side, before, face_e, face_a, column, inv_x, inv_yz,
    force_v, kappa_v, sems,
):
    at = (where_ref[0], where_ref[1], where_ref[2])
    for x in range(32):
        if x < 8:
            ext[x] = edges[x]
        elif x >= 24:
            ext[x] = edges[x - 16]
        else:
            both = dot(my[:, 32:48], halo[x])
            ext[x] = own[x] + both[0:32]
            face_out[x : x + 1, :] = face[x : x + 1, :] + both[32:33]
    face_out[0:8, :] = face[0:8, :]
    face_out[24:32, :] = face[24:32, :]
    for ref, value in ((face_all, face_out), (plane_all, plane)):
        ref[0:8, :] = jnp.zeros((8, 256), F32)
        ref[8:40, :] = value[...]
        ref[40:48, :] = jnp.zeros((8, 256), F32)
    fill_side(at, side, face_ext)
    faces(
        extents, at, my.at[:, 48:96], face_all, plane_all, side,
        face_e, face_a, column, inv_x, inv_yz,
    )

    def layer(x):
        total = gauss(0) * ext[x]
        for a in range(1, REACH + 1):
            total = total + gauss(a) * (ext[x - a] + ext[x + a])
        return total * (inv_x[pl.ds(x, 1), :] * inv_yz[...])

    layer_results(7, layer(7), kappa, free, strain, before, None, None, None, None, None)
    copies = []
    for c in (1, 2):

        @pl.loop(0, CHUNK)
        def _(i):
            x = c * CHUNK + i
            layer_results(
                x, layer(x), kappa, free, strain, before, face_e, face_a, column,
                force_v.at[x - CHUNK], kappa_v.at[x - CHUNK],
            )

        here = pl.ds((c - 1) * CHUNK, CHUNK)
        there = pl.ds(c * CHUNK, CHUNK)
        for k, (src, dst) in enumerate(((force_v, force), (kappa_v, kappa_new))):
            copy = pltpu.make_async_copy(src.at[here], dst.at[there], sems.at[c - 1, k])
            copy.start()
            copies.append(copy)
    for i in range(18):
        x = i - 1 if i < 9 else i + 14
        total = None
        for a in range(-REACH, REACH + 1):
            if 0 <= x + a < 32:
                term = gauss(a) * ext[x + a]
                total = term if total is None else total + term
        part[i] = total
    for copy in copies:
        copy.wait()


def outer_kernel(
    extents, where_ref, strain, free, kappa, part, face, plane, face_ext, got_a, got_b, got_ext, my,
    force_in, kappa_in,
    force, kappa_new,
    low, high, face_all, plane_all, side, before, face_e, face_a, column, inv_x, inv_yz,
    force_v, kappa_v, sems,
):
    at = (where_ref[0], where_ref[1], where_ref[2])

    def choose(upper, lower):
        for j in range(7):
            low[j] = lower[j]
        for j in range(6):
            high[j] = upper[j]
        face_all[0:8, :] = lower[7, 0:8, :]
        face_all[40:48, :] = upper[7, 0:8, :]
        plane_all[0:8, :] = lower[7, 16:24, :]
        plane_all[40:48, :] = upper[7, 16:24, :]
        for e in range(4):
            side[e, 32:33, :] = lower[7, 8 + e : 9 + e, :]

    fill_side(at, side, face_ext)
    by_parity(lax.rem(at[0], 2) == 0, got_a, got_b, choose)
    before[...] = got_ext[...]

    @pl.when(at[0] == 0)
    def _():
        low[...] = jnp.zeros_like(low)
        before[...] = jnp.zeros_like(before)
        face_all[0:8, :] = jnp.zeros((8, 256), F32)
        plane_all[0:8, :] = jnp.zeros((8, 256), F32)
        for e in range(4):
            side[e, 32:33, :] = jnp.zeros((1, 256), F32)

    @pl.when(at[0] == extents[0] // 32 - 1)
    def _():
        high[...] = jnp.zeros_like(high)
        face_all[40:48, :] = jnp.zeros((8, 256), F32)
        plane_all[40:48, :] = jnp.zeros((8, 256), F32)

    face_all[8:40, :] = face[...]
    plane_all[8:40, :] = plane[...]
    faces(
        extents, at, my.at[:, 48:96], face_all, plane_all, side,
        face_e, face_a, column, inv_x, inv_yz,
    )

    def layer(x):
        total = part[x + 1 if x < 8 else x - 14]
        for a in range(-REACH, REACH + 1):
            if x + a < 0:
                total = total + gauss(a) * low[x + a + 7]
            elif x + a >= 32:
                total = total + gauss(a) * high[x + a - 32]
        return total * (inv_x[x % 33 : x % 33 + 1, :] * inv_yz[...])

    kap = jnp.maximum(before[3], layer(-1))
    integ = integrity_of(kap)
    for e in range(3):
        before[e] = integ * before[e]
    copies = []
    for c in (0, 3):
        if c == 3:
            layer_results(23, layer(23), kappa, free, strain, before, None, None, None, None, None)
        for i in range(CHUNK):
            x = c * CHUNK + i
            slot = i if c == 0 else CHUNK + i
            layer_results(
                x, layer(x), kappa, free, strain, before, face_e, face_a, column,
                force_v.at[slot], kappa_v.at[slot],
            )
        here = pl.ds(0 if c == 0 else CHUNK, CHUNK)
        there = pl.ds(c * CHUNK, CHUNK)
        for k, (src, dst) in enumerate(((force_v, force), (kappa_v, kappa_new))):
            copy = pltpu.make_async_copy(src.at[here], dst.at[there], sems.at[c // 3, k])
            copy.start()
            copies.append(copy)
    for copy in copies:
        copy.wait()


AXES = ("gx", "gy", "gz")


def swap(first, second, axis):
    sizes = [lax.axis_size(a) for a in AXES]
    at = AXES.index(axis)
    other = 2 if at == 1 else 1

    def route(start):
        out = []
        for place in np.ndindex(*sizes):
            there = list(place)
            if place[at] >= start and place[at] - start < (sizes[at] - start) // 2 * 2:
                there[at] += 1 if (place[at] - start) % 2 == 0 else -1
            else:
                there[other] ^= 1
            out.append(tuple(int(np.ravel_multi_index(p, sizes)) for p in (place, tuple(there))))
        return out

    return lax.ppermute(first, AXES, route(0)), lax.ppermute(second, AXES, route(1))


def to_next(block, axis):
    count = lax.axis_size(axis)
    return lax.ppermute(block, axis, [(i, (i + 1) % count) for i in range(count)])


def shape_of(*dims):
    return jax.ShapeDtypeStruct(dims, F32)


VM = pl.BlockSpec(memory_space=pltpu.VMEM)
SM = pl.BlockSpec(memory_space=pltpu.SMEM)
HBM = pl.BlockSpec(memory_space=pltpu.HBM)
BLOCK = shape_of(32, 32, 256)
FACE = shape_of(32, 256)


def vmem(*dims):
    return pltpu.VMEM(dims, F32)


def call(kernel, name, in_specs, out_shape, out_specs=None, scratch=(), **kwargs):
    return pl.pallas_call(
        kernel,
        name=name,
        in_specs=in_specs,
        out_specs=out_specs or [VM] * len(out_shape),
        out_shape=out_shape,
        scratch_shapes=list(scratch),
        interpret=INTERPRET,
        compiler_params=pltpu.CompilerParams(vmem_limit_bytes=VMEM_LIMIT),
        **kwargs,
    )


def body(strain_in, plastic_in, alpha_in, kappa_in, flags):
    where = jnp.stack([lax.axis_index(a) for a in AXES]).astype(jnp.int32)
    flags = flags.reshape(32, 32)
    counts = tuple(lax.axis_size(a) for a in AXES)
    extents = (32 * counts[0], 32 * counts[1], 256 * counts[2])
    rows_all = rows_matrix()
    rows_own = np.ascontiguousarray(rows_all[:, 8:40])
    rows_halo = np.concatenate(
        [rows_all[:, 1:8], np.zeros((40, 1), np.float32), rows_all[:, 40:48]], axis=1
    )
    rows_three = np.zeros((40, 128), np.float32)
    rows_three[:, 32:48] = rows_halo
    rows_three[:, 48:96] = rows_all

    whole_in = [
        pltpu.with_memory_space_constraint(v, pltpu.HBM)
        for v in (strain_in, plastic_in, alpha_in, kappa_in, flags)
    ]
    ends, eight = shape_of(4, 32, 256), shape_of(8, 32, 256)
    square = shape_of(128, 128)
    strain, plastic, alpha, kappa, turned, z_a, z_b, yext, xext = call(
        pack_kernel,
        "pack",
        [SM] + [HBM] * 5,
        [
            shape_of(3, 32, 32, 256), BLOCK, BLOCK, BLOCK, shape_of(32, 32), square, square,
            ends, ends,
        ],
        scratch=[pltpu.VMEM((32, 32), jnp.int32)] + [vmem(128, 128)] * 6
        + [pltpu.SemaphoreType.DMA((CHUNKS + 1, 4))],
    )(where, *whole_in)
    got_a, got_b = swap(z_a, z_b, "gz")
    face_ext = to_next(yext, "gy")
    own, free = call(
        inner_kernel, "inner", [VM] * 5, [BLOCK, BLOCK], scratch=[vmem(32, 32, 256)]
    )(strain, plastic, alpha, turned, z_band(256))
    t_low, t_high = z_low_rows(), z_high_rows()
    plane, y_a, y_b, z_low, z_high, xext = call(
        functools.partial(z_kernel, counts),
        "along_z",
        [SM] + [VM] * 11,
        [FACE, eight, eight, square, square, ends],
        scratch=[vmem(128, 128)] + [vmem(32, 128)] * 2 + [vmem(512, 128)] * 2
        + [vmem(2, 32, 8, 256)],
    )(
        where, own, xext, z_a, z_b, got_b, got_a, face_ext,
        t_low, t_high, plane_from_low(), plane_from_own(),
    )
    got_a, got_b = swap(y_a, y_b, "gy")
    ext_a, ext_b = swap(xext, xext, "gx")
    own, own_face = call(
        own_rows_kernel,
        "own_rows",
        [VM] * 6,
        [BLOCK, FACE],
        scratch=[vmem(1024, 128), vmem(32, 32, 256)],
    )(own, z_low, z_high, t_low, t_high, rows_own)

    edges, face, plane, halo, x_a, x_b, got_ext = call(
        functools.partial(y_kernel, counts),
        "along_y",
        [SM] + [VM] * 10,
        [shape_of(16, 32, 256), FACE, FACE, shape_of(32, 16, 256), eight, eight, ends],
        scratch=[vmem(32, 256), vmem(32, 256)],
    )(where, own, own_face, plane, got_b, got_a, face_ext, ext_b, ext_a, rows_halo, plane_y_matrix())
    got_a, got_b = swap(x_a, x_b, "gx")

    shared = [
        vmem(48, 256), vmem(48, 256), vmem(4, 40, 256), vmem(4, 32, 256),
        vmem(32, 256), vmem(32, 256), vmem(32, 128), vmem(40, 256), vmem(32, 256),
        vmem(16, 32, 256), vmem(16, 32, 256), pltpu.SemaphoreType.DMA((2, 2)),
    ]
    force, kappa_new, part, face = call(
        functools.partial(middle_kernel, extents),
        "middle",
        [SM] + [VM] * 10,
        [BLOCK, BLOCK, shape_of(18, 32, 256), FACE],
        out_specs=[HBM, HBM, VM, VM],
        scratch=[vmem(32, 32, 256)] + shared,
    )(where, strain, free, kappa, own, edges, halo, face, plane, face_ext, rows_three)
    force, kappa_new = call(
        functools.partial(outer_kernel, extents),
        "outer",
        [SM] + [VM] * 11 + [HBM, HBM],
        [BLOCK, BLOCK],
        out_specs=[HBM, HBM],
        scratch=[vmem(7, 32, 256), vmem(6, 32, 256)] + shared,
        input_output_aliases={12: 0, 13: 1},
    )(
        where, strain, free, kappa, part, face, plane, face_ext, got_a, got_b, got_ext, rows_three,
        force, kappa_new,
    )
    return (force, kappa_new)


def solution(mesh):
    in_specs = (
        P(None, "gx", "gy", "gz"),
        P("gx", "gy", "gz"),
        P("gx", "gy", "gz"),
        P("gx", "gy", "gz"),
        P("gx", "gy", "gz"),
    )
    out_specs = (P("gx", "gy", "gz"), P("gx", "gy", "gz"))
    return jax.shard_map(body, mesh=mesh, in_specs=in_specs, out_specs=out_specs, check_vma=False)
```

```python
import functools
import math

import jax
import jax.numpy as jnp
import numpy as np
from jax import lax
from jax.experimental import pallas as pl
from jax.experimental.pallas import tpu as pltpu
from jax.sharding import PartitionSpec as P

REACH = 6
RM_ITERS = 2
LENGTH_SCALE = 3.0
HIGHEST = lax.Precision.HIGHEST
F32 = jnp.float32
VMEM_LIMIT = 40 * 1024 * 1024
INTERPRET = False


def gauss(offset):
    return math.exp(-offset * offset / (2.0 * LENGTH_SCALE * LENGTH_SCALE))


def band(offset):
    return gauss(offset) if abs(offset) <= REACH else 0.0


def z_band(width):
    return np.array([[band(i - k) for k in range(width)] for i in range(width)], np.float32)


def z_low_rows():
    out = np.zeros((128, 128), np.float32)
    for r in range(128):
        if r % 16 < 7:
            out[r] = [band(k - (r % 16 - 7)) for k in range(128)]
    return out


def z_high_rows():
    out = np.zeros((128, 128), np.float32)
    for r in range(128):
        if r % 16 < 6:
            out[r] = [band(128 + r % 16 - k) for k in range(128)]
    return out


def plane_from_low():
    out = np.zeros((40, 128), np.float32)
    for g in range(8):
        for c in range(7):
            out[g, 16 * g + c] = band(c - 6)
        for e in range(4):
            out[8 * (1 + e) + g, 16 * g + 7 + e] = 1.0
    return out


def plane_from_own():
    out = np.zeros((40, 128), np.float32)
    for g in range(8):
        for c in range(6):
            out[g, 16 * g + c] = band(c + 1)
    return out


def rows_matrix():
    out = np.zeros((40, 48), np.float32)
    for r in range(33):
        at = r if r < 32 else -1
        for k in range(1, 46):
            out[r, k] = band(k - 8 - at)
    return out


def plane_y_matrix():
    out = np.zeros((128, 128), np.float32)
    for y in range(-1, 32):
        for k in range(45):
            out[k, y + 1] = band(k - 7 - y)
    return out


def lanes(shape):
    return lax.broadcasted_iota(jnp.int32, shape, len(shape) - 1)


def rows(shape):
    return lax.broadcasted_iota(jnp.int32, shape, len(shape) - 2)


def inverse_total(position, extent):
    total = jnp.zeros(position.shape, F32)
    for offset in range(-REACH, REACH + 1):
        inside = (position + offset >= 0) & (position + offset < extent)
        total = total + jnp.where(inside, F32(gauss(offset)), F32(0.0))
    return 1.0 / total


def newton_plastic(trial, alpha_old):
    increment = jnp.zeros(trial.shape, F32)
    for _ in range(RM_ITERS):
        hardened = alpha_old + increment
        soft = 0.5 * jnp.exp(-5.0 * hardened)
        excess = trial - increment - (1.0 + 0.5 * hardened - soft)
        increment = jnp.maximum(increment + excess / (1.5 + 5.0 * soft), 0.0)
    return increment


def field_of(first, second, third):
    return first * first + second * second + third * third


def integrity_of(kappa):
    return jnp.exp(-jnp.maximum(kappa - 3.2, 0.0) / 3.0)


def by_parity(even, first, second, use):
    @pl.when(even)
    def _():
        use(first, second)

    @pl.when(jnp.logical_not(even))
    def _():
        use(second, first)


CONTRACT_LANES = (((1,), (1,)), ((), ()))
CHUNK = 8
CHUNKS = 4


def dot(left, right):
    return jnp.dot(left, right, precision=HIGHEST, preferred_element_type=F32)


def dot_lanes(left, right, precision=HIGHEST):
    return lax.dot_general(
        left, right, CONTRACT_LANES, precision=precision, preferred_element_type=F32
    )


def turned_flags(flags):
    eye = (rows((32, 32)) == lanes((32, 32))).astype(F32)
    return dot_lanes(eye, flags[...].astype(F32), None)


def pack_kernel(
    where_ref, strain_in, plastic_in, alpha_in, kappa_in, flags,
    strain, plastic, alpha, turned, z_b, z_a, yext,
    kappa_high, kappa_low, flags_v, up_trial, up_alpha, up_drive, low_trial, low_alpha, low_drive, sems,
):
    flags_copy = pltpu.make_async_copy(flags, flags_v, sems.at[CHUNKS, 0])
    flags_copy.start()
    copies = []
    for c in range(CHUNKS):
        part = pl.ds(c * CHUNK, CHUNK)
        pairs = [(strain_in.at[:, part], strain.at[:, part])]
        pairs += [
            (src.at[part], dst.at[part])
            for src, dst in ((plastic_in, plastic), (alpha_in, alpha))
        ]
        pairs.append((kappa_in.at[part, :, 128:256], kappa_high.at[part]))
        copies.append(
            [pltpu.make_async_copy(src, dst, sems.at[c, i]) for i, (src, dst) in enumerate(pairs)]
        )
    for group in copies:
        for copy in group:
            copy.start()
    row_copy = pltpu.make_async_copy(
        kappa_in.at[:, 24:32, 0:128], kappa_low, sems.at[CHUNKS, 1]
    )
    row_copy.start()
    flags_copy.wait()
    turned[...] = turned_flags(flags_v)
    flag = jnp.concatenate(
        [
            jnp.dot(
                turned[...],
                (rows((32, 128)) == 4 * (lanes((32, 128)) // 16) + b).astype(F32),
                preferred_element_type=F32,
            )
            for b in range(4)
        ],
        axis=0,
    )
    lane = lanes((128, 128))
    for c in range(CHUNKS):
        for copy in copies[c]:
            copy.wait()
        for g in (2 * c, 2 * c + 1):
            inside = lane // 16 == g

            def tile(ref, half):
                cells = ref[4 * g : 4 * g + 4, :, 128 * half : 128 * half + 128]
                return cells.reshape(128, 128)

            def place(ref, value, move):
                moved = pltpu.roll(value, (move + 16 * g) % 128, 1) if move + 16 * g else value
                ref[...] = jnp.where(inside, moved, ref[...])

            s0, s1, s2 = (tile(strain.at[i], 1) for i in range(3))
            place(up_trial, s0 - tile(plastic, 1), 7)
            place(up_alpha, tile(alpha, 1), 7)
            place(up_drive, field_of(s0, s1, s2), 7)
            mixed = up_drive[...]
            edge = kappa_high[4 * g : 4 * g + 4].reshape(128, 128)
            for e, value in enumerate((s1, s2, edge)):
                moved = pltpu.roll(value, (9 + e + 16 * g) % 128, 1)
                mixed = jnp.where(lane == 16 * g + 8 + e, moved, mixed)
            up_drive[...] = mixed
            s0, s1, s2 = (tile(strain.at[i], 0) for i in range(3))
            place(low_trial, s0 - tile(plastic, 0), 0)
            place(low_alpha, tile(alpha, 0), 0)
            place(low_drive, field_of(s0, s1, s2), 0)

    trial = strain[0, :, 31, :] - plastic[:, 31, :]
    flag_y = jnp.broadcast_to(flags_v[:, 31:32].astype(F32), (32, 256))
    yext[0] = trial - newton_plastic(trial, alpha[:, 31, :]) * flag_y
    yext[1] = strain[1, :, 31, :]
    yext[2] = strain[2, :, 31, :]
    row_copy.wait()
    yext[3, :, 0:128] = kappa_low[:, 7, :]
    yext[3, :, 128:256] = kappa_high[:, 31, :]

    increment = newton_plastic(up_trial[...], up_alpha[...]) * flag
    free = pltpu.roll(up_trial[...] - increment, 1, 1)
    up_drive[...] = jnp.where(
        lane % 16 < 7,
        up_drive[...] + 4.0 * increment,
        jnp.where(lane % 16 == 7, free, up_drive[...]),
    )
    increment = newton_plastic(low_trial[...], low_alpha[...]) * flag
    low_drive[...] = low_drive[...] + 4.0 * increment

    def store(upper, lower):
        upper[...] = up_drive[...]
        lower[...] = low_drive[...]

    by_parity(lax.rem(where_ref[2], 2) == 0, z_a, z_b, store)


def inner_kernel(strain, plastic, alpha, kappa, turned, bz, smooth, free, xext, field):
    @pl.loop(0, 8)
    def _(g):
        for i in range(4):
            x = 4 * g + i
            here = (rows((32, 256)) == x).astype(F32)
            flag = jnp.dot(turned[...], here, preferred_element_type=F32)
            s0 = strain[0, x]
            trial = s0 - plastic[x]
            increment = newton_plastic(trial, alpha[x]) * flag
            field[x] = field_of(s0, strain[1, x], strain[2, x]) + 4.0 * increment
            free[x] = trial - increment

    for g in range(4):
        part = field[8 * g : 8 * g + 8].reshape(256, 256)
        smooth[8 * g : 8 * g + 8] = dot(part, bz[...]).reshape(8, 32, 256)
    for e, ref in enumerate((free, strain.at[1], strain.at[2], kappa)):
        xext[e] = ref[31]


def z_kernel(
    counts, where_ref, own, xext_in, sent_b, sent_a, got_b, got_a, _, t_low, t_high, w_low, w_own,
    plane, y_a, y_b, z_low, z_high, xext,
    own_low, head_rows, tail_rows, some_low, some_high, ends,
):
    xext[...] = xext_in[...]

    def choose(upper, lower):
        z_high[...] = upper[0][...]
        z_low[...] = lower[0][...]
        own_low[...] = lower[1][...]

    by_parity(lax.rem(where_ref[2], 2) == 0, (got_a, sent_a), (got_b, sent_b), choose)

    @pl.when(where_ref[2] == 0)
    def _():
        z_low[...] = jnp.zeros_like(z_low)

    @pl.when(where_ref[2] == counts[2] - 1)
    def _():
        z_high[...] = jnp.zeros_like(z_high)

    group = lanes((8, 128)) // 16
    for half in range(2):
        for x in range(32):
            start = 32 * (x % 4) + 24 * half
            at = 256 * half + 8 * x
            inside = group == x // 4
            for some, ref in ((some_low, z_low), (some_high, z_high)):
                some[at : at + 8, :] = jnp.where(inside, ref[start : start + 8, :], 0.0)
    first = dot(some_low[...], t_low[...])
    last = dot(some_high[...], t_high[...])
    for half in range(2):
        part = slice(256 * half, 256 * half + 256)
        here = slice(24 * half, 24 * half + 8)
        ends[half, :, :, 0:128] = own[:, here, 0:128] + first[part].reshape(32, 8, 128)
        ends[half, :, :, 128:256] = own[:, here, 128:256] + last[part].reshape(32, 8, 128)
    turned = dot_lanes(w_low[...], z_low[...]) + dot_lanes(w_own[...], own_low[...])
    lane = lanes((8, 128))
    for b in range(4):
        head = jnp.zeros((8, 128), F32)
        for c in range(4):
            moved = pltpu.roll(turned[8 * c : 8 * c + 8], (32 * (c - b)) % 128, 1)
            head = jnp.where(lane // 32 == c, moved, head)
        tail = jnp.where(lane < 32, pltpu.roll(turned[32:40], (-32 * b) % 128, 1), 0.0)
        head_rows[pl.ds(b, 8, stride=4), :] = head
        tail_rows[pl.ds(b, 8, stride=4), :] = tail
    plane[:, 0:128] = head_rows[...]
    plane[:, 128:256] = tail_rows[...]

    def store(upper, lower):
        for j in range(7):
            upper[j] = ends[1, :, 1 + j, :]
        upper[7] = plane[...]
        for j in range(6):
            lower[j] = ends[0, :, j, :]
        lower[6] = plane[...]
        lower[7] = plane[...]

    by_parity(lax.rem(where_ref[1], 2) == 0, y_a, y_b, store)


def own_rows_kernel(own, z_low, z_high, t_low, t_high, my, out, out_face, some, smooth):
    group = lanes((128, 128)) // 16
    for half, (ref, band_rows) in enumerate(((z_low, t_low), (z_high, t_high))):
        for g in range(8):
            some[128 * g : 128 * g + 128, :] = jnp.where(group == g, ref[...], 0.0)
        here = slice(128 * half, 128 * half + 128)
        for c in range(4):
            part = dot(some[256 * c : 256 * c + 256, :], band_rows[...])
            at = slice(8 * c, 8 * c + 8)
            smooth[at, :, here] = own[at, :, here] + part.reshape(8, 32, 128)
    for x in range(32):
        both = dot(my[...], smooth[x])
        out[x] = both[0:32]
        out_face[x : x + 1, :] = both[32:33]


def y_kernel(
    counts, where_ref, own, own_face, plane, got_b, got_a, face_ext, ext_b, ext_a, my, v,
    edges, out_face, out_plane, halo, x_a, x_b, got_ext, plane_low, plane_high,
):
    def choose(upper, lower):
        for j in range(7):
            halo[:, j, :] = lower[j]
        for j in range(6):
            halo[:, 8 + j, :] = upper[j]
        plane_low[...] = lower[7]
        plane_high[...] = upper[7]

    halo[:, 7, :] = jnp.zeros((32, 256), F32)
    halo[:, 14, :] = jnp.zeros((32, 256), F32)
    halo[:, 15, :] = jnp.zeros((32, 256), F32)
    by_parity(lax.rem(where_ref[1], 2) == 0, got_a, got_b, choose)

    @pl.when(where_ref[1] == 0)
    def _():
        halo[:, 0:8, :] = jnp.zeros((32, 8, 256), F32)
        plane_low[...] = jnp.zeros_like(plane_low)

    @pl.when(where_ref[1] == counts[1] - 1)
    def _():
        halo[:, 8:16, :] = jnp.zeros((32, 8, 256), F32)
        plane_high[...] = jnp.zeros_like(plane_high)

    out_face[8:24, :] = own_face[8:24, :]
    for i in range(16):
        x = i if i < 8 else i + 16
        both = dot(my[...], halo[x])
        edges[i] = own[x] + both[0:32]
        out_face[x : x + 1, :] = own_face[x : x + 1, :] + both[32:33]
    mine, low, high = plane[...], plane_low[...], plane_high[...]
    lane = lanes((32, 256))
    total = jnp.zeros((32, 256), F32)
    for c in range(1, 5):
        inside = (lane > 40 * c) & (lane <= 40 * c + 32)
        total = jnp.where(inside, pltpu.roll(mine, 8 * c + 1, 1), total)
        total = jnp.where(lane == 40 * c, pltpu.roll(low, (8 * c - 31) % 256, 1), total)
    wide = jnp.where(
        lane < 7,
        pltpu.roll(low, 256 - 25, 1),
        jnp.where(lane < 39, pltpu.roll(mine, 7, 1), jnp.where(lane < 45, pltpu.roll(high, 39, 1), 0.0)),
    )
    smoothed = dot(wide[:, 0:128], v[...])
    out_plane[:, 0:128] = jnp.where(lanes((32, 128)) < 40, smoothed, total[:, 0:128])
    out_plane[:, 128:256] = total[:, 128:256]

    def store(upper, lower):
        for j in range(7):
            upper[j] = edges[9 + j]
        upper[7] = jnp.zeros((32, 256), F32)
        upper[7, 0:8, :] = out_face[24:32, :]
        for e in range(4):
            corner = face_ext[e, 31:32, :]
            upper[7, 8 + e : 9 + e, :] = jnp.where(where_ref[1] == 0, 0.0, corner)
        upper[7, 16:24, :] = out_plane[24:32, :]
        for j in range(6):
            lower[j] = edges[j]
        lower[6] = jnp.zeros((32, 256), F32)
        lower[7] = jnp.zeros((32, 256), F32)
        lower[7, 0:8, :] = out_face[0:8, :]
        lower[7, 16:24, :] = out_plane[0:8, :]

    by_parity(lax.rem(where_ref[0], 2) == 0, x_a, x_b, store)

    def keep(_, lower):
        got_ext[...] = lower[...]

    by_parity(lax.rem(where_ref[0], 2) == 0, ext_a, ext_b, keep)


def fill_side(at, side, face_ext):
    for e in range(4):
        side[e, 0:32, :] = face_ext[e]
        side[e, 32:40, :] = jnp.zeros((8, 256), F32)

    @pl.when(at[1] == 0)
    def _():
        side[...] = jnp.zeros_like(side)


def faces(extents, at, mx, face_all, plane_all, side, face_e, face_a, column, inv_x, inv_yz):
    nx, ny, nz = extents
    ix, iy, iz = at
    shape = (40, 256)
    row, lane = rows(shape), lanes(shape)
    invx = inverse_total(ix * 32 + jnp.where(row < 32, row, -1), nx)
    inv_x[...] = invx
    small = (32, 256)
    invz = inverse_total(iz * 256 + lanes(small), nz)
    inv_yz[...] = inverse_total(iy * 32 + rows(small), ny) * invz

    def previous(value):
        return jnp.where(row == 0, value[32:33, :], pltpu.roll(value, 1, 0))

    def joined(t0, t1, t2):
        a0 = previous(t0) - t0
        a1 = previous(t1) + t1
        a2 = previous(t2) + t2
        return a0 + a1, a0 - a1, a2

    at_y = inverse_total(jnp.full((1, 256), iy * 32 - 1, jnp.int32), ny)
    kap = jnp.maximum(side[3], dot(mx[...], face_all[...]) * (invx * (at_y * invz[0:1, :])))
    integ = integrity_of(kap)
    e, _, a2 = joined(integ * side[0], integ * side[1], integ * side[2])
    face_e[...] = e[0:32]
    face_a[...] = a2[0:32]

    avg = dot(mx[...], plane_all[...])
    own = jnp.where(row == 32, plane_all[7:8, :], plane_all[8:48, :])

    def value(c):
        return pltpu.roll(own, (256 - 40 * c) % 256, 1)

    at_z = inverse_total(jnp.full((1, 256), iz * 256 - 1, jnp.int32), nz)
    invy = inverse_total(iy * 32 - 1 + jnp.minimum(lane, 32), ny)
    kap = jnp.maximum(value(4), avg * (invx * (invy * at_z)))
    integ = integrity_of(kap)
    e, f, a2 = joined(integ * value(1), integ * value(2), integ * value(3))
    parts = e + a2 + pltpu.roll(f + a2, 255, 1)
    parts = jnp.where(lane < 32, parts, 0.0)
    eye = (rows((32, 128)) == lanes((32, 128))).astype(F32)
    pad = jnp.concatenate([parts[0:32, 0:128], jnp.zeros((96, 128), F32)], axis=0)
    column[...] = dot_lanes(eye, pad)


def layer_results(x, avg, kappa, free, strain, before, face_e, face_a, column, force_at, kappa_at):
    first_row = rows((32, 256)) == 0
    first_lane = lanes((32, 128)) == 0
    kap = jnp.maximum(kappa[x], avg)
    integ = integrity_of(kap)
    s0, s1, s2 = integ * free[x], integ * strain[1, x], integ * strain[2, x]
    if force_at is not None:
        kappa_at[...] = kap
        a0 = before[0] - s0
        a1 = before[1] + s1
        a2 = before[2] + s2
        e, f = a0 + a1, a0 - a1
        b = f + jnp.where(first_row, face_e[pl.ds(x, 1), :], pltpu.roll(e, 1, 0))
        c = a2 + jnp.where(first_row, face_a[pl.ds(x, 1), :], pltpu.roll(a2, 1, 0))
        p, q = b + c, b - c
        moved = pltpu.roll(p, 1, 1)
        edge = pltpu.roll(column[...], lax.rem(128 - x, 128), 1)
        force_at[:, 0:128] = 0.25 * (q[:, 0:128] + jnp.where(first_lane, edge, moved[:, 0:128]))
        force_at[:, 128:256] = 0.25 * (q[:, 128:256] + moved[:, 128:256])
    before[0] = s0
    before[1] = s1
    before[2] = s2


def middle_kernel(
    extents, where_ref, strain, free, kappa, own, edges, halo, face, plane, face_ext, my,
    force, kappa_new, part, face_out,
    ext, face_all, plane_all, side, before, face_e, face_a, column, inv_x, inv_yz,
    force_v, kappa_v, sems,
):
    at = (where_ref[0], where_ref[1], where_ref[2])
    for x in range(32):
        if x < 8:
            ext[x] = edges[x]
        elif x >= 24:
            ext[x] = edges[x - 16]
        else:
            both = dot(my[:, 32:48], halo[x])
            ext[x] = own[x] + both[0:32]
            face_out[x : x + 1, :] = face[x : x + 1, :] + both[32:33]
    face_out[0:8, :] = face[0:8, :]
    face_out[24:32, :] = face[24:32, :]
    for ref, value in ((face_all, face_out), (plane_all, plane)):
        ref[0:8, :] = jnp.zeros((8, 256), F32)
        ref[8:40, :] = value[...]
        ref[40:48, :] = jnp.zeros((8, 256), F32)
    fill_side(at, side, face_ext)
    faces(
        extents, at, my.at[:, 48:96], face_all, plane_all, side,
        face_e, face_a, column, inv_x, inv_yz,
    )

    def layer(x):
        total = gauss(0) * ext[x]
        for a in range(1, REACH + 1):
            total = total + gauss(a) * (ext[x - a] + ext[x + a])
        return total * (inv_x[pl.ds(x, 1), :] * inv_yz[...])

    layer_results(7, layer(7), kappa, free, strain, before, None, None, None, None, None)
    copies = []
    for c in (1, 2):

        @pl.loop(0, CHUNK)
        def _(i):
            x = c * CHUNK + i
            layer_results(
                x, layer(x), kappa, free, strain, before, face_e, face_a, column,
                force_v.at[x - CHUNK], kappa_v.at[x - CHUNK],
            )

        here = pl.ds((c - 1) * CHUNK, CHUNK)
        there = pl.ds(c * CHUNK, CHUNK)
        for k, (src, dst) in enumerate(((force_v, force), (kappa_v, kappa_new))):
            copy = pltpu.make_async_copy(src.at[here], dst.at[there], sems.at[c - 1, k])
            copy.start()
            copies.append(copy)
    for i in range(18):
        x = i - 1 if i < 9 else i + 14
        total = None
        for a in range(-REACH, REACH + 1):
            if 0 <= x + a < 32:
                term = gauss(a) * ext[x + a]
                total = term if total is None else total + term
        part[i] = total
    for copy in copies:
        copy.wait()


def outer_kernel(
    extents, where_ref, strain, free, kappa, part, face, plane, face_ext, got_a, got_b, got_ext, my,
    force_in, kappa_in,
    force, kappa_new,
    low, high, face_all, plane_all, side, before, face_e, face_a, column, inv_x, inv_yz,
    force_v, kappa_v, sems,
):
    at = (where_ref[0], where_ref[1], where_ref[2])

    def choose(upper, lower):
        for j in range(7):
            low[j] = lower[j]
        for j in range(6):
            high[j] = upper[j]
        face_all[0:8, :] = lower[7, 0:8, :]
        face_all[40:48, :] = upper[7, 0:8, :]
        plane_all[0:8, :] = lower[7, 16:24, :]
        plane_all[40:48, :] = upper[7, 16:24, :]
        for e in range(4):
            side[e, 32:33, :] = lower[7, 8 + e : 9 + e, :]

    fill_side(at, side, face_ext)
    by_parity(lax.rem(at[0], 2) == 0, got_a, got_b, choose)
    before[...] = got_ext[...]

    @pl.when(at[0] == 0)
    def _():
        low[...] = jnp.zeros_like(low)
        before[...] = jnp.zeros_like(before)
        face_all[0:8, :] = jnp.zeros((8, 256), F32)
        plane_all[0:8, :] = jnp.zeros((8, 256), F32)
        for e in range(4):
            side[e, 32:33, :] = jnp.zeros((1, 256), F32)

    @pl.when(at[0] == extents[0] // 32 - 1)
    def _():
        high[...] = jnp.zeros_like(high)
        face_all[40:48, :] = jnp.zeros((8, 256), F32)
        plane_all[40:48, :] = jnp.zeros((8, 256), F32)

    face_all[8:40, :] = face[...]
    plane_all[8:40, :] = plane[...]
    faces(
        extents, at, my.at[:, 48:96], face_all, plane_all, side,
        face_e, face_a, column, inv_x, inv_yz,
    )

    def layer(x):
        total = part[x + 1 if x < 8 else x - 14]
        for a in range(-REACH, REACH + 1):
            if x + a < 0:
                total = total + gauss(a) * low[x + a + 7]
            elif x + a >= 32:
                total = total + gauss(a) * high[x + a - 32]
        return total * (inv_x[x % 33 : x % 33 + 1, :] * inv_yz[...])

    kap = jnp.maximum(before[3], layer(-1))
    integ = integrity_of(kap)
    for e in range(3):
        before[e] = integ * before[e]
    copies = []
    for c in (0, 3):
        if c == 3:
            layer_results(23, layer(23), kappa, free, strain, before, None, None, None, None, None)
        for i in range(CHUNK):
            x = c * CHUNK + i
            slot = i if c == 0 else CHUNK + i
            layer_results(
                x, layer(x), kappa, free, strain, before, face_e, face_a, column,
                force_v.at[slot], kappa_v.at[slot],
            )
        here = pl.ds(0 if c == 0 else CHUNK, CHUNK)
        there = pl.ds(c * CHUNK, CHUNK)
        for k, (src, dst) in enumerate(((force_v, force), (kappa_v, kappa_new))):
            copy = pltpu.make_async_copy(src.at[here], dst.at[there], sems.at[c // 3, k])
            copy.start()
            copies.append(copy)
    for copy in copies:
        copy.wait()


AXES = ("gx", "gy", "gz")


def swap(first, second, axis):
    sizes = [lax.axis_size(a) for a in AXES]
    at = AXES.index(axis)
    other = 0 if at == 1 else 1

    def route(start):
        out = []
        for place in np.ndindex(*sizes):
            there = list(place)
            if place[at] >= start and place[at] - start < (sizes[at] - start) // 2 * 2:
                there[at] += 1 if (place[at] - start) % 2 == 0 else -1
            else:
                there[other] ^= 1
            out.append(tuple(int(np.ravel_multi_index(p, sizes)) for p in (place, tuple(there))))
        return out

    return lax.ppermute(first, AXES, route(0)), lax.ppermute(second, AXES, route(1))


def to_next(block, axis):
    count = lax.axis_size(axis)
    return lax.ppermute(block, axis, [(i, (i + 1) % count) for i in range(count)])


def shape_of(*dims):
    return jax.ShapeDtypeStruct(dims, F32)


VM = pl.BlockSpec(memory_space=pltpu.VMEM)
SM = pl.BlockSpec(memory_space=pltpu.SMEM)
HBM = pl.BlockSpec(memory_space=pltpu.HBM)
BLOCK = shape_of(32, 32, 256)
FACE = shape_of(32, 256)


def vmem(*dims):
    return pltpu.VMEM(dims, F32)


def call(kernel, name, in_specs, out_shape, out_specs=None, scratch=(), **kwargs):
    return pl.pallas_call(
        kernel,
        name=name,
        in_specs=in_specs,
        out_specs=out_specs or [VM] * len(out_shape),
        out_shape=out_shape,
        scratch_shapes=list(scratch),
        interpret=INTERPRET,
        compiler_params=pltpu.CompilerParams(vmem_limit_bytes=VMEM_LIMIT),
        **kwargs,
    )


def body(strain_in, plastic_in, alpha_in, kappa, flags):
    where = jnp.stack([lax.axis_index(a) for a in AXES]).astype(jnp.int32)
    flags = flags.reshape(32, 32)
    counts = tuple(lax.axis_size(a) for a in AXES)
    extents = (32 * counts[0], 32 * counts[1], 256 * counts[2])
    rows_all = rows_matrix()
    rows_own = np.ascontiguousarray(rows_all[:, 8:40])
    rows_halo = np.concatenate(
        [rows_all[:, 1:8], np.zeros((40, 1), np.float32), rows_all[:, 40:48]], axis=1
    )
    rows_three = np.zeros((40, 128), np.float32)
    rows_three[:, 32:48] = rows_halo
    rows_three[:, 48:96] = rows_all

    whole_in = [
        pltpu.with_memory_space_constraint(v, pltpu.HBM)
        for v in (strain_in, plastic_in, alpha_in, kappa, flags)
    ]
    ends, eight = shape_of(4, 32, 256), shape_of(8, 32, 256)
    square = shape_of(128, 128)
    strain, plastic, alpha, turned, z_b, z_a, yext = call(
        pack_kernel,
        "pack",
        [SM] + [HBM] * 5,
        [
            shape_of(3, 32, 32, 256), BLOCK, BLOCK, shape_of(32, 32), square, square, ends,
        ],
        scratch=[vmem(32, 32, 128), vmem(32, 8, 128), pltpu.VMEM((32, 32), jnp.int32)]
        + [vmem(128, 128)] * 6
        + [pltpu.SemaphoreType.DMA((CHUNKS + 1, 4))],
    )(where, *whole_in)
    got_a, got_b = swap(z_a, z_b, "gz")
    face_ext = to_next(yext, "gy")
    own, free, xext = call(
        inner_kernel, "inner", [VM] * 6, [BLOCK, BLOCK, ends], scratch=[vmem(32, 32, 256)]
    )(strain, plastic, alpha, kappa, turned, z_band(256))
    t_low, t_high = z_low_rows(), z_high_rows()
    plane, y_a, y_b, z_low, z_high, xext = call(
        functools.partial(z_kernel, counts),
        "along_z",
        [SM] + [VM] * 11,
        [FACE, eight, eight, square, square, ends],
        scratch=[vmem(128, 128)] + [vmem(32, 128)] * 2 + [vmem(512, 128)] * 2
        + [vmem(2, 32, 8, 256)],
    )(
        where, own, xext, z_b, z_a, got_b, got_a, face_ext,
        t_low, t_high, plane_from_low(), plane_from_own(),
    )
    got_a, got_b = swap(y_a, y_b, "gy")
    ext_a, ext_b = swap(xext, xext, "gx")
    own, own_face = call(
        own_rows_kernel,
        "own_rows",
        [VM] * 6,
        [BLOCK, FACE],
        scratch=[vmem(1024, 128), vmem(32, 32, 256)],
    )(own, z_low, z_high, t_low, t_high, rows_own)

    edges, face, plane, halo, x_a, x_b, got_ext = call(
        functools.partial(y_kernel, counts),
        "along_y",
        [SM] + [VM] * 10,
        [shape_of(16, 32, 256), FACE, FACE, shape_of(32, 16, 256), eight, eight, ends],
        scratch=[vmem(32, 256), vmem(32, 256)],
    )(where, own, own_face, plane, got_b, got_a, face_ext, ext_b, ext_a, rows_halo, plane_y_matrix())
    got_a, got_b = swap(x_a, x_b, "gx")

    shared = [
        vmem(48, 256), vmem(48, 256), vmem(4, 40, 256), vmem(4, 32, 256),
        vmem(32, 256), vmem(32, 256), vmem(32, 128), vmem(40, 256), vmem(32, 256),
        vmem(16, 32, 256), vmem(16, 32, 256), pltpu.SemaphoreType.DMA((2, 2)),
    ]
    force, kappa_new, part, face = call(
        functools.partial(middle_kernel, extents),
        "middle",
        [SM] + [VM] * 10,
        [BLOCK, BLOCK, shape_of(18, 32, 256), FACE],
        out_specs=[HBM, HBM, VM, VM],
        scratch=[vmem(32, 32, 256)] + shared,
    )(where, strain, free, kappa, own, edges, halo, face, plane, face_ext, rows_three)
    force, kappa_new = call(
        functools.partial(outer_kernel, extents),
        "outer",
        [SM] + [VM] * 11 + [HBM, HBM],
        [BLOCK, BLOCK],
        out_specs=[HBM, HBM],
        scratch=[vmem(7, 32, 256), vmem(6, 32, 256)] + shared,
        input_output_aliases={12: 0, 13: 1},
    )(
        where, strain, free, kappa, part, face, plane, face_ext, got_a, got_b, got_ext, rows_three,
        force, kappa_new,
    )
    return (force, kappa_new)


def solution(mesh):
    in_specs = (
        P(None, "gx", "gy", "gz"),
        P("gx", "gy", "gz"),
        P("gx", "gy", "gz"),
        P("gx", "gy", "gz"),
        P("gx", "gy", "gz"),
    )
    out_specs = (P("gx", "gy", "gz"), P("gx", "gy", "gz"))
    return jax.shard_map(body, mesh=mesh, in_specs=in_specs, out_specs=out_specs, check_vma=False)
```

```python
import functools
import math

import jax
import jax.numpy as jnp
import numpy as np
from jax import lax
from jax.experimental import pallas as pl
from jax.experimental.pallas import tpu as pltpu
from jax.sharding import PartitionSpec as P

REACH = 6
RM_ITERS = 2
LENGTH_SCALE = 3.0
HIGHEST = lax.Precision.HIGHEST
F32 = jnp.float32
VMEM_LIMIT = 40 * 1024 * 1024
INTERPRET = False


def gauss(offset):
    return math.exp(-offset * offset / (2.0 * LENGTH_SCALE * LENGTH_SCALE))


def band(offset):
    return gauss(offset) if abs(offset) <= REACH else 0.0


def z_band(width):
    return np.array([[band(i - k) for k in range(width)] for i in range(width)], np.float32)


def z_halo_rows():
    out = np.zeros((256, 256), np.float32)
    for r in range(128):
        c = r % 16
        for k in range(256):
            out[r, k] = band(k - (c - 7)) if c < 7 else 0.0
            out[128 + r, k] = band(256 + c - k) if c < 6 else 0.0
    return out


def plane_from_low():
    out = np.zeros((40, 128), np.float32)
    for g in range(8):
        for c in range(7):
            out[g, 16 * g + c] = band(c - 6)
        for e in range(4):
            out[8 * (1 + e) + g, 16 * g + 7 + e] = 1.0
    return out


def plane_from_own():
    out = np.zeros((40, 128), np.float32)
    for g in range(8):
        for c in range(6):
            out[g, 16 * g + c] = band(c + 1)
    return out


def rows_matrix():
    out = np.zeros((40, 48), np.float32)
    for r in range(33):
        at = r if r < 32 else -1
        for k in range(1, 46):
            out[r, k] = band(k - 8 - at)
    return out


def plane_y_matrix():
    out = np.zeros((128, 128), np.float32)
    for y in range(-1, 32):
        for k in range(45):
            out[k, y + 1] = band(k - 7 - y)
    return out


def lanes(shape):
    return lax.broadcasted_iota(jnp.int32, shape, len(shape) - 1)


def rows(shape):
    return lax.broadcasted_iota(jnp.int32, shape, len(shape) - 2)


def inverse_total(position, extent):
    total = jnp.zeros(position.shape, F32)
    for offset in range(-REACH, REACH + 1):
        inside = (position + offset >= 0) & (position + offset < extent)
        total = total + jnp.where(inside, F32(gauss(offset)), F32(0.0))
    return 1.0 / total


def newton_plastic(trial, alpha_old):
    increment = jnp.zeros(trial.shape, F32)
    for _ in range(RM_ITERS):
        hardened = alpha_old + increment
        soft = 0.5 * jnp.exp(-5.0 * hardened)
        excess = trial - increment - (1.0 + 0.5 * hardened - soft)
        increment = jnp.maximum(increment + excess / (1.5 + 5.0 * soft), 0.0)
    return increment


def field_of(first, second, third):
    return first * first + second * second + third * third


def integrity_of(kappa):
    return jnp.exp(-jnp.maximum(kappa - 3.2, 0.0) / 3.0)


def by_parity(even, first, second, use):
    @pl.when(even)
    def _():
        use(first, second)

    @pl.when(jnp.logical_not(even))
    def _():
        use(second, first)


CONTRACT_LANES = (((1,), (1,)), ((), ()))
CHUNK = 8
CHUNKS = 4


def dot(left, right):
    return jnp.dot(left, right, precision=HIGHEST, preferred_element_type=F32)


def dot_lanes(left, right, precision=HIGHEST):
    return lax.dot_general(
        left, right, CONTRACT_LANES, precision=precision, preferred_element_type=F32
    )


def turned_flags(flags):
    eye = (rows((32, 32)) == lanes((32, 32))).astype(F32)
    return dot_lanes(eye, flags[...].astype(F32), None)


def pack_kernel(
    where_ref, strain_in, plastic_in, alpha_in, kappa_in, flags,
    strain, plastic, alpha, turned, z_b, z_a, yext,
    kappa_high, kappa_low, flags_v, up_trial, up_alpha, up_drive, low_trial, low_alpha, low_drive, sems,
):
    flags_copy = pltpu.make_async_copy(flags, flags_v, sems.at[CHUNKS, 0])
    flags_copy.start()
    copies = []
    for c in range(CHUNKS):
        part = pl.ds(c * CHUNK, CHUNK)
        pairs = [(strain_in.at[:, part], strain.at[:, part])]
        pairs += [
            (src.at[part], dst.at[part])
            for src, dst in ((plastic_in, plastic), (alpha_in, alpha))
        ]
        pairs.append((kappa_in.at[part, :, 128:256], kappa_high.at[part]))
        copies.append(
            [pltpu.make_async_copy(src, dst, sems.at[c, i]) for i, (src, dst) in enumerate(pairs)]
        )
    for group in copies:
        for copy in group:
            copy.start()
    row_copy = pltpu.make_async_copy(
        kappa_in.at[:, 24:32, 0:128], kappa_low, sems.at[CHUNKS, 1]
    )
    row_copy.start()
    flags_copy.wait()
    turned[...] = turned_flags(flags_v)
    flag = jnp.concatenate(
        [
            jnp.dot(
                turned[...],
                (rows((32, 128)) == 4 * (lanes((32, 128)) // 16) + b).astype(F32),
                preferred_element_type=F32,
            )
            for b in range(4)
        ],
        axis=0,
    )
    lane = lanes((128, 128))
    for c in range(CHUNKS):
        for copy in copies[c]:
            copy.wait()
        for g in (2 * c, 2 * c + 1):
            inside = lane // 16 == g

            def tile(ref, half):
                cells = ref[4 * g : 4 * g + 4, :, 128 * half : 128 * half + 128]
                return cells.reshape(128, 128)

            def place(ref, value, move):
                moved = pltpu.roll(value, (move + 16 * g) % 128, 1) if move + 16 * g else value
                ref[...] = jnp.where(inside, moved, ref[...])

            s0, s1, s2 = (tile(strain.at[i], 1) for i in range(3))
            place(up_trial, s0 - tile(plastic, 1), 7)
            place(up_alpha, tile(alpha, 1), 7)
            place(up_drive, field_of(s0, s1, s2), 7)
            mixed = up_drive[...]
            edge = kappa_high[4 * g : 4 * g + 4].reshape(128, 128)
            for e, value in enumerate((s1, s2, edge)):
                moved = pltpu.roll(value, (9 + e + 16 * g) % 128, 1)
                mixed = jnp.where(lane == 16 * g + 8 + e, moved, mixed)
            up_drive[...] = mixed
            s0, s1, s2 = (tile(strain.at[i], 0) for i in range(3))
            place(low_trial, s0 - tile(plastic, 0), 0)
            place(low_alpha, tile(alpha, 0), 0)
            place(low_drive, field_of(s0, s1, s2), 0)

    trial = strain[0, :, 31, :] - plastic[:, 31, :]
    flag_y = jnp.broadcast_to(flags_v[:, 31:32].astype(F32), (32, 256))
    yext[0] = trial - newton_plastic(trial, alpha[:, 31, :]) * flag_y
    yext[1] = strain[1, :, 31, :]
    yext[2] = strain[2, :, 31, :]
    row_copy.wait()
    yext[3, :, 0:128] = kappa_low[:, 7, :]
    yext[3, :, 128:256] = kappa_high[:, 31, :]

    increment = newton_plastic(up_trial[...], up_alpha[...]) * flag
    free = pltpu.roll(up_trial[...] - increment, 1, 1)
    up_drive[...] = jnp.where(
        lane % 16 < 7,
        up_drive[...] + 4.0 * increment,
        jnp.where(lane % 16 == 7, free, up_drive[...]),
    )
    increment = newton_plastic(low_trial[...], low_alpha[...]) * flag
    low_drive[...] = low_drive[...] + 4.0 * increment

    def store(upper, lower):
        upper[...] = up_drive[...]
        lower[...] = low_drive[...]

    by_parity(lax.rem(where_ref[2], 2) == 0, z_a, z_b, store)


def inner_kernel(strain, plastic, alpha, kappa, turned, bz, smooth, free, xext, field):
    @pl.loop(0, 8)
    def _(g):
        for i in range(4):
            x = 4 * g + i
            here = (rows((32, 256)) == x).astype(F32)
            flag = jnp.dot(turned[...], here, preferred_element_type=F32)
            s0 = strain[0, x]
            trial = s0 - plastic[x]
            increment = newton_plastic(trial, alpha[x]) * flag
            field[x] = field_of(s0, strain[1, x], strain[2, x]) + 4.0 * increment
            free[x] = trial - increment

    for g in range(4):
        part = field[8 * g : 8 * g + 8].reshape(256, 256)
        smooth[8 * g : 8 * g + 8] = dot(part, bz[...]).reshape(8, 32, 256)
    for e, ref in enumerate((free, strain.at[1], strain.at[2], kappa)):
        xext[e] = ref[31]


def z_kernel(
    counts, where_ref, own, xext_in, sent_b, sent_a, got_b, got_a, _, t, w,
    plane, y_a, y_b, z_both, xext, turn, head_rows, tail_rows, some, ends,
):
    xext[...] = xext_in[...]

    def choose(upper, lower):
        z_both[:, 128:256] = upper[0][...]
        z_both[:, 0:128] = lower[0][...]
        turn[:, 0:128] = lower[0][...]
        turn[:, 128:256] = lower[1][...]

    by_parity(lax.rem(where_ref[2], 2) == 0, (got_a, sent_a), (got_b, sent_b), choose)

    @pl.when(where_ref[2] == 0)
    def _():
        z_both[:, 0:128] = jnp.zeros((128, 128), F32)
        turn[:, 0:128] = jnp.zeros((128, 128), F32)

    @pl.when(where_ref[2] == counts[2] - 1)
    def _():
        z_both[:, 128:256] = jnp.zeros((128, 128), F32)

    group = lanes((8, 256)) % 128 // 16
    for half in range(2):
        for x in range(32):
            start = 32 * (x % 4) + 24 * half
            at = 256 * half + 8 * x
            some[at : at + 8, :] = jnp.where(group == x // 4, z_both[start : start + 8, :], 0.0)
    added = dot(some[...], t[...])
    for half in range(2):
        here = slice(24 * half, 24 * half + 8)
        part = added[256 * half : 256 * half + 256]
        ends[half] = own[:, here, :] + part.reshape(32, 8, 256)
    turned = dot_lanes(w[...], turn[...])
    lane = lanes((8, 128))
    for b in range(4):
        head = jnp.zeros((8, 128), F32)
        for c in range(4):
            moved = pltpu.roll(turned[8 * c : 8 * c + 8], (32 * (c - b)) % 128, 1)
            head = jnp.where(lane // 32 == c, moved, head)
        tail = jnp.where(lane < 32, pltpu.roll(turned[32:40], (-32 * b) % 128, 1), 0.0)
        head_rows[pl.ds(b, 8, stride=4), :] = head
        tail_rows[pl.ds(b, 8, stride=4), :] = tail
    plane[:, 0:128] = head_rows[...]
    plane[:, 128:256] = tail_rows[...]

    def store(upper, lower):
        for j in range(7):
            upper[j] = ends[1, :, 1 + j, :]
        upper[7] = plane[...]
        for j in range(6):
            lower[j] = ends[0, :, j, :]
        lower[6] = plane[...]
        lower[7] = plane[...]

    by_parity(lax.rem(where_ref[1], 2) == 0, y_a, y_b, store)


def own_rows_kernel(
    extents, where_ref, own, z_both, t, my,
    out, out_face, inv_x, inv_yz, inv_face, inv_plane, some, smooth,
):
    group = lanes((128, 256)) % 128 // 16
    for g in range(8):
        some[128 * g : 128 * g + 128, :] = jnp.where(group == g, z_both[...], 0.0)
    for c in range(4):
        part = dot(some[256 * c : 256 * c + 256, :], t[...])
        at = slice(8 * c, 8 * c + 8)
        smooth[at] = own[at] + part.reshape(8, 32, 256)
    for x in range(32):
        both = dot(my[...], smooth[x])
        out[x] = both[0:32]
        out_face[x : x + 1, :] = both[32:33]

    nx, ny, nz = extents
    ix, iy, iz = where_ref[0], where_ref[1], where_ref[2]
    shape, small, line = (40, 256), (32, 256), (1, 256)
    row, lane = rows(shape), lanes(shape)
    invx = inverse_total(ix * 32 + jnp.where(row < 32, row, -1), nx)
    inv_x[...] = invx
    invz = inverse_total(iz * 256 + lanes(line), nz)
    inv_yz[...] = inverse_total(iy * 32 + rows(small), ny) * invz
    at_y = inverse_total(jnp.full(line, iy * 32 - 1, jnp.int32), ny)
    inv_face[...] = invx * (at_y * invz)
    at_z = inverse_total(jnp.full(line, iz * 256 - 1, jnp.int32), nz)
    invy = inverse_total(iy * 32 - 1 + jnp.minimum(lanes(line), 32), ny)
    inv_plane[...] = invx * (invy * at_z)


def y_kernel(
    counts, where_ref, own, own_face, plane, got_b, got_a, face_ext, ext_b, ext_a, my, v,
    edges, out_face, out_plane, halo, x_a, x_b, got_ext, plane_low, plane_high,
):
    def choose(upper, lower):
        for j in range(7):
            halo[:, j, :] = lower[j]
        for j in range(6):
            halo[:, 8 + j, :] = upper[j]
        plane_low[...] = lower[7]
        plane_high[...] = upper[7]

    halo[:, 7, :] = jnp.zeros((32, 256), F32)
    halo[:, 14, :] = jnp.zeros((32, 256), F32)
    halo[:, 15, :] = jnp.zeros((32, 256), F32)
    by_parity(lax.rem(where_ref[1], 2) == 0, got_a, got_b, choose)

    @pl.when(where_ref[1] == 0)
    def _():
        halo[:, 0:8, :] = jnp.zeros((32, 8, 256), F32)
        plane_low[...] = jnp.zeros_like(plane_low)

    @pl.when(where_ref[1] == counts[1] - 1)
    def _():
        halo[:, 8:16, :] = jnp.zeros((32, 8, 256), F32)
        plane_high[...] = jnp.zeros_like(plane_high)

    out_face[8:24, :] = own_face[8:24, :]
    for i in range(16):
        x = i if i < 8 else i + 16
        both = dot(my[...], halo[x])
        edges[i, 0:8, :] = own[x, 0:8, :] + both[0:8]
        edges[i, 8:24, :] = own[x, 8:24, :]
        edges[i, 24:32, :] = own[x, 24:32, :] + both[8:16]
        out_face[x : x + 1, :] = own_face[x : x + 1, :] + both[16:17]
    mine, low, high = plane[...], plane_low[...], plane_high[...]
    lane = lanes((32, 256))
    total = jnp.zeros((32, 256), F32)
    for c in range(1, 5):
        inside = (lane > 40 * c) & (lane <= 40 * c + 32)
        total = jnp.where(inside, pltpu.roll(mine, 8 * c + 1, 1), total)
        total = jnp.where(lane == 40 * c, pltpu.roll(low, (8 * c - 31) % 256, 1), total)
    wide = jnp.where(
        lane < 7,
        pltpu.roll(low, 256 - 25, 1),
        jnp.where(lane < 39, pltpu.roll(mine, 7, 1), jnp.where(lane < 45, pltpu.roll(high, 39, 1), 0.0)),
    )
    smoothed = dot(wide[:, 0:128], v[...])
    out_plane[:, 0:128] = jnp.where(lanes((32, 128)) < 40, smoothed, total[:, 0:128])
    out_plane[:, 128:256] = total[:, 128:256]

    def store(upper, lower):
        for j in range(7):
            upper[j] = edges[9 + j]
        upper[7] = jnp.zeros((32, 256), F32)
        upper[7, 0:8, :] = out_face[24:32, :]
        for e in range(4):
            corner = face_ext[e, 31:32, :]
            upper[7, 8 + e : 9 + e, :] = jnp.where(where_ref[1] == 0, 0.0, corner)
        upper[7, 16:24, :] = out_plane[24:32, :]
        for j in range(6):
            lower[j] = edges[j]
        lower[6] = jnp.zeros((32, 256), F32)
        lower[7] = jnp.zeros((32, 256), F32)
        lower[7, 0:8, :] = out_face[0:8, :]
        lower[7, 16:24, :] = out_plane[0:8, :]

    by_parity(lax.rem(where_ref[0], 2) == 0, x_a, x_b, store)

    def keep(_, lower):
        got_ext[...] = lower[...]

    by_parity(lax.rem(where_ref[0], 2) == 0, ext_a, ext_b, keep)


def fill_side(at, side, face_ext):
    for e in range(4):
        side[e, 0:32, :] = face_ext[e]
        side[e, 32:40, :] = jnp.zeros((8, 256), F32)

    @pl.when(at[1] == 0)
    def _():
        side[...] = jnp.zeros_like(side)


def faces(mx, face_all, plane_all, side, face_e, face_a, column, inv_face, inv_plane):
    shape = (40, 256)
    row, lane = rows(shape), lanes(shape)

    def previous(value):
        return jnp.where(row == 0, value[32:33, :], pltpu.roll(value, 1, 0))

    def joined(t0, t1, t2):
        a0 = previous(t0) - t0
        a1 = previous(t1) + t1
        a2 = previous(t2) + t2
        return a0 + a1, a0 - a1, a2

    kap = jnp.maximum(side[3], dot(mx[...], face_all[...]) * inv_face[...])
    integ = integrity_of(kap)
    e, _, a2 = joined(integ * side[0], integ * side[1], integ * side[2])
    face_e[...] = e[0:32]
    face_a[...] = a2[0:32]

    avg = dot(mx[...], plane_all[...])
    own = jnp.where(row == 32, plane_all[7:8, :], plane_all[8:48, :])

    def value(c):
        return pltpu.roll(own, (256 - 40 * c) % 256, 1)

    kap = jnp.maximum(value(4), avg * inv_plane[...])
    integ = integrity_of(kap)
    e, f, a2 = joined(integ * value(1), integ * value(2), integ * value(3))
    parts = e + a2 + pltpu.roll(f + a2, 255, 1)
    parts = jnp.where(lane < 32, parts, 0.0)
    eye = (rows((32, 128)) == lanes((32, 128))).astype(F32)
    pad = jnp.concatenate([parts[0:32, 0:128], jnp.zeros((96, 128), F32)], axis=0)
    column[...] = dot_lanes(eye, pad)


def layer_results(x, avg, kappa, free, strain, before, face_e, face_a, column, force_at, kappa_at):
    first_row = rows((32, 256)) == 0
    first_lane = lanes((32, 128)) == 0
    kap = jnp.maximum(kappa[x], avg)
    integ = integrity_of(kap)
    s0, s1, s2 = integ * free[x], integ * strain[1, x], integ * strain[2, x]
    if force_at is not None:
        kappa_at[...] = kap
        a0 = before[0] - s0
        a1 = before[1] + s1
        a2 = before[2] + s2
        e, f = a0 + a1, a0 - a1
        b = f + jnp.where(first_row, face_e[pl.ds(x, 1), :], pltpu.roll(e, 1, 0))
        c = a2 + jnp.where(first_row, face_a[pl.ds(x, 1), :], pltpu.roll(a2, 1, 0))
        p, q = b + c, b - c
        moved = pltpu.roll(p, 1, 1)
        edge = pltpu.roll(column[...], lax.rem(128 - x, 128), 1)
        force_at[:, 0:128] = 0.25 * (q[:, 0:128] + jnp.where(first_lane, edge, moved[:, 0:128]))
        force_at[:, 128:256] = 0.25 * (q[:, 128:256] + moved[:, 128:256])
    before[0] = s0
    before[1] = s1
    before[2] = s2


def middle_kernel(
    where_ref, strain, free, kappa, own, edges, halo, face, plane, face_ext,
    inv_x, inv_yz, inv_face, inv_plane, my,
    force, kappa_new, part, face_out,
    ext, face_all, plane_all, side, before, face_e, face_a, column,
    force_v, kappa_v, sems,
):
    at = (where_ref[0], where_ref[1], where_ref[2])
    for x in range(32):
        if x < 8:
            ext[x] = edges[x]
        elif x >= 24:
            ext[x] = edges[x - 16]
        else:
            both = dot(my[0:24, 0:16], halo[x])
            ext[x, 0:8, :] = own[x, 0:8, :] + both[0:8]
            ext[x, 8:24, :] = own[x, 8:24, :]
            ext[x, 24:32, :] = own[x, 24:32, :] + both[8:16]
            face_out[x : x + 1, :] = face[x : x + 1, :] + both[16:17]
    face_out[0:8, :] = face[0:8, :]
    face_out[24:32, :] = face[24:32, :]
    for ref, value in ((face_all, face_out), (plane_all, plane)):
        ref[0:8, :] = jnp.zeros((8, 256), F32)
        ref[8:40, :] = value[...]
        ref[40:48, :] = jnp.zeros((8, 256), F32)
    fill_side(at, side, face_ext)
    faces(
        my.at[:, 48:96], face_all, plane_all, side, face_e, face_a, column, inv_face, inv_plane
    )

    def layer(x):
        total = gauss(0) * ext[x]
        for a in range(1, REACH + 1):
            total = total + gauss(a) * (ext[x - a] + ext[x + a])
        return total * (inv_x[pl.ds(x, 1), :] * inv_yz[...])

    layer_results(7, layer(7), kappa, free, strain, before, None, None, None, None, None)
    copies = []
    for c in (1, 2):

        @pl.loop(0, CHUNK)
        def _(i):
            x = c * CHUNK + i
            layer_results(
                x, layer(x), kappa, free, strain, before, face_e, face_a, column,
                force_v.at[x - CHUNK], kappa_v.at[x - CHUNK],
            )

        here = pl.ds((c - 1) * CHUNK, CHUNK)
        there = pl.ds(c * CHUNK, CHUNK)
        for k, (src, dst) in enumerate(((force_v, force), (kappa_v, kappa_new))):
            copy = pltpu.make_async_copy(src.at[here], dst.at[there], sems.at[c - 1, k])
            copy.start()
            copies.append(copy)
    for i in range(18):
        x = i - 1 if i < 9 else i + 14
        total = None
        for a in range(-REACH, REACH + 1):
            if 0 <= x + a < 32:
                term = gauss(a) * ext[x + a]
                total = term if total is None else total + term
        part[i] = total
    for copy in copies:
        copy.wait()


def outer_kernel(
    counts, where_ref, strain, free, kappa, part, face, plane, face_ext, got_a, got_b, got_ext,
    inv_x, inv_yz, inv_face, inv_plane, my,
    force_in, kappa_in,
    force, kappa_new,
    low, high, face_all, plane_all, side, before, face_e, face_a, column,
    force_v, kappa_v, sems,
):
    at = (where_ref[0], where_ref[1], where_ref[2])

    def choose(upper, lower):
        for j in range(7):
            low[j] = lower[j]
        for j in range(6):
            high[j] = upper[j]
        face_all[0:8, :] = lower[7, 0:8, :]
        face_all[40:48, :] = upper[7, 0:8, :]
        plane_all[0:8, :] = lower[7, 16:24, :]
        plane_all[40:48, :] = upper[7, 16:24, :]
        for e in range(4):
            side[e, 32:33, :] = lower[7, 8 + e : 9 + e, :]

    fill_side(at, side, face_ext)
    by_parity(lax.rem(at[0], 2) == 0, got_a, got_b, choose)
    before[...] = got_ext[...]

    @pl.when(at[0] == 0)
    def _():
        low[...] = jnp.zeros_like(low)
        before[...] = jnp.zeros_like(before)
        face_all[0:8, :] = jnp.zeros((8, 256), F32)
        plane_all[0:8, :] = jnp.zeros((8, 256), F32)
        for e in range(4):
            side[e, 32:33, :] = jnp.zeros((1, 256), F32)

    @pl.when(at[0] == counts[0] - 1)
    def _():
        high[...] = jnp.zeros_like(high)
        face_all[40:48, :] = jnp.zeros((8, 256), F32)
        plane_all[40:48, :] = jnp.zeros((8, 256), F32)

    face_all[8:40, :] = face[...]
    plane_all[8:40, :] = plane[...]
    faces(
        my.at[:, 48:96], face_all, plane_all, side, face_e, face_a, column, inv_face, inv_plane
    )

    def layer(x):
        total = part[x + 1 if x < 8 else x - 14]
        for a in range(-REACH, REACH + 1):
            if x + a < 0:
                total = total + gauss(a) * low[x + a + 7]
            elif x + a >= 32:
                total = total + gauss(a) * high[x + a - 32]
        return total * (inv_x[x % 33 : x % 33 + 1, :] * inv_yz[...])

    kap = jnp.maximum(before[3], layer(-1))
    integ = integrity_of(kap)
    for e in range(3):
        before[e] = integ * before[e]
    copies = []
    for c in (0, 3):
        if c == 3:
            layer_results(23, layer(23), kappa, free, strain, before, None, None, None, None, None)
        for i in range(CHUNK):
            x = c * CHUNK + i
            slot = i if c == 0 else CHUNK + i
            layer_results(
                x, layer(x), kappa, free, strain, before, face_e, face_a, column,
                force_v.at[slot], kappa_v.at[slot],
            )
        here = pl.ds(0 if c == 0 else CHUNK, CHUNK)
        there = pl.ds(c * CHUNK, CHUNK)
        for k, (src, dst) in enumerate(((force_v, force), (kappa_v, kappa_new))):
            copy = pltpu.make_async_copy(src.at[here], dst.at[there], sems.at[c // 3, k])
            copy.start()
            copies.append(copy)
    for copy in copies:
        copy.wait()


AXES = ("gx", "gy", "gz")


def swap(first, second, axis):
    sizes = [lax.axis_size(a) for a in AXES]
    at = AXES.index(axis)
    other = 0 if at == 1 else 1

    def route(start):
        out = []
        for place in np.ndindex(*sizes):
            there = list(place)
            if place[at] >= start and place[at] - start < (sizes[at] - start) // 2 * 2:
                there[at] += 1 if (place[at] - start) % 2 == 0 else -1
            else:
                there[other] ^= 1
            out.append(tuple(int(np.ravel_multi_index(p, sizes)) for p in (place, tuple(there))))
        return out

    return lax.ppermute(first, AXES, route(0)), lax.ppermute(second, AXES, route(1))


def to_next(block, axis):
    count = lax.axis_size(axis)
    return lax.ppermute(block, axis, [(i, (i + 1) % count) for i in range(count)])


def shape_of(*dims):
    return jax.ShapeDtypeStruct(dims, F32)


VM = pl.BlockSpec(memory_space=pltpu.VMEM)
SM = pl.BlockSpec(memory_space=pltpu.SMEM)
HBM = pl.BlockSpec(memory_space=pltpu.HBM)
BLOCK = shape_of(32, 32, 256)
FACE = shape_of(32, 256)


def vmem(*dims):
    return pltpu.VMEM(dims, F32)


def call(kernel, name, in_specs, out_shape, out_specs=None, scratch=(), **kwargs):
    return pl.pallas_call(
        kernel,
        name=name,
        in_specs=in_specs,
        out_specs=out_specs or [VM] * len(out_shape),
        out_shape=out_shape,
        scratch_shapes=list(scratch),
        interpret=INTERPRET,
        compiler_params=pltpu.CompilerParams(vmem_limit_bytes=VMEM_LIMIT),
        **kwargs,
    )


def body(strain_in, plastic_in, alpha_in, kappa, flags):
    where = jnp.stack([lax.axis_index(a) for a in AXES]).astype(jnp.int32)
    flags = flags.reshape(32, 32)
    counts = tuple(lax.axis_size(a) for a in AXES)
    extents = (32 * counts[0], 32 * counts[1], 256 * counts[2])
    rows_all = rows_matrix()
    rows_own = np.ascontiguousarray(rows_all[:, 8:40])
    rows_halo = np.concatenate(
        [rows_all[:, 1:8], np.zeros((40, 1), np.float32), rows_all[:, 40:48]], axis=1
    )
    rows_halo = np.concatenate([rows_halo[0:8], rows_halo[24:40]], axis=0)
    rows_three = np.zeros((40, 128), np.float32)
    rows_three[0:24, 0:16] = rows_halo
    rows_three[:, 48:96] = rows_all

    whole_in = [
        pltpu.with_memory_space_constraint(v, pltpu.HBM)
        for v in (strain_in, plastic_in, alpha_in, kappa, flags)
    ]
    ends, eight = shape_of(4, 32, 256), shape_of(8, 32, 256)
    square = shape_of(128, 128)
    strain, plastic, alpha, turned, z_b, z_a, yext = call(
        pack_kernel,
        "pack",
        [SM] + [HBM] * 5,
        [
            shape_of(3, 32, 32, 256), BLOCK, BLOCK, shape_of(32, 32), square, square, ends,
        ],
        scratch=[vmem(32, 32, 128), vmem(32, 8, 128), pltpu.VMEM((32, 32), jnp.int32)]
        + [vmem(128, 128)] * 6
        + [pltpu.SemaphoreType.DMA((CHUNKS + 1, 4))],
    )(where, *whole_in)
    got_a, got_b = swap(z_a, z_b, "gz")
    face_ext = to_next(yext, "gy")
    own, free, xext = call(
        inner_kernel, "inner", [VM] * 6, [BLOCK, BLOCK, ends], scratch=[vmem(32, 32, 256)]
    )(strain, plastic, alpha, kappa, turned, z_band(256))
    t = z_halo_rows()
    w = np.concatenate([plane_from_low(), plane_from_own()], axis=1)
    plane, y_a, y_b, z_both, xext = call(
        functools.partial(z_kernel, counts),
        "along_z",
        [SM] + [VM] * 9,
        [FACE, eight, eight, shape_of(128, 256), ends],
        scratch=[vmem(128, 256)] + [vmem(32, 128)] * 2 + [vmem(512, 256), vmem(2, 32, 8, 256)],
    )(where, own, xext, z_b, z_a, got_b, got_a, face_ext, t, w)
    got_a, got_b = swap(y_a, y_b, "gy")
    ext_a, ext_b = swap(xext, xext, "gx")
    own, own_face, *inverse = call(
        functools.partial(own_rows_kernel, extents),
        "own_rows",
        [SM] + [VM] * 4,
        [BLOCK, FACE, shape_of(40, 256), FACE, shape_of(40, 256), shape_of(40, 256)],
        scratch=[vmem(1024, 256), vmem(32, 32, 256)],
    )(where, own, z_both, t, rows_own)

    edges, face, plane, halo, x_a, x_b, got_ext = call(
        functools.partial(y_kernel, counts),
        "along_y",
        [SM] + [VM] * 10,
        [shape_of(16, 32, 256), FACE, FACE, shape_of(32, 16, 256), eight, eight, ends],
        scratch=[vmem(32, 256), vmem(32, 256)],
    )(where, own, own_face, plane, got_b, got_a, face_ext, ext_b, ext_a, rows_halo, plane_y_matrix())
    got_a, got_b = swap(x_a, x_b, "gx")

    shared = [
        vmem(48, 256), vmem(48, 256), vmem(4, 40, 256), vmem(4, 32, 256),
        vmem(32, 256), vmem(32, 256), vmem(32, 128),
        vmem(16, 32, 256), vmem(16, 32, 256), pltpu.SemaphoreType.DMA((2, 2)),
    ]
    force, kappa_new, part, face = call(
        middle_kernel,
        "middle",
        [SM] + [VM] * 14,
        [BLOCK, BLOCK, shape_of(18, 32, 256), FACE],
        out_specs=[HBM, HBM, VM, VM],
        scratch=[vmem(32, 32, 256)] + shared,
    )(where, strain, free, kappa, own, edges, halo, face, plane, face_ext, *inverse, rows_three)
    force, kappa_new = call(
        functools.partial(outer_kernel, counts),
        "outer",
        [SM] + [VM] * 15 + [HBM, HBM],
        [BLOCK, BLOCK],
        out_specs=[HBM, HBM],
        scratch=[vmem(7, 32, 256), vmem(6, 32, 256)] + shared,
        input_output_aliases={16: 0, 17: 1},
    )(
        where, strain, free, kappa, part, face, plane, face_ext, got_a, got_b, got_ext,
        *inverse, rows_three,
        force, kappa_new,
    )
    return (force, kappa_new)


def solution(mesh):
    in_specs = (
        P(None, "gx", "gy", "gz"),
        P("gx", "gy", "gz"),
        P("gx", "gy", "gz"),
        P("gx", "gy", "gz"),
        P("gx", "gy", "gz"),
    )
    out_specs = (P("gx", "gy", "gz"), P("gx", "gy", "gz"))
    return jax.shard_map(body, mesh=mesh, in_specs=in_specs, out_specs=out_specs, check_vma=False)
```

```python
import functools
import math

import jax
import jax.numpy as jnp
import numpy as np
from jax import lax
from jax.experimental import pallas as pl
from jax.experimental.pallas import tpu as pltpu
from jax.sharding import PartitionSpec as P

REACH = 6
RM_ITERS = 2
LENGTH_SCALE = 3.0
HIGHEST = lax.Precision.HIGHEST
F32 = jnp.float32
VMEM_LIMIT = 40 * 1024 * 1024
INTERPRET = False


def gauss(offset):
    return math.exp(-offset * offset / (2.0 * LENGTH_SCALE * LENGTH_SCALE))


def band(offset):
    return gauss(offset) if abs(offset) <= REACH else 0.0


def z_band(width):
    return np.array([[band(i - k) for k in range(width)] for i in range(width)], np.float32)


def z_halo_rows():
    out = np.zeros((256, 256), np.float32)
    for r in range(128):
        c = r % 16
        for k in range(256):
            out[r, k] = band(k - (c - 7)) if c < 7 else 0.0
            out[128 + r, k] = band(256 + c - k) if c < 6 else 0.0
    return out


def plane_from_low():
    out = np.zeros((40, 128), np.float32)
    for g in range(8):
        for c in range(7):
            out[g, 16 * g + c] = band(c - 6)
        for e in range(4):
            out[8 * (1 + e) + g, 16 * g + 7 + e] = 1.0
    return out


def plane_from_own():
    out = np.zeros((40, 128), np.float32)
    for g in range(8):
        for c in range(6):
            out[g, 16 * g + c] = band(c + 1)
    return out


def rows_matrix():
    out = np.zeros((40, 48), np.float32)
    for r in range(33):
        at = r if r < 32 else -1
        for k in range(1, 46):
            out[r, k] = band(k - 8 - at)
    return out


def plane_y_matrix():
    out = np.zeros((128, 128), np.float32)
    for y in range(-1, 32):
        for k in range(45):
            out[k, y + 1] = band(k - 7 - y)
    return out


def lanes(shape):
    return lax.broadcasted_iota(jnp.int32, shape, len(shape) - 1)


def rows(shape):
    return lax.broadcasted_iota(jnp.int32, shape, len(shape) - 2)


def inverse_total(position, extent):
    total = jnp.zeros(position.shape, F32)
    for offset in range(-REACH, REACH + 1):
        inside = (position + offset >= 0) & (position + offset < extent)
        total = total + jnp.where(inside, F32(gauss(offset)), F32(0.0))
    return 1.0 / total


def newton_plastic(trial, alpha_old):
    increment = jnp.zeros(trial.shape, F32)
    for _ in range(RM_ITERS):
        hardened = alpha_old + increment
        soft = 0.5 * jnp.exp(-5.0 * hardened)
        excess = trial - increment - (1.0 + 0.5 * hardened - soft)
        increment = jnp.maximum(increment + excess / (1.5 + 5.0 * soft), 0.0)
    return increment


def field_of(first, second, third):
    return first * first + second * second + third * third


def integrity_of(kappa):
    return jnp.exp(-jnp.maximum(kappa - 3.2, 0.0) / 3.0)


def by_parity(even, first, second, use):
    @pl.when(even)
    def _():
        use(first, second)

    @pl.when(jnp.logical_not(even))
    def _():
        use(second, first)


CONTRACT_LANES = (((1,), (1,)), ((), ()))
CHUNK = 8
CHUNKS = 4


def dot(left, right):
    return jnp.dot(left, right, precision=HIGHEST, preferred_element_type=F32)


def dot_lanes(left, right, precision=HIGHEST):
    return lax.dot_general(
        left, right, CONTRACT_LANES, precision=precision, preferred_element_type=F32
    )


def turned_flags(flags):
    eye = (rows((32, 32)) == lanes((32, 32))).astype(F32)
    return dot_lanes(eye, flags[...].astype(F32), None)


def pack_kernel(
    where_ref, strain_in, plastic_in, alpha_in, kappa_in, flags,
    strain, plastic, alpha, turned, z_b, z_a, yext,
    kappa_high, kappa_low, flags_v, up_trial, up_alpha, up_drive, low_trial, low_alpha, low_drive, sems,
):
    flags_copy = pltpu.make_async_copy(flags, flags_v, sems.at[CHUNKS, 0])
    flags_copy.start()
    copies = []
    for c in range(CHUNKS):
        part = pl.ds(c * CHUNK, CHUNK)
        pairs = [(strain_in.at[:, part], strain.at[:, part])]
        pairs += [
            (src.at[part], dst.at[part])
            for src, dst in ((plastic_in, plastic), (alpha_in, alpha))
        ]
        pairs.append((kappa_in.at[part, :, 128:256], kappa_high.at[part]))
        copies.append(
            [pltpu.make_async_copy(src, dst, sems.at[c, i]) for i, (src, dst) in enumerate(pairs)]
        )
    for group in copies:
        for copy in group:
            copy.start()
    row_copy = pltpu.make_async_copy(
        kappa_in.at[:, 24:32, 0:128], kappa_low, sems.at[CHUNKS, 1]
    )
    row_copy.start()
    flags_copy.wait()
    turned[...] = turned_flags(flags_v)
    flag = jnp.concatenate(
        [
            jnp.dot(
                turned[...],
                (rows((32, 128)) == 4 * (lanes((32, 128)) // 16) + b).astype(F32),
                preferred_element_type=F32,
            )
            for b in range(4)
        ],
        axis=0,
    )
    lane = lanes((128, 128))
    for c in range(CHUNKS):
        for copy in copies[c]:
            copy.wait()
        for g in (2 * c, 2 * c + 1):
            inside = lane // 16 == g

            def tile(ref, half):
                cells = ref[4 * g : 4 * g + 4, :, 128 * half : 128 * half + 128]
                return cells.reshape(128, 128)

            def place(ref, value, move):
                moved = pltpu.roll(value, (move + 16 * g) % 128, 1) if move + 16 * g else value
                ref[...] = jnp.where(inside, moved, ref[...])

            s0, s1, s2 = (tile(strain.at[i], 1) for i in range(3))
            place(up_trial, s0 - tile(plastic, 1), 7)
            place(up_alpha, tile(alpha, 1), 7)
            place(up_drive, field_of(s0, s1, s2), 7)
            mixed = up_drive[...]
            edge = kappa_high[4 * g : 4 * g + 4].reshape(128, 128)
            for e, value in enumerate((s1, s2, edge)):
                moved = pltpu.roll(value, (9 + e + 16 * g) % 128, 1)
                mixed = jnp.where(lane == 16 * g + 8 + e, moved, mixed)
            up_drive[...] = mixed
            s0, s1, s2 = (tile(strain.at[i], 0) for i in range(3))
            place(low_trial, s0 - tile(plastic, 0), 0)
            place(low_alpha, tile(alpha, 0), 0)
            place(low_drive, field_of(s0, s1, s2), 0)

    trial = strain[0, :, 31, :] - plastic[:, 31, :]
    flag_y = jnp.broadcast_to(flags_v[:, 31:32].astype(F32), (32, 256))
    yext[0] = trial - newton_plastic(trial, alpha[:, 31, :]) * flag_y
    yext[1] = strain[1, :, 31, :]
    yext[2] = strain[2, :, 31, :]
    row_copy.wait()
    yext[3, :, 0:128] = kappa_low[:, 7, :]
    yext[3, :, 128:256] = kappa_high[:, 31, :]

    increment = newton_plastic(up_trial[...], up_alpha[...]) * flag
    free = pltpu.roll(up_trial[...] - increment, 1, 1)
    up_drive[...] = jnp.where(
        lane % 16 < 7,
        up_drive[...] + 4.0 * increment,
        jnp.where(lane % 16 == 7, free, up_drive[...]),
    )
    increment = newton_plastic(low_trial[...], low_alpha[...]) * flag
    low_drive[...] = low_drive[...] + 4.0 * increment

    def store(upper, lower):
        upper[...] = up_drive[...]
        lower[...] = low_drive[...]

    by_parity(lax.rem(where_ref[2], 2) == 0, z_a, z_b, store)


def inner_kernel(strain, plastic, alpha, kappa, turned, bz, smooth, free, xext, field):
    @pl.loop(0, 8)
    def _(g):
        for i in range(4):
            x = 4 * g + i
            here = (rows((32, 256)) == x).astype(F32)
            flag = jnp.dot(turned[...], here, preferred_element_type=F32)
            s0 = strain[0, x]
            trial = s0 - plastic[x]
            increment = newton_plastic(trial, alpha[x]) * flag
            field[x] = field_of(s0, strain[1, x], strain[2, x]) + 4.0 * increment
            free[x] = trial - increment

    for g in range(4):
        part = field[8 * g : 8 * g + 8].reshape(256, 256)
        smooth[8 * g : 8 * g + 8] = dot(part, bz[...]).reshape(8, 32, 256)
    for e, ref in enumerate((free, strain.at[1], strain.at[2], kappa)):
        xext[e] = ref[31]


def z_kernel(
    counts, where_ref, own, xext_in, sent_b, sent_a, got_b, got_a, _, t, w,
    plane, y_a, y_b, z_both, xext, turn, head_rows, tail_rows, some, ends,
):
    xext[...] = xext_in[...]

    def choose(upper, lower):
        z_both[:, 128:256] = upper[0][...]
        z_both[:, 0:128] = lower[0][...]
        turn[:, 0:128] = lower[0][...]
        turn[:, 128:256] = lower[1][...]

    by_parity(lax.rem(where_ref[2], 2) == 0, (got_a, sent_a), (got_b, sent_b), choose)

    @pl.when(where_ref[2] == 0)
    def _():
        z_both[:, 0:128] = jnp.zeros((128, 128), F32)
        turn[:, 0:128] = jnp.zeros((128, 128), F32)

    @pl.when(where_ref[2] == counts[2] - 1)
    def _():
        z_both[:, 128:256] = jnp.zeros((128, 128), F32)

    group = lanes((8, 256)) % 128 // 16
    for half in range(2):
        for x in range(32):
            start = 32 * (x % 4) + 24 * half
            at = 256 * half + 8 * x
            some[at : at + 8, :] = jnp.where(group == x // 4, z_both[start : start + 8, :], 0.0)
    added = dot(some[...], t[...])
    for half in range(2):
        here = slice(24 * half, 24 * half + 8)
        part = added[256 * half : 256 * half + 256]
        ends[half] = own[:, here, :] + part.reshape(32, 8, 256)
    turned = dot_lanes(w[...], turn[...])
    lane = lanes((8, 128))
    for b in range(4):
        head = jnp.zeros((8, 128), F32)
        for c in range(4):
            moved = pltpu.roll(turned[8 * c : 8 * c + 8], (32 * (c - b)) % 128, 1)
            head = jnp.where(lane // 32 == c, moved, head)
        tail = jnp.where(lane < 32, pltpu.roll(turned[32:40], (-32 * b) % 128, 1), 0.0)
        head_rows[pl.ds(b, 8, stride=4), :] = head
        tail_rows[pl.ds(b, 8, stride=4), :] = tail
    plane[:, 0:128] = head_rows[...]
    plane[:, 128:256] = tail_rows[...]

    def store(upper, lower):
        for j in range(7):
            upper[j] = ends[1, :, 1 + j, :]
        upper[7] = plane[...]
        for j in range(6):
            lower[j] = ends[0, :, j, :]
        lower[6] = plane[...]
        lower[7] = plane[...]

    by_parity(lax.rem(where_ref[1], 2) == 0, y_a, y_b, store)


def own_rows_kernel(
    extents, where_ref, own, z_both, t, my,
    out, out_face, inv_x, inv_yz, inv_face, inv_plane, some, smooth,
):
    group = lanes((128, 256)) % 128 // 16
    for g in range(8):
        some[128 * g : 128 * g + 128, :] = jnp.where(group == g, z_both[...], 0.0)
    for c in range(4):
        part = dot(some[256 * c : 256 * c + 256, :], t[...])
        at = slice(8 * c, 8 * c + 8)
        smooth[at] = own[at] + part.reshape(8, 32, 256)
    for x in range(32):
        both = dot(my[...], smooth[x])
        out[x] = both[0:32]
        out_face[x : x + 1, :] = both[32:33]

    nx, ny, nz = extents
    ix, iy, iz = where_ref[0], where_ref[1], where_ref[2]
    shape, small, line = (40, 256), (32, 256), (1, 256)
    row, lane = rows(shape), lanes(shape)
    invx = inverse_total(ix * 32 + jnp.where(row < 32, row, -1), nx)
    inv_x[...] = invx
    invz = inverse_total(iz * 256 + lanes(line), nz)
    inv_yz[...] = inverse_total(iy * 32 + rows(small), ny) * invz
    at_y = inverse_total(jnp.full(line, iy * 32 - 1, jnp.int32), ny)
    inv_face[...] = invx * (at_y * invz)
    at_z = inverse_total(jnp.full(line, iz * 256 - 1, jnp.int32), nz)
    invy = inverse_total(iy * 32 - 1 + jnp.minimum(lanes(line), 32), ny)
    inv_plane[...] = invx * (invy * at_z)


def read_y_halo(counts, at, got_a, got_b, halo, parts, more):
    for j in (7, 14, 15):
        halo[:, j, :] = jnp.zeros((16, 256), F32)

    def choose(upper, lower):
        to = 0
        for first, last in parts:
            here = slice(to, to + last - first)
            for j in range(7):
                halo[here, j, :] = lower[j, first:last, :]
            for j in range(6):
                halo[here, 8 + j, :] = upper[j, first:last, :]
            to += last - first
        more(upper, lower)

    by_parity(lax.rem(at, 2) == 0, got_a, got_b, choose)

    @pl.when(at == 0)
    def _():
        halo[:, 0:8, :] = jnp.zeros((16, 8, 256), F32)

    @pl.when(at == counts[1] - 1)
    def _():
        halo[:, 8:16, :] = jnp.zeros((16, 8, 256), F32)


def y_kernel(
    counts, where_ref, own, own_face, plane, got_b, got_a, face_ext, _, __, my, v,
    edges, out_face, out_plane, x_a, x_b, halo, plane_low, plane_high,
):
    def planes(upper, lower):
        plane_low[...] = lower[7]
        plane_high[...] = upper[7]

    at = where_ref[1]
    read_y_halo(counts, at, got_a, got_b, halo, ((0, 8), (24, 32)), planes)

    @pl.when(at == 0)
    def _():
        plane_low[...] = jnp.zeros_like(plane_low)

    @pl.when(at == counts[1] - 1)
    def _():
        plane_high[...] = jnp.zeros_like(plane_high)

    out_face[8:24, :] = own_face[8:24, :]
    for i in range(16):
        x = i if i < 8 else i + 16
        both = dot(my[...], halo[i])
        edges[i, 0:8, :] = own[x, 0:8, :] + both[0:8]
        edges[i, 8:24, :] = own[x, 8:24, :]
        edges[i, 24:32, :] = own[x, 24:32, :] + both[8:16]
        out_face[x : x + 1, :] = own_face[x : x + 1, :] + both[16:17]
    mine, low, high = plane[...], plane_low[...], plane_high[...]
    lane = lanes((32, 256))
    total = jnp.zeros((32, 256), F32)
    for c in range(1, 5):
        inside = (lane > 40 * c) & (lane <= 40 * c + 32)
        total = jnp.where(inside, pltpu.roll(mine, 8 * c + 1, 1), total)
        total = jnp.where(lane == 40 * c, pltpu.roll(low, (8 * c - 31) % 256, 1), total)
    wide = jnp.where(
        lane < 7,
        pltpu.roll(low, 256 - 25, 1),
        jnp.where(lane < 39, pltpu.roll(mine, 7, 1), jnp.where(lane < 45, pltpu.roll(high, 39, 1), 0.0)),
    )
    smoothed = dot(wide[:, 0:128], v[...])
    out_plane[:, 0:128] = jnp.where(lanes((32, 128)) < 40, smoothed, total[:, 0:128])
    out_plane[:, 128:256] = total[:, 128:256]

    def store(upper, lower):
        for j in range(7):
            upper[32 * j : 32 * j + 32, :] = edges[9 + j]
        upper[224:232, :] = out_face[24:32, :]
        upper[232:240, :] = jnp.zeros((8, 256), F32)
        for e in range(4):
            corner = face_ext[e, 31:32, :]
            upper[232 + e : 233 + e, :] = jnp.where(where_ref[1] == 0, 0.0, corner)
        upper[240:248, :] = out_plane[24:32, :]
        for j in range(6):
            lower[32 * j : 32 * j + 32, :] = edges[j]
        lower[192:224, :] = jnp.zeros((32, 256), F32)
        lower[224:232, :] = out_face[0:8, :]
        lower[232:240, :] = jnp.zeros((8, 256), F32)
        lower[240:248, :] = out_plane[0:8, :]

    by_parity(lax.rem(where_ref[0], 2) == 0, x_a, x_b, store)


def fill_side(at, side, face_ext):
    for e in range(4):
        side[e, 0:32, :] = face_ext[e]
        side[e, 32:40, :] = jnp.zeros((8, 256), F32)

    @pl.when(at[1] == 0)
    def _():
        side[...] = jnp.zeros_like(side)


def faces(mx, face_all, plane_all, side, face_e, face_a, column, inv_face, inv_plane):
    shape = (40, 256)
    row, lane = rows(shape), lanes(shape)

    def previous(value):
        return jnp.where(row == 0, value[32:33, :], pltpu.roll(value, 1, 0))

    def joined(t0, t1, t2):
        a0 = previous(t0) - t0
        a1 = previous(t1) + t1
        a2 = previous(t2) + t2
        return a0 + a1, a0 - a1, a2

    kap = jnp.maximum(side[3], dot(mx[...], face_all[...]) * inv_face[...])
    integ = integrity_of(kap)
    e, _, a2 = joined(integ * side[0], integ * side[1], integ * side[2])
    face_e[...] = e[0:32]
    face_a[...] = a2[0:32]

    avg = dot(mx[...], plane_all[...])
    own = jnp.where(row == 32, plane_all[7:8, :], plane_all[8:48, :])

    def value(c):
        return pltpu.roll(own, (256 - 40 * c) % 256, 1)

    kap = jnp.maximum(value(4), avg * inv_plane[...])
    integ = integrity_of(kap)
    e, f, a2 = joined(integ * value(1), integ * value(2), integ * value(3))
    parts = e + a2 + pltpu.roll(f + a2, 255, 1)
    parts = jnp.where(lane < 32, parts, 0.0)
    eye = (rows((32, 128)) == lanes((32, 128))).astype(F32)
    pad = jnp.concatenate([parts[0:32, 0:128], jnp.zeros((96, 128), F32)], axis=0)
    column[...] = dot_lanes(eye, pad)


def layer_results(x, avg, kappa, free, strain, before, face_e, face_a, column, force_at, kappa_at):
    first_row = rows((32, 256)) == 0
    first_lane = lanes((32, 128)) == 0
    kap = jnp.maximum(kappa[x], avg)
    integ = integrity_of(kap)
    s0, s1, s2 = integ * free[x], integ * strain[1, x], integ * strain[2, x]
    if force_at is not None:
        kappa_at[...] = kap
        a0 = before[0] - s0
        a1 = before[1] + s1
        a2 = before[2] + s2
        e, f = a0 + a1, a0 - a1
        b = f + jnp.where(first_row, face_e[pl.ds(x, 1), :], pltpu.roll(e, 1, 0))
        c = a2 + jnp.where(first_row, face_a[pl.ds(x, 1), :], pltpu.roll(a2, 1, 0))
        p, q = b + c, b - c
        moved = pltpu.roll(p, 1, 1)
        edge = pltpu.roll(column[...], lax.rem(128 - x, 128), 1)
        force_at[:, 0:128] = 0.25 * (q[:, 0:128] + jnp.where(first_lane, edge, moved[:, 0:128]))
        force_at[:, 128:256] = 0.25 * (q[:, 128:256] + moved[:, 128:256])
    before[0] = s0
    before[1] = s1
    before[2] = s2


def middle_kernel(
    counts, where_ref, strain, free, kappa, own, edges, y_a, y_b, ext_a, ext_b, face, plane, face_ext,
    inv_x, inv_yz, inv_face, inv_plane, my,
    force, kappa_new, part, face_out, got_ext,
    halo, ext, face_all, plane_all, side, before, face_e, face_a, column,
    force_v, kappa_v, sems,
):
    at = (where_ref[0], where_ref[1], where_ref[2])
    read_y_halo(counts, at[1], y_a, y_b, halo, ((8, 24),), lambda upper, lower: None)

    def keep(_, lower):
        got_ext[...] = lower[...]

    by_parity(lax.rem(at[0], 2) == 0, ext_a, ext_b, keep)
    for x in range(32):
        if x < 8:
            ext[x] = edges[x]
        elif x >= 24:
            ext[x] = edges[x - 16]
        else:
            both = dot(my[0:24, 0:16], halo[x - 8])
            ext[x, 0:8, :] = own[x, 0:8, :] + both[0:8]
            ext[x, 8:24, :] = own[x, 8:24, :]
            ext[x, 24:32, :] = own[x, 24:32, :] + both[8:16]
            face_out[x : x + 1, :] = face[x : x + 1, :] + both[16:17]
    face_out[0:8, :] = face[0:8, :]
    face_out[24:32, :] = face[24:32, :]
    for ref, value in ((face_all, face_out), (plane_all, plane)):
        ref[0:8, :] = jnp.zeros((8, 256), F32)
        ref[8:40, :] = value[...]
        ref[40:48, :] = jnp.zeros((8, 256), F32)
    fill_side(at, side, face_ext)
    faces(
        my.at[:, 48:96], face_all, plane_all, side, face_e, face_a, column, inv_face, inv_plane
    )

    def layer(x):
        total = gauss(0) * ext[x]
        for a in range(1, REACH + 1):
            total = total + gauss(a) * (ext[x - a] + ext[x + a])
        return total * (inv_x[pl.ds(x, 1), :] * inv_yz[...])

    layer_results(7, layer(7), kappa, free, strain, before, None, None, None, None, None)
    copies = []
    for c in (1, 2):

        @pl.loop(0, CHUNK)
        def _(i):
            x = c * CHUNK + i
            layer_results(
                x, layer(x), kappa, free, strain, before, face_e, face_a, column,
                force_v.at[x - CHUNK], kappa_v.at[x - CHUNK],
            )

        here = pl.ds((c - 1) * CHUNK, CHUNK)
        there = pl.ds(c * CHUNK, CHUNK)
        for k, (src, dst) in enumerate(((force_v, force), (kappa_v, kappa_new))):
            copy = pltpu.make_async_copy(src.at[here], dst.at[there], sems.at[c - 1, k])
            copy.start()
            copies.append(copy)
    for i in range(18):
        x = i - 1 if i < 9 else i + 14
        total = None
        for a in range(-REACH, REACH + 1):
            if 0 <= x + a < 32:
                term = gauss(a) * ext[x + a]
                total = term if total is None else total + term
        part[i] = total
    for copy in copies:
        copy.wait()


def outer_kernel(
    counts, where_ref, strain, free, kappa, part, face, plane, face_ext, got_a, got_b, got_ext,
    inv_x, inv_yz, inv_face, inv_plane, my,
    force_in, kappa_in,
    force, kappa_new,
    low, high, face_all, plane_all, side, before, face_e, face_a, column,
    force_v, kappa_v, sems,
):
    at = (where_ref[0], where_ref[1], where_ref[2])

    def choose(upper, lower):
        for j in range(7):
            low[j] = lower[32 * j : 32 * j + 32, :]
        for j in range(6):
            high[j] = upper[32 * j : 32 * j + 32, :]
        face_all[0:8, :] = lower[224:232, :]
        face_all[40:48, :] = upper[224:232, :]
        plane_all[0:8, :] = lower[240:248, :]
        plane_all[40:48, :] = upper[240:248, :]
        for e in range(4):
            side[e, 32:33, :] = lower[232 + e : 233 + e, :]

    fill_side(at, side, face_ext)
    by_parity(lax.rem(at[0], 2) == 0, got_a, got_b, choose)
    before[...] = got_ext[...]

    @pl.when(at[0] == 0)
    def _():
        low[...] = jnp.zeros_like(low)
        before[...] = jnp.zeros_like(before)
        face_all[0:8, :] = jnp.zeros((8, 256), F32)
        plane_all[0:8, :] = jnp.zeros((8, 256), F32)
        for e in range(4):
            side[e, 32:33, :] = jnp.zeros((1, 256), F32)

    @pl.when(at[0] == counts[0] - 1)
    def _():
        high[...] = jnp.zeros_like(high)
        face_all[40:48, :] = jnp.zeros((8, 256), F32)
        plane_all[40:48, :] = jnp.zeros((8, 256), F32)

    face_all[8:40, :] = face[...]
    plane_all[8:40, :] = plane[...]
    faces(
        my.at[:, 48:96], face_all, plane_all, side, face_e, face_a, column, inv_face, inv_plane
    )

    def layer(x):
        total = part[x + 1 if x < 8 else x - 14]
        for a in range(-REACH, REACH + 1):
            if x + a < 0:
                total = total + gauss(a) * low[x + a + 7]
            elif x + a >= 32:
                total = total + gauss(a) * high[x + a - 32]
        return total * (inv_x[x % 33 : x % 33 + 1, :] * inv_yz[...])

    kap = jnp.maximum(before[3], layer(-1))
    integ = integrity_of(kap)
    for e in range(3):
        before[e] = integ * before[e]
    copies = []
    for c in (0, 3):
        if c == 3:
            layer_results(23, layer(23), kappa, free, strain, before, None, None, None, None, None)
        for i in range(CHUNK):
            x = c * CHUNK + i
            slot = i if c == 0 else CHUNK + i
            layer_results(
                x, layer(x), kappa, free, strain, before, face_e, face_a, column,
                force_v.at[slot], kappa_v.at[slot],
            )
        here = pl.ds(0 if c == 0 else CHUNK, CHUNK)
        there = pl.ds(c * CHUNK, CHUNK)
        for k, (src, dst) in enumerate(((force_v, force), (kappa_v, kappa_new))):
            copy = pltpu.make_async_copy(src.at[here], dst.at[there], sems.at[c // 3, k])
            copy.start()
            copies.append(copy)
    for copy in copies:
        copy.wait()


AXES = ("gx", "gy", "gz")


def swap(first, second, axis):
    sizes = [lax.axis_size(a) for a in AXES]
    at = AXES.index(axis)
    other = 0 if at == 1 else 1

    def route(start):
        out = []
        for place in np.ndindex(*sizes):
            there = list(place)
            if place[at] >= start and place[at] - start < (sizes[at] - start) // 2 * 2:
                there[at] += 1 if (place[at] - start) % 2 == 0 else -1
            else:
                there[other] ^= 1
            out.append(tuple(int(np.ravel_multi_index(p, sizes)) for p in (place, tuple(there))))
        return out

    return lax.ppermute(first, AXES, route(0)), lax.ppermute(second, AXES, route(1))


def to_next(block, axis):
    count = lax.axis_size(axis)
    return lax.ppermute(block, axis, [(i, (i + 1) % count) for i in range(count)])


def shape_of(*dims):
    return jax.ShapeDtypeStruct(dims, F32)


VM = pl.BlockSpec(memory_space=pltpu.VMEM)
SM = pl.BlockSpec(memory_space=pltpu.SMEM)
HBM = pl.BlockSpec(memory_space=pltpu.HBM)
BLOCK = shape_of(32, 32, 256)
FACE = shape_of(32, 256)


def vmem(*dims):
    return pltpu.VMEM(dims, F32)


def call(kernel, name, in_specs, out_shape, out_specs=None, scratch=(), **kwargs):
    return pl.pallas_call(
        kernel,
        name=name,
        in_specs=in_specs,
        out_specs=out_specs or [VM] * len(out_shape),
        out_shape=out_shape,
        scratch_shapes=list(scratch),
        interpret=INTERPRET,
        compiler_params=pltpu.CompilerParams(vmem_limit_bytes=VMEM_LIMIT),
        **kwargs,
    )


def body(strain_in, plastic_in, alpha_in, kappa, flags):
    where = jnp.stack([lax.axis_index(a) for a in AXES]).astype(jnp.int32)
    flags = flags.reshape(32, 32)
    counts = tuple(lax.axis_size(a) for a in AXES)
    extents = (32 * counts[0], 32 * counts[1], 256 * counts[2])
    rows_all = rows_matrix()
    rows_own = np.ascontiguousarray(rows_all[:, 8:40])
    rows_halo = np.concatenate(
        [rows_all[:, 1:8], np.zeros((40, 1), np.float32), rows_all[:, 40:48]], axis=1
    )
    rows_halo = np.concatenate([rows_halo[0:8], rows_halo[24:40]], axis=0)
    rows_three = np.zeros((40, 128), np.float32)
    rows_three[0:24, 0:16] = rows_halo
    rows_three[:, 48:96] = rows_all

    whole_in = [
        pltpu.with_memory_space_constraint(v, pltpu.HBM)
        for v in (strain_in, plastic_in, alpha_in, kappa, flags)
    ]
    ends, eight = shape_of(4, 32, 256), shape_of(8, 32, 256)
    square = shape_of(128, 128)
    strain, plastic, alpha, turned, z_b, z_a, yext = call(
        pack_kernel,
        "pack",
        [SM] + [HBM] * 5,
        [
            shape_of(3, 32, 32, 256), BLOCK, BLOCK, shape_of(32, 32), square, square, ends,
        ],
        scratch=[vmem(32, 32, 128), vmem(32, 8, 128), pltpu.VMEM((32, 32), jnp.int32)]
        + [vmem(128, 128)] * 6
        + [pltpu.SemaphoreType.DMA((CHUNKS + 1, 4))],
    )(where, *whole_in)
    got_a, got_b = swap(z_a, z_b, "gz")
    face_ext = to_next(yext, "gy")
    own, free, xext = call(
        inner_kernel, "inner", [VM] * 6, [BLOCK, BLOCK, ends], scratch=[vmem(32, 32, 256)]
    )(strain, plastic, alpha, kappa, turned, z_band(256))
    t = z_halo_rows()
    w = np.concatenate([plane_from_low(), plane_from_own()], axis=1)
    plane, y_a, y_b, z_both, xext = call(
        functools.partial(z_kernel, counts),
        "along_z",
        [SM] + [VM] * 9,
        [FACE, eight, eight, shape_of(128, 256), ends],
        scratch=[vmem(128, 256)] + [vmem(32, 128)] * 2 + [vmem(512, 256), vmem(2, 32, 8, 256)],
    )(where, own, xext, z_b, z_a, got_b, got_a, face_ext, t, w)
    y_got_a, y_got_b = swap(y_a, y_b, "gy")
    ext_a, ext_b = swap(xext, xext, "gx")
    own, own_face, *inverse = call(
        functools.partial(own_rows_kernel, extents),
        "own_rows",
        [SM] + [VM] * 4,
        [BLOCK, FACE, shape_of(40, 256), FACE, shape_of(40, 256), shape_of(40, 256)],
        scratch=[vmem(1024, 256), vmem(32, 32, 256)],
    )(where, own, z_both, t, rows_own)

    edges, face, plane, x_a, x_b = call(
        functools.partial(y_kernel, counts),
        "along_y",
        [SM] + [VM] * 10,
        [shape_of(16, 32, 256), FACE, FACE] + [shape_of(248, 256)] * 2,
        scratch=[vmem(16, 16, 256), vmem(32, 256), vmem(32, 256)],
    )(where, own, own_face, plane, y_got_b, y_got_a, face_ext, ext_b, ext_a, rows_halo, plane_y_matrix())
    got_a, got_b = swap(x_a, x_b, "gx")

    shared = [
        vmem(48, 256), vmem(48, 256), vmem(4, 40, 256), vmem(4, 32, 256),
        vmem(32, 256), vmem(32, 256), vmem(32, 128),
        vmem(16, 32, 256), vmem(16, 32, 256), pltpu.SemaphoreType.DMA((2, 2)),
    ]
    force, kappa_new, part, face, got_ext = call(
        functools.partial(middle_kernel, counts),
        "middle",
        [SM] + [VM] * 17,
        [BLOCK, BLOCK, shape_of(18, 32, 256), FACE, ends],
        out_specs=[HBM, HBM, VM, VM, VM],
        scratch=[vmem(16, 16, 256), vmem(32, 32, 256)] + shared,
    )(where, strain, free, kappa, own, edges, y_got_a, y_got_b, ext_a, ext_b, face, plane, face_ext,
      *inverse, rows_three)
    force, kappa_new = call(
        functools.partial(outer_kernel, counts),
        "outer",
        [SM] + [VM] * 15 + [HBM, HBM],
        [BLOCK, BLOCK],
        out_specs=[HBM, HBM],
        scratch=[vmem(7, 32, 256), vmem(6, 32, 256)] + shared,
        input_output_aliases={16: 0, 17: 1},
    )(
        where, strain, free, kappa, part, face, plane, face_ext, got_a, got_b, got_ext,
        *inverse, rows_three,
        force, kappa_new,
    )
    return (force, kappa_new)


def solution(mesh):
    in_specs = (
        P(None, "gx", "gy", "gz"),
        P("gx", "gy", "gz"),
        P("gx", "gy", "gz"),
        P("gx", "gy", "gz"),
        P("gx", "gy", "gz"),
    )
    out_specs = (P("gx", "gy", "gz"), P("gx", "gy", "gz"))
    return jax.shard_map(body, mesh=mesh, in_specs=in_specs, out_specs=out_specs, check_vma=False)
```

```python
import functools
import math

import jax
import jax.numpy as jnp
import numpy as np
from jax import lax
from jax.experimental import pallas as pl
from jax.experimental.pallas import tpu as pltpu
from jax.sharding import PartitionSpec as P

REACH = 6
RM_ITERS = 2
LENGTH_SCALE = 3.0
HIGHEST = lax.Precision.HIGHEST
F32 = jnp.float32
VMEM_LIMIT = 40 * 1024 * 1024
INTERPRET = False


def gauss(offset):
    return math.exp(-offset * offset / (2.0 * LENGTH_SCALE * LENGTH_SCALE))


def band(offset):
    return gauss(offset) if abs(offset) <= REACH else 0.0


def z_band(width):
    return np.array([[band(i - k) for k in range(width)] for i in range(width)], np.float32)


def z_halo_rows():
    out = np.zeros((256, 256), np.float32)
    for r in range(128):
        c = r % 16
        for k in range(256):
            out[r, k] = band(k - (c - 7)) if c < 7 else 0.0
            out[128 + r, k] = band(256 + c - k) if c < 6 else 0.0
    return out


def plane_from_low():
    out = np.zeros((40, 128), np.float32)
    for g in range(8):
        for c in range(7):
            out[g, 16 * g + c] = band(c - 6)
        for e in range(4):
            out[8 * (1 + e) + g, 16 * g + 7 + e] = 1.0
    return out


def plane_from_own():
    out = np.zeros((40, 128), np.float32)
    for g in range(8):
        for c in range(6):
            out[g, 16 * g + c] = band(c + 1)
    return out


def rows_matrix():
    out = np.zeros((40, 48), np.float32)
    for r in range(33):
        at = r if r < 32 else -1
        for k in range(1, 46):
            out[r, k] = band(k - 8 - at)
    return out


def plane_y_matrix():
    out = np.zeros((128, 128), np.float32)
    for y in range(-1, 32):
        for k in range(45):
            out[k, y + 1] = band(k - 7 - y)
    return out


def lanes(shape):
    return lax.broadcasted_iota(jnp.int32, shape, len(shape) - 1)


def rows(shape):
    return lax.broadcasted_iota(jnp.int32, shape, len(shape) - 2)


def inverse_total(position, extent):
    total = jnp.zeros(position.shape, F32)
    for offset in range(-REACH, REACH + 1):
        inside = (position + offset >= 0) & (position + offset < extent)
        total = total + jnp.where(inside, F32(gauss(offset)), F32(0.0))
    return 1.0 / total


def newton_plastic(trial, alpha_old):
    increment = jnp.zeros(trial.shape, F32)
    for _ in range(RM_ITERS):
        hardened = alpha_old + increment
        soft = 0.5 * jnp.exp(-5.0 * hardened)
        excess = trial - increment - (1.0 + 0.5 * hardened - soft)
        increment = jnp.maximum(increment + excess / (1.5 + 5.0 * soft), 0.0)
    return increment


def field_of(first, second, third):
    return first * first + second * second + third * third


def integrity_of(kappa):
    return jnp.exp(jnp.maximum(kappa - 3.2, 0.0) * (-1.0 / 3.0))


def by_parity(even, first, second, use):
    @pl.when(even)
    def _():
        use(first, second)

    @pl.when(jnp.logical_not(even))
    def _():
        use(second, first)


CONTRACT_LANES = (((1,), (1,)), ((), ()))
CHUNK = 8
CHUNKS = 4


def dot(left, right):
    return jnp.dot(left, right, precision=HIGHEST, preferred_element_type=F32)


def dot_lanes(left, right, precision=HIGHEST):
    return lax.dot_general(
        left, right, CONTRACT_LANES, precision=precision, preferred_element_type=F32
    )


def turned_flags(flags):
    eye = (rows((32, 32)) == lanes((32, 32))).astype(F32)
    return dot_lanes(eye, flags[...].astype(F32), None)


def pack_kernel(
    where_ref, strain_in, plastic_in, alpha_in, kappa_in, flags,
    strain, plastic, alpha, turned, z_b, z_a, yext,
    kappa_high, kappa_low, flags_v, up_trial, up_alpha, up_drive, low_trial, low_alpha, low_drive, sems,
):
    flags_copy = pltpu.make_async_copy(flags, flags_v, sems.at[CHUNKS, 0])
    flags_copy.start()
    copies = []
    for c in range(CHUNKS):
        part = pl.ds(c * CHUNK, CHUNK)
        pairs = [(strain_in.at[:, part], strain.at[:, part])]
        pairs += [
            (src.at[part], dst.at[part])
            for src, dst in ((plastic_in, plastic), (alpha_in, alpha))
        ]
        pairs.append((kappa_in.at[part, :, 128:256], kappa_high.at[part]))
        copies.append(
            [pltpu.make_async_copy(src, dst, sems.at[c, i]) for i, (src, dst) in enumerate(pairs)]
        )
    for group in copies:
        for copy in group:
            copy.start()
    row_copy = pltpu.make_async_copy(
        kappa_in.at[:, 24:32, 0:128], kappa_low, sems.at[CHUNKS, 1]
    )
    row_copy.start()
    flags_copy.wait()
    turned[...] = turned_flags(flags_v)
    flag = jnp.concatenate(
        [
            jnp.dot(
                turned[...],
                (rows((32, 128)) == 4 * (lanes((32, 128)) // 16) + b).astype(F32),
                preferred_element_type=F32,
            )
            for b in range(4)
        ],
        axis=0,
    )
    lane = lanes((128, 128))
    for c in range(CHUNKS):
        for copy in copies[c]:
            copy.wait()
        for g in (2 * c, 2 * c + 1):
            inside = lane // 16 == g

            def tile(ref, half):
                cells = ref[4 * g : 4 * g + 4, :, 128 * half : 128 * half + 128]
                return cells.reshape(128, 128)

            def place(ref, value, move):
                moved = pltpu.roll(value, (move + 16 * g) % 128, 1) if move + 16 * g else value
                ref[...] = jnp.where(inside, moved, ref[...])

            s0, s1, s2 = (tile(strain.at[i], 1) for i in range(3))
            place(up_trial, s0 - tile(plastic, 1), 7)
            place(up_alpha, tile(alpha, 1), 7)
            place(up_drive, field_of(s0, s1, s2), 7)
            mixed = up_drive[...]
            edge = kappa_high[4 * g : 4 * g + 4].reshape(128, 128)
            for e, value in enumerate((s1, s2, edge)):
                moved = pltpu.roll(value, (9 + e + 16 * g) % 128, 1)
                mixed = jnp.where(lane == 16 * g + 8 + e, moved, mixed)
            up_drive[...] = mixed
            s0, s1, s2 = (tile(strain.at[i], 0) for i in range(3))
            place(low_trial, s0 - tile(plastic, 0), 0)
            place(low_alpha, tile(alpha, 0), 0)
            place(low_drive, field_of(s0, s1, s2), 0)

    trial = strain[0, :, 31, :] - plastic[:, 31, :]
    flag_y = jnp.broadcast_to(flags_v[:, 31:32].astype(F32), (32, 256))
    yext[0] = trial - newton_plastic(trial, alpha[:, 31, :]) * flag_y
    yext[1] = strain[1, :, 31, :]
    yext[2] = strain[2, :, 31, :]
    row_copy.wait()
    yext[3, :, 0:128] = kappa_low[:, 7, :]
    yext[3, :, 128:256] = kappa_high[:, 31, :]

    increment = newton_plastic(up_trial[...], up_alpha[...]) * flag
    free = pltpu.roll(up_trial[...] - increment, 1, 1)
    up_drive[...] = jnp.where(
        lane % 16 < 7,
        up_drive[...] + 4.0 * increment,
        jnp.where(lane % 16 == 7, free, up_drive[...]),
    )
    increment = newton_plastic(low_trial[...], low_alpha[...]) * flag
    low_drive[...] = low_drive[...] + 4.0 * increment

    def store(upper, lower):
        upper[...] = up_drive[...]
        lower[...] = low_drive[...]

    by_parity(lax.rem(where_ref[2], 2) == 0, z_a, z_b, store)


def inner_kernel(strain, plastic, alpha, kappa, turned, bz, smooth, free, xext, field):
    @pl.loop(0, 8)
    def _(g):
        for i in range(4):
            x = 4 * g + i
            here = (rows((32, 256)) == x).astype(F32)
            flag = jnp.dot(turned[...], here, preferred_element_type=F32)
            s0 = strain[0, x]
            trial = s0 - plastic[x]
            increment = newton_plastic(trial, alpha[x]) * flag
            field[x] = field_of(s0, strain[1, x], strain[2, x]) + 4.0 * increment
            free[x] = trial - increment

    for g in range(4):
        part = field[8 * g : 8 * g + 8].reshape(256, 256)
        smooth[8 * g : 8 * g + 8] = dot(part, bz[...]).reshape(8, 32, 256)
    for e, ref in enumerate((free, strain.at[1], strain.at[2], kappa)):
        xext[e] = ref[31]


def z_kernel(
    counts, where_ref, own, xext_in, sent_b, sent_a, got_b, got_a, _, t, w,
    plane, y_a, y_b, z_both, xext, turn, head_rows, tail_rows, some, ends,
):
    xext[...] = xext_in[...]

    def choose(upper, lower):
        z_both[:, 128:256] = upper[0][...]
        z_both[:, 0:128] = lower[0][...]
        turn[:, 0:128] = lower[0][...]
        turn[:, 128:256] = lower[1][...]

    by_parity(lax.rem(where_ref[2], 2) == 0, (got_a, sent_a), (got_b, sent_b), choose)

    @pl.when(where_ref[2] == 0)
    def _():
        z_both[:, 0:128] = jnp.zeros((128, 128), F32)
        turn[:, 0:128] = jnp.zeros((128, 128), F32)

    @pl.when(where_ref[2] == counts[2] - 1)
    def _():
        z_both[:, 128:256] = jnp.zeros((128, 128), F32)

    group = lanes((8, 256)) % 128 // 16
    for half in range(2):
        for x in range(32):
            start = 32 * (x % 4) + 24 * half
            at = 256 * half + 8 * x
            some[at : at + 8, :] = jnp.where(group == x // 4, z_both[start : start + 8, :], 0.0)
    added = dot(some[...], t[...])
    for half in range(2):
        here = slice(24 * half, 24 * half + 8)
        part = added[256 * half : 256 * half + 256]
        ends[half] = own[:, here, :] + part.reshape(32, 8, 256)
    turned = dot_lanes(w[...], turn[...])
    lane = lanes((8, 128))
    for b in range(4):
        head = jnp.zeros((8, 128), F32)
        for c in range(4):
            moved = pltpu.roll(turned[8 * c : 8 * c + 8], (32 * (c - b)) % 128, 1)
            head = jnp.where(lane // 32 == c, moved, head)
        tail = jnp.where(lane < 32, pltpu.roll(turned[32:40], (-32 * b) % 128, 1), 0.0)
        head_rows[pl.ds(b, 8, stride=4), :] = head
        tail_rows[pl.ds(b, 8, stride=4), :] = tail
    plane[:, 0:128] = head_rows[...]
    plane[:, 128:256] = tail_rows[...]

    def store(upper, lower):
        for j in range(7):
            upper[j] = ends[1, :, 1 + j, :]
        upper[7] = plane[...]
        for j in range(6):
            lower[j] = ends[0, :, j, :]
        lower[6] = plane[...]
        lower[7] = plane[...]

    by_parity(lax.rem(where_ref[1], 2) == 0, y_a, y_b, store)


def own_rows_kernel(
    extents, where_ref, own, z_both, t, my,
    out, out_face, inv_x, inv_yz, inv_face, inv_plane, some, smooth,
):
    group = lanes((128, 256)) % 128 // 16
    for g in range(8):
        some[128 * g : 128 * g + 128, :] = jnp.where(group == g, z_both[...], 0.0)
    for c in range(4):
        part = dot(some[256 * c : 256 * c + 256, :], t[...])
        at = slice(8 * c, 8 * c + 8)
        smooth[at] = own[at] + part.reshape(8, 32, 256)
    for x in range(32):
        both = dot(my[...], smooth[x])
        out[x] = both[0:32]
        out_face[x : x + 1, :] = both[32:33]

    nx, ny, nz = extents
    ix, iy, iz = where_ref[0], where_ref[1], where_ref[2]
    shape, small, line = (40, 256), (32, 256), (1, 256)
    row, lane = rows(shape), lanes(shape)
    invx = inverse_total(ix * 32 + jnp.where(row < 32, row, -1), nx)
    inv_x[...] = invx
    invz = inverse_total(iz * 256 + lanes(line), nz)
    inv_yz[...] = inverse_total(iy * 32 + rows(small), ny) * invz
    at_y = inverse_total(jnp.full(line, iy * 32 - 1, jnp.int32), ny)
    inv_face[...] = invx * (at_y * invz)
    at_z = inverse_total(jnp.full(line, iz * 256 - 1, jnp.int32), nz)
    invy = inverse_total(iy * 32 - 1 + jnp.minimum(lanes(line), 32), ny)
    inv_plane[...] = invx * (invy * at_z)


def read_y_halo(counts, at, got_a, got_b, halo, parts, more):
    for j in (7, 14, 15):
        halo[:, j, :] = jnp.zeros((16, 256), F32)

    def choose(upper, lower):
        to = 0
        for first, last in parts:
            here = slice(to, to + last - first)
            for j in range(7):
                halo[here, j, :] = lower[j, first:last, :]
            for j in range(6):
                halo[here, 8 + j, :] = upper[j, first:last, :]
            to += last - first
        more(upper, lower)

    by_parity(lax.rem(at, 2) == 0, got_a, got_b, choose)

    @pl.when(at == 0)
    def _():
        halo[:, 0:8, :] = jnp.zeros((16, 8, 256), F32)

    @pl.when(at == counts[1] - 1)
    def _():
        halo[:, 8:16, :] = jnp.zeros((16, 8, 256), F32)


def y_kernel(
    counts, where_ref, own, own_face, plane, got_b, got_a, face_ext, _, __, my, v,
    edges, out_face, out_plane, x_a, x_b, halo, plane_low, plane_high,
):
    def planes(upper, lower):
        plane_low[...] = lower[7]
        plane_high[...] = upper[7]

    at = where_ref[1]
    read_y_halo(counts, at, got_a, got_b, halo, ((0, 8), (24, 32)), planes)

    @pl.when(at == 0)
    def _():
        plane_low[...] = jnp.zeros_like(plane_low)

    @pl.when(at == counts[1] - 1)
    def _():
        plane_high[...] = jnp.zeros_like(plane_high)

    out_face[8:24, :] = own_face[8:24, :]
    for i in range(16):
        x = i if i < 8 else i + 16
        both = dot(my[...], halo[i])
        edges[i, 0:8, :] = own[x, 0:8, :] + both[0:8]
        edges[i, 8:24, :] = own[x, 8:24, :]
        edges[i, 24:32, :] = own[x, 24:32, :] + both[8:16]
        out_face[x : x + 1, :] = own_face[x : x + 1, :] + both[16:17]
    mine, low, high = plane[...], plane_low[...], plane_high[...]
    lane = lanes((32, 256))
    total = jnp.zeros((32, 256), F32)
    for c in range(1, 5):
        inside = (lane > 40 * c) & (lane <= 40 * c + 32)
        total = jnp.where(inside, pltpu.roll(mine, 8 * c + 1, 1), total)
        total = jnp.where(lane == 40 * c, pltpu.roll(low, (8 * c - 31) % 256, 1), total)
    wide = jnp.where(
        lane < 7,
        pltpu.roll(low, 256 - 25, 1),
        jnp.where(lane < 39, pltpu.roll(mine, 7, 1), jnp.where(lane < 45, pltpu.roll(high, 39, 1), 0.0)),
    )
    smoothed = dot(wide[:, 0:128], v[...])
    out_plane[:, 0:128] = jnp.where(lanes((32, 128)) < 40, smoothed, total[:, 0:128])
    out_plane[:, 128:256] = total[:, 128:256]

    def store(upper, lower):
        for j in range(7):
            upper[32 * j : 32 * j + 32, :] = edges[9 + j]
        upper[224:232, :] = out_face[24:32, :]
        upper[232:240, :] = jnp.zeros((8, 256), F32)
        for e in range(4):
            corner = face_ext[e, 31:32, :]
            upper[232 + e : 233 + e, :] = jnp.where(where_ref[1] == 0, 0.0, corner)
        upper[240:248, :] = out_plane[24:32, :]
        for j in range(6):
            lower[32 * j : 32 * j + 32, :] = edges[j]
        lower[192:224, :] = jnp.zeros((32, 256), F32)
        lower[224:232, :] = out_face[0:8, :]
        lower[232:240, :] = jnp.zeros((8, 256), F32)
        lower[240:248, :] = out_plane[0:8, :]

    by_parity(lax.rem(where_ref[0], 2) == 0, x_a, x_b, store)


def fill_side(at, side, face_ext):
    for e in range(4):
        side[e, 0:32, :] = face_ext[e]
        side[e, 32:40, :] = jnp.zeros((8, 256), F32)

    @pl.when(at[1] == 0)
    def _():
        side[...] = jnp.zeros_like(side)


def faces(mx, face_all, plane_all, side, face_e, face_a, column, inv_face, inv_plane):
    shape = (40, 256)
    row, lane = rows(shape), lanes(shape)

    def previous(value):
        return jnp.where(row == 0, value[32:33, :], pltpu.roll(value, 1, 0))

    def joined(t0, t1, t2):
        a0 = previous(t0) - t0
        a1 = previous(t1) + t1
        a2 = previous(t2) + t2
        return a0 + a1, a0 - a1, a2

    kap = jnp.maximum(side[3], dot(mx[...], face_all[...]) * inv_face[...])
    integ = integrity_of(kap)
    e, _, a2 = joined(integ * side[0], integ * side[1], integ * side[2])
    face_e[...] = e[0:32]
    face_a[...] = a2[0:32]

    avg = dot(mx[...], plane_all[...])
    own = jnp.where(row == 32, plane_all[7:8, :], plane_all[8:48, :])

    def value(c):
        return pltpu.roll(own, (256 - 40 * c) % 256, 1)

    kap = jnp.maximum(value(4), avg * inv_plane[...])
    integ = integrity_of(kap)
    e, f, a2 = joined(integ * value(1), integ * value(2), integ * value(3))
    parts = e + a2 + pltpu.roll(f + a2, 255, 1)
    parts = jnp.where(lane < 32, parts, 0.0)
    eye = (rows((32, 128)) == lanes((32, 128))).astype(F32)
    pad = jnp.concatenate([parts[0:32, 0:128], jnp.zeros((96, 128), F32)], axis=0)
    column[...] = dot_lanes(eye, pad)


def layer_results(x, avg, kappa, free, strain, before, face_e, face_a, column, force_at, kappa_at):
    first_row = rows((32, 256)) == 0
    first_lane = lanes((32, 128)) == 0
    kap = jnp.maximum(kappa[x], avg)
    integ = integrity_of(kap)
    s0, s1, s2 = integ * free[x], integ * strain[1, x], integ * strain[2, x]
    if force_at is not None:
        kappa_at[...] = kap
        a0 = before[0] - s0
        a1 = before[1] + s1
        a2 = before[2] + s2
        e, f = a0 + a1, a0 - a1
        b = f + jnp.where(first_row, face_e[pl.ds(x, 1), :], pltpu.roll(e, 1, 0))
        c = a2 + jnp.where(first_row, face_a[pl.ds(x, 1), :], pltpu.roll(a2, 1, 0))
        p, q = b + c, b - c
        moved = pltpu.roll(p, 1, 1)
        edge = pltpu.roll(column[...], lax.rem(128 - x, 128), 1)
        force_at[:, 0:128] = 0.25 * (q[:, 0:128] + jnp.where(first_lane, edge, moved[:, 0:128]))
        force_at[:, 128:256] = 0.25 * (q[:, 128:256] + moved[:, 128:256])
    before[0] = s0
    before[1] = s1
    before[2] = s2


def middle_kernel(
    counts, where_ref, strain, free, kappa, own, edges, y_a, y_b, ext_a, ext_b, face, plane, face_ext,
    inv_x, inv_yz, inv_face, inv_plane, my,
    force, kappa_new, part, face_out, got_ext,
    halo, ext, face_all, plane_all, side, before, face_e, face_a, column,
    force_v, kappa_v, sems,
):
    at = (where_ref[0], where_ref[1], where_ref[2])
    read_y_halo(counts, at[1], y_a, y_b, halo, ((8, 24),), lambda upper, lower: None)

    def keep(_, lower):
        got_ext[...] = lower[...]

    by_parity(lax.rem(at[0], 2) == 0, ext_a, ext_b, keep)
    for x in range(32):
        if x < 8:
            ext[x] = edges[x]
        elif x >= 24:
            ext[x] = edges[x - 16]
        else:
            both = dot(my[0:24, 0:16], halo[x - 8])
            ext[x, 0:8, :] = own[x, 0:8, :] + both[0:8]
            ext[x, 8:24, :] = own[x, 8:24, :]
            ext[x, 24:32, :] = own[x, 24:32, :] + both[8:16]
            face_out[x : x + 1, :] = face[x : x + 1, :] + both[16:17]
    face_out[0:8, :] = face[0:8, :]
    face_out[24:32, :] = face[24:32, :]
    for ref, value in ((face_all, face_out), (plane_all, plane)):
        ref[0:8, :] = jnp.zeros((8, 256), F32)
        ref[8:40, :] = value[...]
        ref[40:48, :] = jnp.zeros((8, 256), F32)
    fill_side(at, side, face_ext)
    faces(
        my.at[:, 48:96], face_all, plane_all, side, face_e, face_a, column, inv_face, inv_plane
    )

    def layer(x):
        total = gauss(0) * ext[x]
        for a in range(1, REACH + 1):
            total = total + gauss(a) * (ext[x - a] + ext[x + a])
        return total * (inv_x[pl.ds(x, 1), :] * inv_yz[...])

    layer_results(7, layer(7), kappa, free, strain, before, None, None, None, None, None)
    copies = []
    for c in (1, 2):

        @pl.loop(0, CHUNK)
        def _(i):
            x = c * CHUNK + i
            layer_results(
                x, layer(x), kappa, free, strain, before, face_e, face_a, column,
                force_v.at[x - CHUNK], kappa_v.at[x - CHUNK],
            )

        here = pl.ds((c - 1) * CHUNK, CHUNK)
        there = pl.ds(c * CHUNK, CHUNK)
        for k, (src, dst) in enumerate(((force_v, force), (kappa_v, kappa_new))):
            copy = pltpu.make_async_copy(src.at[here], dst.at[there], sems.at[c - 1, k])
            copy.start()
            copies.append(copy)
    for i in range(18):
        x = i - 1 if i < 9 else i + 14
        total = None
        for a in range(-REACH, REACH + 1):
            if 0 <= x + a < 32:
                term = gauss(a) * ext[x + a]
                total = term if total is None else total + term
        part[i] = total
    for copy in copies:
        copy.wait()


def outer_kernel(
    counts, where_ref, strain, free, kappa, part, face, plane, face_ext, got_a, got_b, got_ext,
    inv_x, inv_yz, inv_face, inv_plane, my,
    force_in, kappa_in,
    force, kappa_new,
    low, high, face_all, plane_all, side, before, face_e, face_a, column,
    force_v, kappa_v, sems,
):
    at = (where_ref[0], where_ref[1], where_ref[2])

    def choose(upper, lower):
        for j in range(7):
            low[j] = lower[32 * j : 32 * j + 32, :]
        for j in range(6):
            high[j] = upper[32 * j : 32 * j + 32, :]
        face_all[0:8, :] = lower[224:232, :]
        face_all[40:48, :] = upper[224:232, :]
        plane_all[0:8, :] = lower[240:248, :]
        plane_all[40:48, :] = upper[240:248, :]
        for e in range(4):
            side[e, 32:33, :] = lower[232 + e : 233 + e, :]

    fill_side(at, side, face_ext)
    by_parity(lax.rem(at[0], 2) == 0, got_a, got_b, choose)
    before[...] = got_ext[...]

    @pl.when(at[0] == 0)
    def _():
        low[...] = jnp.zeros_like(low)
        before[...] = jnp.zeros_like(before)
        face_all[0:8, :] = jnp.zeros((8, 256), F32)
        plane_all[0:8, :] = jnp.zeros((8, 256), F32)
        for e in range(4):
            side[e, 32:33, :] = jnp.zeros((1, 256), F32)

    @pl.when(at[0] == counts[0] - 1)
    def _():
        high[...] = jnp.zeros_like(high)
        face_all[40:48, :] = jnp.zeros((8, 256), F32)
        plane_all[40:48, :] = jnp.zeros((8, 256), F32)

    face_all[8:40, :] = face[...]
    plane_all[8:40, :] = plane[...]
    faces(
        my.at[:, 48:96], face_all, plane_all, side, face_e, face_a, column, inv_face, inv_plane
    )

    def layer(x):
        total = part[x + 1 if x < 8 else x - 14]
        for a in range(-REACH, REACH + 1):
            if x + a < 0:
                total = total + gauss(a) * low[x + a + 7]
            elif x + a >= 32:
                total = total + gauss(a) * high[x + a - 32]
        return total * (inv_x[x % 33 : x % 33 + 1, :] * inv_yz[...])

    kap = jnp.maximum(before[3], layer(-1))
    integ = integrity_of(kap)
    for e in range(3):
        before[e] = integ * before[e]
    copies = []
    for c in (0, 3):
        if c == 3:
            layer_results(23, layer(23), kappa, free, strain, before, None, None, None, None, None)
        for i in range(CHUNK):
            x = c * CHUNK + i
            slot = i if c == 0 else CHUNK + i
            layer_results(
                x, layer(x), kappa, free, strain, before, face_e, face_a, column,
                force_v.at[slot], kappa_v.at[slot],
            )
        here = pl.ds(0 if c == 0 else CHUNK, CHUNK)
        there = pl.ds(c * CHUNK, CHUNK)
        for k, (src, dst) in enumerate(((force_v, force), (kappa_v, kappa_new))):
            copy = pltpu.make_async_copy(src.at[here], dst.at[there], sems.at[c // 3, k])
            copy.start()
            copies.append(copy)
    for copy in copies:
        copy.wait()


AXES = ("gx", "gy", "gz")


def swap(first, second, axis):
    sizes = [lax.axis_size(a) for a in AXES]
    at = AXES.index(axis)
    other = 0 if at == 1 else 1

    def route(start):
        out = []
        for place in np.ndindex(*sizes):
            there = list(place)
            if place[at] >= start and place[at] - start < (sizes[at] - start) // 2 * 2:
                there[at] += 1 if (place[at] - start) % 2 == 0 else -1
            else:
                there[other] ^= 1
            out.append(tuple(int(np.ravel_multi_index(p, sizes)) for p in (place, tuple(there))))
        return out

    return lax.ppermute(first, AXES, route(0)), lax.ppermute(second, AXES, route(1))


def to_next(block, axis):
    count = lax.axis_size(axis)
    return lax.ppermute(block, axis, [(i, (i + 1) % count) for i in range(count)])


def shape_of(*dims):
    return jax.ShapeDtypeStruct(dims, F32)


VM = pl.BlockSpec(memory_space=pltpu.VMEM)
SM = pl.BlockSpec(memory_space=pltpu.SMEM)
HBM = pl.BlockSpec(memory_space=pltpu.HBM)
BLOCK = shape_of(32, 32, 256)
FACE = shape_of(32, 256)


def vmem(*dims):
    return pltpu.VMEM(dims, F32)


def call(kernel, name, in_specs, out_shape, out_specs=None, scratch=(), **kwargs):
    return pl.pallas_call(
        kernel,
        name=name,
        in_specs=in_specs,
        out_specs=out_specs or [VM] * len(out_shape),
        out_shape=out_shape,
        scratch_shapes=list(scratch),
        interpret=INTERPRET,
        compiler_params=pltpu.CompilerParams(vmem_limit_bytes=VMEM_LIMIT),
        **kwargs,
    )


def body(strain_in, plastic_in, alpha_in, kappa, flags):
    where = jnp.stack([lax.axis_index(a) for a in AXES]).astype(jnp.int32)
    flags = flags.reshape(32, 32)
    counts = tuple(lax.axis_size(a) for a in AXES)
    extents = (32 * counts[0], 32 * counts[1], 256 * counts[2])
    rows_all = rows_matrix()
    rows_own = np.ascontiguousarray(rows_all[:, 8:40])
    rows_halo = np.concatenate(
        [rows_all[:, 1:8], np.zeros((40, 1), np.float32), rows_all[:, 40:48]], axis=1
    )
    rows_halo = np.concatenate([rows_halo[0:8], rows_halo[24:40]], axis=0)
    rows_three = np.zeros((40, 128), np.float32)
    rows_three[0:24, 0:16] = rows_halo
    rows_three[:, 48:96] = rows_all

    whole_in = [
        pltpu.with_memory_space_constraint(v, pltpu.HBM)
        for v in (strain_in, plastic_in, alpha_in, kappa, flags)
    ]
    ends, eight = shape_of(4, 32, 256), shape_of(8, 32, 256)
    square = shape_of(128, 128)
    strain, plastic, alpha, turned, z_b, z_a, yext = call(
        pack_kernel,
        "pack",
        [SM] + [HBM] * 5,
        [
            shape_of(3, 32, 32, 256), BLOCK, BLOCK, shape_of(32, 32), square, square, ends,
        ],
        scratch=[vmem(32, 32, 128), vmem(32, 8, 128), pltpu.VMEM((32, 32), jnp.int32)]
        + [vmem(128, 128)] * 6
        + [pltpu.SemaphoreType.DMA((CHUNKS + 1, 4))],
    )(where, *whole_in)
    got_a, got_b = swap(z_a, z_b, "gz")
    face_ext = to_next(yext, "gy")
    own, free, xext = call(
        inner_kernel, "inner", [VM] * 6, [BLOCK, BLOCK, ends], scratch=[vmem(32, 32, 256)]
    )(strain, plastic, alpha, kappa, turned, z_band(256))
    t = z_halo_rows()
    w = np.concatenate([plane_from_low(), plane_from_own()], axis=1)
    plane, y_a, y_b, z_both, xext = call(
        functools.partial(z_kernel, counts),
        "along_z",
        [SM] + [VM] * 9,
        [FACE, eight, eight, shape_of(128, 256), ends],
        scratch=[vmem(128, 256)] + [vmem(32, 128)] * 2 + [vmem(512, 256), vmem(2, 32, 8, 256)],
    )(where, own, xext, z_b, z_a, got_b, got_a, face_ext, t, w)
    y_got_a, y_got_b = swap(y_a, y_b, "gy")
    ext_a, ext_b = swap(xext, xext, "gx")
    own, own_face, *inverse = call(
        functools.partial(own_rows_kernel, extents),
        "own_rows",
        [SM] + [VM] * 4,
        [BLOCK, FACE, shape_of(40, 256), FACE, shape_of(40, 256), shape_of(40, 256)],
        scratch=[vmem(1024, 256), vmem(32, 32, 256)],
    )(where, own, z_both, t, rows_own)

    edges, face, plane, x_a, x_b = call(
        functools.partial(y_kernel, counts),
        "along_y",
        [SM] + [VM] * 10,
        [shape_of(16, 32, 256), FACE, FACE] + [shape_of(248, 256)] * 2,
        scratch=[vmem(16, 16, 256), vmem(32, 256), vmem(32, 256)],
    )(where, own, own_face, plane, y_got_b, y_got_a, face_ext, ext_b, ext_a, rows_halo, plane_y_matrix())
    got_a, got_b = swap(x_a, x_b, "gx")

    shared = [
        vmem(48, 256), vmem(48, 256), vmem(4, 40, 256), vmem(4, 32, 256),
        vmem(32, 256), vmem(32, 256), vmem(32, 128),
        vmem(16, 32, 256), vmem(16, 32, 256), pltpu.SemaphoreType.DMA((2, 2)),
    ]
    force, kappa_new, part, face, got_ext = call(
        functools.partial(middle_kernel, counts),
        "middle",
        [SM] + [VM] * 17,
        [BLOCK, BLOCK, shape_of(18, 32, 256), FACE, ends],
        out_specs=[HBM, HBM, VM, VM, VM],
        scratch=[vmem(16, 16, 256), vmem(32, 32, 256)] + shared,
    )(where, strain, free, kappa, own, edges, y_got_a, y_got_b, ext_a, ext_b, face, plane, face_ext,
      *inverse, rows_three)
    force, kappa_new = call(
        functools.partial(outer_kernel, counts),
        "outer",
        [SM] + [VM] * 15 + [HBM, HBM],
        [BLOCK, BLOCK],
        out_specs=[HBM, HBM],
        scratch=[vmem(7, 32, 256), vmem(6, 32, 256)] + shared,
        input_output_aliases={16: 0, 17: 1},
    )(
        where, strain, free, kappa, part, face, plane, face_ext, got_a, got_b, got_ext,
        *inverse, rows_three,
        force, kappa_new,
    )
    return (force, kappa_new)


def solution(mesh):
    in_specs = (
        P(None, "gx", "gy", "gz"),
        P("gx", "gy", "gz"),
        P("gx", "gy", "gz"),
        P("gx", "gy", "gz"),
        P("gx", "gy", "gz"),
    )
    out_specs = (P("gx", "gy", "gz"), P("gx", "gy", "gz"))
    return jax.shard_map(body, mesh=mesh, in_specs=in_specs, out_specs=out_specs, check_vma=False)
```
